32 devices in a mesh: dp: 8 (over z, x), mp: 4 (over y, core).
Axes of the slice: x: 2, y: 2, z: 4, core: 2. Of those that a mesh axis runs over, the one named last changes fastest.
Arguments:
- tokens: bfloat16 [16, 2048, 512], P('dp', 'mp'), may hold values from -6 to 6
- segment_ids: int32 [16, 2048], P('dp'), may hold values from 0 to 7, as said below
- routes: int32 [16, 2048, 8], P('dp', 'mp'), may hold values from 0 to 23, as said below
- out_grad: bfloat16 [16, 2048, 512], P('dp', 'mp'), may hold values from -6 to 6
- w_query: bfloat16 [512, 1536], P(('dp', 'mp')), may hold values from -0.25 to 0.25
- w_keyval: bfloat16 [512, 128], P(('dp', 'mp')), may hold values from -0.25 to 0.25
- w_output: bfloat16 [512, 1536], P(('dp', 'mp')), may hold values from -12 to 12
- w_router: bfloat16 [512, 24], P(('dp', 'mp')), may hold values from -0.12988281 to 0.12988281
- norm_gains: float32 [512, 2], P(('dp', 'mp')), may hold values from 0.5 to 1.5
- norm_biases: float32 [512, 2], P(('dp', 'mp')), may hold values from -0.6 to 0.6
- w_up: bfloat16 [512, 2048], P('dp', 'mp'), may hold values from -0.25 to 0.25
- w_down: bfloat16 [512, 2048], P('dp', 'mp'), may hold values from -0.1875 to 0.1875
Outputs:
- outputs: bfloat16 [16, 2048, 512], P('dp', 'mp')
- input_grad: float32 [16, 2048, 512], P('dp', 'mp')
- counts: float32 [24], replicated
- w_query_grad: float32 [512, 1536], P(('dp', 'mp'))
- w_keyval_grad: float32 [512, 128], P(('dp', 'mp'))
- w_output_grad: float32 [512, 1536], P(('dp', 'mp'))
- w_router_grad: float32 [512, 24], P(('dp', 'mp'))
- norm_gains_grad: float32 [512, 2], P(('dp', 'mp'))
- norm_biases_grad: float32 [512, 2], P(('dp', 'mp'))
- w_up_grad: float32 [512, 2048], P('dp', 'mp')
- w_down_grad: float32 [512, 2048], P('dp', 'mp')
The draws below stay inside these ranges and needn't reach their ends.
Inputs may be any that keep to these rules, and one draw needn't show every extreme that they name: `segment_ids`: within a row the segment ids start at 0 and rise by at most one from a position to the next; in each aligned block of 2 rows one row is a single document. `routes`: each token names 8 different head experts.
All inputs are finite; a program needn't handle non-finite values.
Results may differ from the reference program's by a relative error of at most 0.03.
Values may be sent and summed in bfloat16 or wider, within the bound.
No kernel may reach another device: no remote copies, remote signals or barrier semaphores. Data moves between devices by JAX's collectives and lax.ppermute only.
A program may use at most 192 MiB of HBM per device.

```python
from functools import partial
import jax
import jax.numpy as jnp
from jax import lax

D = 512
H = 24
HD = 64
TOPK = 8
FF = 2048
SEQ = 2048
ROWS_DEV = 2
BATCH = 16


def draw_segment_ids(key, part):
    key = jax.random.fold_in(key, 11)
    order_key, count_key, row_key = jax.random.split(key, 3)
    row_keys = jax.random.split(order_key, BATCH)
    orders = jax.vmap(lambda k: jax.random.permutation(k, SEQ - 1))(row_keys)
    ranks = jnp.argsort(orders, axis=1, stable=True).astype(jnp.int32)
    documents = jax.random.randint(count_key, (BATCH, 1), 2, 9)
    chosen_row = jax.random.randint(row_key, (BATCH // ROWS_DEV, 1), 0, ROWS_DEV)
    row_place = (jnp.arange(BATCH, dtype=jnp.int32) % ROWS_DEV).reshape(BATCH // ROWS_DEV, ROWS_DEV)
    whole_row = (row_place == chosen_row).reshape(BATCH, 1)
    full_row = (row_place == (chosen_row + 1) % ROWS_DEV).reshape(BATCH, 1)
    documents = jnp.where(whole_row, 1, jnp.where(full_row, 8, documents))
    inner = (ranks < documents - 1).astype(jnp.int32)
    breaks = jnp.concatenate([jnp.zeros((BATCH, 1), jnp.int32), inner], axis=1)
    return jnp.cumsum(breaks, axis=1).astype(jnp.int32)


def draw_routes(key, part):
    key = jax.random.fold_in(key, 23)
    experts = jnp.arange(H, dtype=jnp.int32)
    centre = jnp.arange(BATCH, dtype=jnp.int32) * H // BATCH
    offset = jnp.abs(experts[None, :] - centre[:, None])
    distance = jnp.minimum(offset, H - offset)
    noise = jax.random.randint(key, (BATCH, SEQ, H), 0, 4096)
    scores = (noise - 300 * distance[:, None, :]) * H + experts[None, None, :]
    picked = lax.top_k(scores, TOPK)[1]
    return picked.astype(jnp.int32)


def block_levels(rng, shape, shards, least, largest):
    level = 1.0
    for axis_at, parts in shards:
        steps = jax.random.uniform(jax.random.fold_in(jax.random.fold_in(rng, 6), axis_at), (parts,), jnp.float32, least / len(shards), largest / len(shards))
        level = level * jnp.repeat(jnp.exp(steps), shape[axis_at] // parts).reshape((-1,) + (1,) * (len(shape) - 1 - axis_at))
    return level


def gaussian(key, shape, scale, most, shards=(), kind=jnp.bfloat16):
    entries = scale * jax.random.normal(key, shape, jnp.float32)
    if shards:
        entries = entries * block_levels(key, shape, shards, -0.22, 0.18)
    return jnp.clip(entries, -most, most).astype(kind)


def setup_inputs(seed: int = 0) -> dict:
    arg_keys = jax.random.split(jax.random.key(seed), 13)
    return {
        "tokens": gaussian(arg_keys[0], (BATCH, SEQ, D), 1.0, 6.0, ((0, 8), (1, 4))),
        "segment_ids": draw_segment_ids(jax.random.fold_in(arg_keys[12], 71), 0),
        "routes": draw_routes(jax.random.fold_in(arg_keys[12], 71), 0),
        "out_grad": gaussian(arg_keys[3], (BATCH, SEQ, D), 1.0, 6.0, ((0, 8), (1, 4))),
        "w_query": gaussian(arg_keys[4], (D, H * HD), D ** -0.5, 0.25, ((0, 32),)),
        "w_keyval": gaussian(arg_keys[5], (D, 2 * HD), D ** -0.5, 0.25, ((0, 32),)),
        "w_output": gaussian(arg_keys[6], (D, H * HD), 2.0, 12.0, ((0, 32),)),
        "w_router": gaussian(arg_keys[7], (D, H), 0.022, 0.12988281, ((0, 32),)),
        "norm_gains": jnp.clip(1.0 + 0.1 * jax.random.normal(arg_keys[8], (D, 2), jnp.float32), 0.5, 1.5),
        "norm_biases": gaussian(arg_keys[9], (D, 2), 0.1, 0.6, ((0, 32),), jnp.float32),
        "w_up": gaussian(arg_keys[10], (D, FF), D ** -0.5, 0.25, ((0, 8), (1, 4))),
        "w_down": gaussian(arg_keys[11], (D, FF), (FF // 2) ** -0.5, 0.1875, ((0, 8), (1, 4))),
    }


@jax.custom_vjp
def low(v):
    return lax.optimization_barrier(v.astype(jnp.bfloat16)).astype(jnp.float32)

@jax.custom_vjp
def low_back(v):
    return v

def low_keep(v):
    return (low(v), None)

def low_pass(kept, grad):
    return (grad,)

def back_keep(v):
    return (v, None)

def back_low(kept, grad):
    return (low(grad),)
low.defvjp(low_keep, low_pass)
low_back.defvjp(back_keep, back_low)
epsilon = 1e-05

def layer_norm(values, gain, bias):
    mean = lax.optimization_barrier(jnp.mean(values, axis=-1, keepdims=True))
    centred = values - mean
    rstd = lax.rsqrt(lax.optimization_barrier(jnp.mean(centred * centred, axis=-1, keepdims=True)) + epsilon)
    return centred * rstd * gain + bias

def product(left, right):
    return jnp.dot(left, right, precision=lax.Precision.HIGHEST, preferred_element_type=jnp.float32)

def row_attention(inputs):
    queries, keyvals, segments = inputs
    head_view = queries.reshape(SEQ, H, HD)
    key_rows = keyvals[:, :HD]
    value_rows = keyvals[:, HD:]
    scores = jnp.einsum('qhd,kd->hqk', head_view, key_rows, precision=lax.Precision.HIGHEST) * HD ** (-0.5)
    scores = low_back(scores)
    places = jnp.arange(SEQ, dtype=jnp.int32)
    visible = (places[None, :] <= places[:, None]) & (segments[:, None] == segments[None, :])
    probabilities = low(jax.nn.softmax(jnp.where(visible[None], scores, -1e+30), axis=-1))
    attended = jnp.einsum('hqk,kd->qhd', probabilities, value_rows, precision=lax.Precision.HIGHEST)
    return low_back(attended).reshape(SEQ, H * HD)

def forward(inputs, w_query, w_keyval, w_output, w_router, norm_gains, norm_biases, w_up, w_down, chosen=None, segment_ids=None):
    normed_one = low(layer_norm(inputs, norm_gains[:, 0], norm_biases[:, 0]))
    queries = low(low_back(product(normed_one, w_query)))
    keyvals = low(low_back(product(normed_one, w_keyval)))
    logits = low_back(product(normed_one, w_router))
    gate_weights = jax.nn.softmax(jnp.where(chosen > 0, logits, -1e+30), axis=-1)
    attended = lax.map(jax.checkpoint(row_attention), (queries.reshape(BATCH, SEQ, H * HD), keyvals.reshape(BATCH, SEQ, 2 * HD), segment_ids))
    attended = attended.reshape(-1, H, HD)
    gated = low((attended * gate_weights[:, :, None]).reshape(-1, H * HD))
    middle = inputs + low_back(product(gated, w_output.T))
    normed_two = low(layer_norm(middle, norm_gains[:, 1], norm_biases[:, 1]))
    before = low_back(product(normed_two, w_up))
    hidden = low(jax.nn.gelu(before))
    return middle + product(hidden, w_down.T)

def reference(tokens, segment_ids, routes, out_grad, w_query, w_keyval, w_output, w_router, norm_gains, norm_biases, w_up, w_down):
    chosen = lax.optimization_barrier(jnp.sum((routes.reshape(-1, TOPK)[:, :, None] == jnp.arange(H, dtype=jnp.int32)).astype(jnp.float32), axis=1))
    counts = lax.optimization_barrier(jnp.sum(chosen, axis=0))
    inputs = tokens.reshape(-1, D).astype(jnp.float32)
    weights = (w_query.astype(jnp.float32), w_keyval.astype(jnp.float32), w_output.astype(jnp.float32), w_router.astype(jnp.float32), norm_gains.astype(jnp.float32), norm_biases.astype(jnp.float32), w_up.astype(jnp.float32), w_down.astype(jnp.float32))
    outputs, pullback = jax.vjp(partial(forward, chosen=chosen, segment_ids=segment_ids), inputs, *weights)
    gradients = pullback(out_grad.reshape(-1, D).astype(jnp.float32))
    return (outputs.reshape(tokens.shape).astype(jnp.bfloat16), gradients[0].reshape(tokens.shape), counts, gradients[1], gradients[2], gradients[3], gradients[4], gradients[5], gradients[6], gradients[7], gradients[8])
```

```python
import functools
import math
import jax
import jax.numpy as jnp
from jax import lax
from jax.experimental import pallas as pl
from jax.experimental.pallas import tpu as pltpu
from jax.sharding import PartitionSpec as P

epsilon = 1e-05
f32, bf16 = jnp.float32, jnp.bfloat16
NN = (((1,), (0,)), ((), ()))
NT = (((1,), (1,)), ((), ()))
LANES = 128
LOG2E = math.log2(math.e)
MIB = 2**20


def dot(left, right, dims=NN):
    return lax.dot_general(left, right, dims, preferred_element_type=f32)


def bits_of(axis):
    return (lax.axis_size(axis) - 1).bit_length()


def bit_groups(axis):
    count = bits_of(axis)
    groups, at = [], 0
    if count % 2:
        groups.append((0, 1))
        at = 1
    while at < count:
        groups.append((at, 2))
        at += 2
    return groups


def flip(x, axis, mask):
    return lax.ppermute(x, axis, [(i, i ^ mask) for i in range(lax.axis_size(axis))])


def gather_bits(x, axis, group, dim):
    low, width = group
    mine = lax.axis_index(axis) >> low
    pieces = [x] + [flip(x, axis, k << low) for k in range(1, 2**width)]
    for b in range(width):
        odd = (mine >> b) & 1 == 1
        pieces = [jnp.where(odd, pieces[q ^ (1 << b)], pieces[q]) for q in range(2**width)]
    return jnp.stack(pieces, axis=dim)


def gather_axis(x, axis, dim):
    for group in reversed(bit_groups(axis)):
        x = gather_bits(x, axis, group, dim)
        dim += 1
    return x


def gather_each_bit(x, axis, dim):
    for b in reversed(range(bits_of(axis))):
        x = gather_bits(x, axis, (b, 1), dim)
        dim += 1
    return x


def scatter_bits(x, axis, group, dim):
    low, width = group
    mine = (lax.axis_index(axis) >> low) & (2**width - 1)
    total = None
    got = [
        flip(lax.dynamic_index_in_dim(x, mine ^ k, dim, keepdims=False), axis, k << low)
        for k in range(1, 2**width)
    ]
    total = lax.dynamic_index_in_dim(x, mine, dim, keepdims=False).astype(f32)
    for g in got:
        total = total + g.astype(f32)
    return total


def split_dims(axis, each):
    groups = [(b, 1) for b in range(bits_of(axis))] if each else bit_groups(axis)
    return groups, [2**width for _, width in reversed(groups)]


def halves(row_first, row_second, like):
    lane = lax.broadcasted_iota(jnp.int32, like, 1)
    return jnp.where(lane < LANES // 2, row_first, row_second)


def slot_experts(routes, pairs):
    shape = (routes.shape[0], LANES)
    return [halves(routes[:, 2 * j : 2 * j + 1], routes[:, 2 * j + 1 : 2 * j + 2], shape) for j in range(pairs)]


def turn_half(x):
    return pltpu.roll(x, LANES // 2, 1)


def compact(wide, experts, head_pairs):
    lane = lax.broadcasted_iota(jnp.int32, experts[0].shape, 1)
    high = (lane >= LANES // 2).astype(jnp.int32)
    straight = [e - high for e in experts]
    crossed = [e + high for e in experts]
    found = [jnp.zeros(experts[0].shape, f32) for _ in experts]
    for i in range(head_pairs):
        block = wide(i)
        turned = turn_half(block)
        for j in range(len(experts)):
            found[j] = jnp.where(straight[j] == 2 * i, block, found[j])
            found[j] = jnp.where(crossed[j] == 2 * i + 1, turned, found[j])
    return found


def expand(narrow, experts, head_pairs):
    lane = lax.broadcasted_iota(jnp.int32, experts[0].shape, 1)
    high = (lane >= LANES // 2).astype(jnp.int32)
    sources = []
    for block, e in zip(narrow, experts):
        sources.append((e - high, block))
        sources.append((turn_half(e) - high, turn_half(block)))
    wide = []
    for i in range(head_pairs):
        out = jnp.zeros(experts[0].shape, f32)
        for e, block in sources:
            out = jnp.where(e == 2 * i, block, out)
        wide.append(out.astype(bf16))
    return jnp.concatenate(wide, axis=1)


def normed_parts(values):
    mean = jnp.mean(values, axis=1, keepdims=True)
    centred = values - mean
    rstd = lax.rsqrt(jnp.mean(centred * centred, axis=1, keepdims=True) + epsilon)
    return centred * rstd, rstd


def norm_back(grad, normed, rstd, gain):
    scaled = grad * gain
    return rstd * (
        scaled
        - jnp.mean(scaled, axis=1, keepdims=True)
        - normed * jnp.mean(scaled * normed, axis=1, keepdims=True)
    )


def norm_kernel(x_ref, w_ref, n_ref, kv_ref, norms_ref, *, at_kv, at_misc, heads):
    misc = w_ref[:, at_misc : at_misc + LANES].astype(f32).T
    norms = misc[heads : heads + 8, :]
    norms = jnp.concatenate(
        [norms[0:2] + norms[2:4], norms[4:6] + norms[6:8], jnp.zeros_like(norms[0:4])], axis=0
    )
    norms_ref[...] = norms
    normed, _ = normed_parts(x_ref[0].astype(f32))
    low = (normed * norms[0:1] + norms[2:3]).astype(bf16)
    n_ref[0] = low
    kv_ref[0] = dot(low, w_ref[:, at_kv : at_kv + LANES]).astype(bf16)


def query_kernel(
    n_ref, w_ref, routes_ref, routes_t_ref, q_ref, gate_ref, gate_t_ref, *, at_misc, heads, slots, hs
):
    low = n_ref[0]
    head_pairs = heads // 2
    queries = dot(low, w_ref[:, : heads * hs]) * (hs**-0.5 * LOG2E)
    experts = slot_experts(routes_ref[0], slots // 2)
    found = compact(lambda i: queries[:, i * LANES : (i + 1) * LANES], experts, head_pairs)
    q_ref[0] = jnp.concatenate([f.astype(bf16) for f in found], axis=1)
    logits = dot(low, w_ref[:, at_misc : at_misc + LANES]).T[:heads, :]
    expert = lax.broadcasted_iota(jnp.int32, logits.shape, 0)
    routes_t = routes_t_ref[0]
    picked = [
        jnp.sum(jnp.where(expert == routes_t[s : s + 1, :], logits, 0.0), axis=0, keepdims=True)
        for s in range(slots)
    ]
    chosen = jnp.concatenate(picked, axis=0)
    lifted = jnp.exp(chosen - jnp.max(chosen, axis=0, keepdims=True))
    gate = lifted / jnp.sum(lifted, axis=0, keepdims=True)
    gate_t_ref[0] = gate
    padded = jnp.concatenate([gate, jnp.zeros((LANES - slots, gate.shape[1]), f32)], axis=0)
    gate_ref[0] = padded.T


def key_bias(first_key, first_query, start, keys, queries):
    key = first_key + lax.broadcasted_iota(jnp.int32, (keys, queries), 0)
    query = first_query + lax.broadcasted_iota(jnp.int32, (keys, queries), 1)
    return jnp.where((key <= query) & (key >= start), 0.0, -1e30)


def kv_place(row, chunk, rows, peers):
    half = chunk % 2
    owner = jnp.where(half == 0, chunk // 2, peers - 1 - chunk // 2)
    return owner * (2 * rows) + row * 2 + half


def over_keys(plan, start_ref, bias, block, keys, queries):
    b = pl.program_id(0)
    row, last, first, full = plan[4 * b], plan[4 * b + 1], plan[4 * b + 2], plan[4 * b + 3]

    def masked(i, carry):
        chunk = jnp.where(i == 0, last, first + i - 1)
        bias[...] = key_bias(chunk * keys, last * keys, start_ref[0], keys, queries)
        block(row, chunk, True)
        return carry

    def plain(chunk, carry):
        block(row, chunk, False)
        return carry

    lax.fori_loop(0, 1 + full - first, masked, 0)
    lax.fori_loop(full, last, plain, 0)


def attend_kernel(
    plan, q_ref, kv_ref, start_ref, gate_ref, out_ref, lse_ref, kvt, qt, acc, top, tot, bias, *, slots, hs, rows, peers
):
    queries, keys = q_ref.shape[1], kv_ref.shape[1]

    @pl.when(pl.program_id(0) == 0)
    def _():
        for i in range(kv_ref.shape[0]):
            kvt[i] = kv_ref[i].T

    qt[...] = q_ref[0].T
    acc[...] = jnp.zeros_like(acc)
    top[...] = jnp.full_like(top, -1e30)
    tot[...] = jnp.zeros_like(tot)
    part = [slice(h * hs, (h + 1) * hs) for h in range(slots)]

    def block(row, chunk, masked):
        at = kv_place(row, chunk, rows, peers)
        k = kv_ref[at][:, :hs]
        vt = kvt[at, hs : 2 * hs, :]
        tops, tots = top[...], tot[...]
        scores = [dot(k, qt[part[h], :]) for h in range(slots)]
        if masked:
            scores = [s + bias[...] for s in scores]
        highest = [
            jnp.maximum(tops[h : h + 1], jnp.max(scores[h], axis=0, keepdims=True)) for h in range(slots)
        ]
        probs = [jnp.exp2(scores[h] - highest[h]) for h in range(slots)]
        shrink = [jnp.exp2(tops[h : h + 1] - highest[h]) for h in range(slots)]
        totals = [
            tots[h : h + 1] * shrink[h] + jnp.sum(probs[h], axis=0, keepdims=True) for h in range(slots)
        ]
        for h in range(slots):
            acc[part[h], :] = acc[part[h], :] * shrink[h] + dot(vt, probs[h].astype(bf16))
        top[...] = jnp.concatenate(highest, axis=0)
        tot[...] = jnp.concatenate(totals, axis=0)

    over_keys(plan, start_ref, bias, block, keys, queries)
    for h in range(slots):
        acc[part[h], :] = acc[part[h], :] * (gate_ref[0, h : h + 1, :] / tot[h : h + 1, :])
    lse_ref[0] = top[...] + jnp.log2(tot[...])
    out_ref[0] = acc[...].astype(bf16).T


def attend_back_kernel(
    plan, q_ref, g_ref, kv_ref, start_ref, lse_ref, delta_ref, dq_ref, dkv_ref,
    kvt, v_rows, qt, gt, dqt, dk, dv, bias, *, slots, hs, rows, peers,
):
    queries, keys = q_ref.shape[1], kv_ref.shape[1]
    b = pl.program_id(0)

    @pl.when(b == 0)
    def _():
        for i in range(kv_ref.shape[0]):
            kvt[i] = kv_ref[i].T
            v_rows[i] = kv_ref[i][:, hs:]
        dk[...] = jnp.zeros_like(dk)
        dv[...] = jnp.zeros_like(dv)

    qt[...] = q_ref[0].T
    gt[...] = g_ref[0].T
    dqt[...] = jnp.zeros_like(dqt)
    part = [slice(h * hs, (h + 1) * hs) for h in range(slots)]

    def block(row, chunk, masked):
        at = kv_place(row, chunk, rows, peers)
        k = kv_ref[at][:, :hs]
        v = v_rows[at]
        kt = kvt[at, :hs, :]
        scores = [dot(k, qt[part[h], :]) for h in range(slots)]
        grads = [dot(v, gt[part[h], :]) for h in range(slots)]
        if masked:
            scores = [s + bias[...] for s in scores]
        probs = [jnp.exp2(scores[h] - lse_ref[0, h : h + 1, :]) for h in range(slots)]
        ds = [(probs[h] * (grads[h] - delta_ref[0, h : h + 1, :])).astype(bf16) for h in range(slots)]
        low = [p.astype(bf16) for p in probs]
        for h in range(slots):
            dqt[part[h], :] += dot(kt, ds[h])
        dk[at] += sum(dot(ds[h], qt[part[h], :], NT) for h in range(slots))
        dv[at] += sum(dot(low[h], gt[part[h], :], NT) for h in range(slots))

    over_keys(plan, start_ref, bias, block, keys, queries)
    dq_ref[0] = (dqt[...] * hs**-0.5).astype(bf16).T

    @pl.when(b == pl.num_programs(0) - 1)
    def _():
        for i in range(kv_ref.shape[0]):
            dkv_ref[i] = jnp.concatenate([dk[i] * (1.0 / LOG2E), dv[i]], axis=1).astype(bf16)


def middle_kernel(
    gc_ref, gate_ref, routes_ref, x_ref, og_ref, wo_ref, ff_ref, norms_ref,
    out_ref, gm_ref, gbr_ref, gated_ref, n2_ref, hid_ref, gbef_ref, gatt_ref, delta_ref, glog_ref, sums_ref,
    *, heads, slots, hs, width,
):
    tokens, model = x_ref.shape[1], x_ref.shape[2]
    head_pairs, pairs = heads // 2, slots // 2
    experts = slot_experts(routes_ref[0], pairs)
    gc = [gc_ref[0][:, j * LANES : (j + 1) * LANES].astype(f32) for j in range(pairs)]
    gated = expand(gc, experts, head_pairs)
    gated_ref[0] = gated
    middle = x_ref[0].astype(f32) + dot(gated, wo_ref[...], NT)
    gain, shift = norms_ref[1:2, :], norms_ref[3:4, :]
    vhat, rstd = normed_parts(middle)
    low = (vhat * gain + shift).astype(bf16)
    n2_ref[0] = low
    og = og_ref[0]
    out = middle
    back = jnp.zeros((tokens, model), f32)
    slope = math.sqrt(2.0 / math.pi)
    for c in range(ff_ref.shape[0]):
        up, down = ff_ref[c, :, :width], ff_ref[c, :, width:]
        v = dot(low, up)
        square = v * v
        bent = jnp.tanh(slope * v * (1.0 + 0.044715 * square))
        rise = 0.5 * (1.0 + bent)
        hidden = (v * rise).astype(bf16)
        slant = rise + 0.5 * v * (1.0 - bent * bent) * (slope + 3.0 * slope * 0.044715 * square)
        before = (dot(og, down) * slant).astype(bf16)
        out = out + dot(hidden, down, NT)
        back = back + dot(before, up, NT)
        hid_ref[0, :, c * width : (c + 1) * width] = hidden
        gbef_ref[0, :, c * width : (c + 1) * width] = before
    out_ref[0] = out.astype(bf16)
    gm = og.astype(f32) + norm_back(back, vhat, rstd, gain)
    gm_ref[0] = gm
    sums = jnp.concatenate(
        [
            jnp.sum(back * vhat, axis=0, keepdims=True),
            jnp.sum(back, axis=0, keepdims=True),
            jnp.zeros((6, model), f32),
        ],
        axis=0,
    )

    @pl.when(pl.program_id(0) == 0)
    def _():
        sums_ref[...] = jnp.zeros_like(sums_ref)

    sums_ref[...] += sums
    gbr = gm.astype(bf16)
    gbr_ref[0] = gbr
    found = compact(
        lambda i: dot(gbr, wo_ref[:, i * LANES : (i + 1) * LANES]), experts, head_pairs
    )
    gate = gate_ref[0]
    shape = (tokens, LANES)
    attended, products = [], []
    for j in range(pairs):
        spread = halves(gate[:, 2 * j : 2 * j + 1], gate[:, 2 * j + 1 : 2 * j + 2], shape)
        attended.append((found[j] * spread).astype(bf16))
        products.append(found[j] * gc[j])
    gatt_ref[0] = jnp.concatenate(attended, axis=1)
    product = jnp.concatenate(products, axis=1)
    owner = lax.broadcasted_iota(jnp.int32, (slots * hs, LANES), 0) // hs
    ones = (owner == lax.broadcasted_iota(jnp.int32, (slots * hs, LANES), 1)).astype(bf16)
    coarse = product.astype(bf16)
    fine = (product - coarse.astype(f32)).astype(bf16)
    inner = dot(coarse, ones) + dot(fine, ones)
    delta_ref[0] = inner.T[:slots, :]
    logit = inner - gate * jnp.sum(inner, axis=1, keepdims=True)
    lane = lax.broadcasted_iota(jnp.int32, shape, 1)
    spread_out = jnp.zeros(shape, f32)
    routes = routes_ref[0]
    for s in range(slots):
        spread_out = jnp.where(lane == routes[:, s : s + 1], logit[:, s : s + 1], spread_out)
    glog_ref[0] = spread_out.astype(bf16)


def weights_kernel(
    n2_ref, og_ref, gbr_ref, gbef_ref, hid_ref, gated_ref, ff_ref, wo_ref, n2t, ogt, gbrt, *, width
):
    @pl.when(pl.program_id(0) == 0)
    def _():
        n2t[...] = n2_ref[...].T
        ogt[...] = og_ref[...].T
        gbrt[...] = gbr_ref[...].T

    ff_ref[0, :, :width] = dot(n2t[...], gbef_ref[...]).astype(bf16)
    ff_ref[0, :, width:] = dot(ogt[...], hid_ref[...]).astype(bf16)
    wo_ref[...] = dot(gbrt[...], gated_ref[...]).astype(bf16)


def query_back_kernel(
    dq_ref, routes_ref, n_ref, w_ref, glog_ref, wq_ref, wr_ref, dn_ref, accq, accr, *, at_misc, heads, slots, hs
):
    pairs = slots // 2
    experts = slot_experts(routes_ref[0], pairs)
    dq = [dq_ref[0][:, j * LANES : (j + 1) * LANES].astype(f32) for j in range(pairs)]
    wide = expand(dq, experts, heads // 2)
    nt = n_ref[0].T
    glog = glog_ref[0]
    dn_ref[0] = dot(wide, w_ref[:, : heads * hs], NT) + dot(
        glog, w_ref[:, at_misc : at_misc + LANES], NT
    )

    @pl.when(pl.program_id(0) == 0)
    def _():
        accq[...] = jnp.zeros_like(accq)
        accr[...] = jnp.zeros_like(accr)

    accq[...] += dot(nt, wide)
    accr[...] += dot(nt, glog)

    @pl.when(pl.program_id(0) == pl.num_programs(0) - 1)
    def _():
        wq_ref[...] = accq[...].astype(bf16)
        wr_ref[...] = accr[...]


def input_kernel(
    dn_ref, dkv_ref, w_ref, x_ref, n_ref, gm_ref, norms_ref, wr_ref, sums_ref, ig_ref, small_ref, acck, sums, *, at_kv, heads
):
    dkv = dkv_ref[0]
    dn = dn_ref[0] + dot(dkv, w_ref[:, at_kv : at_kv + LANES], NT)
    vhat, rstd = normed_parts(x_ref[0].astype(f32))
    ig_ref[0] = gm_ref[0] + norm_back(dn, vhat, rstd, norms_ref[0:1, :])

    @pl.when(pl.program_id(0) == 0)
    def _():
        acck[...] = jnp.zeros_like(acck)
        sums[...] = jnp.zeros_like(sums)

    acck[...] += dot(n_ref[0].T, dkv)
    sums[0:1, :] += jnp.sum(dn * vhat, axis=0, keepdims=True)
    sums[1:2, :] += jnp.sum(dn, axis=0, keepdims=True)

    @pl.when(pl.program_id(0) == pl.num_programs(0) - 1)
    def _():
        second = sums_ref[...]
        model = second.shape[1]
        rows = jnp.concatenate(
            [
                jnp.zeros((heads, model), f32),
                sums[0:1, :], second[0:1, :], sums[1:2, :], second[1:2, :],
                jnp.zeros((LANES - heads - 4, model), f32),
            ],
            axis=0,
        )
        small_ref[:, :LANES] = acck[...].astype(bf16)
        small_ref[:, LANES:] = (wr_ref[...] + rows.T).astype(bf16)


def fixed(shape):
    return pl.BlockSpec(shape, lambda b, *_: (0,) * len(shape))


def per_block(*shape):
    return pl.BlockSpec((1, *shape), lambda b, *_: (b,) + (0,) * len(shape))


def like(shape, kind):
    return jax.ShapeDtypeStruct(shape, kind)


def cost(flops, size, exps=0):
    return pl.CostEstimate(flops=int(flops), bytes_accessed=int(size), transcendentals=int(exps))


def shards(
    tokens, segment_ids, routes, out_grad, w_query, w_keyval, w_output, w_router,
    norm_gains, norm_biases, w_up, w_down,
):
    rows, local, model = tokens.shape
    peers = lax.axis_size("mp")
    slots = routes.shape[2]
    heads = w_router.shape[1]
    hs = w_keyval.shape[1] // 2
    width = w_up.shape[1]
    chunk = local // 2
    blocks = rows * 2
    count = rows * local
    place = lax.axis_index("mp")
    wide = heads * hs
    slim = slots * hs
    at_kv, at_misc = wide, wide + 2 * hs

    def two(v):
        high = lax.reduce_precision(v, 8, 7)
        return [high.astype(bf16), (v - high).astype(bf16)]

    pads = jnp.zeros((w_query.shape[0], LANES - heads - 8), bf16)
    first = jnp.concatenate(
        [w_query, w_keyval, w_router, *two(norm_gains), *two(norm_biases), pads], axis=1
    )
    first = gather_axis(first, "dp", 0)
    held_out, held_up, held_down, first = lax.optimization_barrier((w_output, w_up, w_down, first))
    first = gather_each_bit(first, "mp", len(bit_groups("dp")))
    weights = first.reshape(model, at_misc + LANES)

    def swap(a):
        return flip(a, "mp", peers - 1)

    half_tokens = tokens[:, chunk:, :].reshape(rows * chunk, model)
    half_routes = routes[:, chunk:, :].astype(bf16).reshape(-1, model)
    met = swap(jnp.concatenate([half_tokens, half_routes], axis=0))
    met_tokens = met[: rows * chunk].reshape(rows, chunk, model)
    met_routes = met[rows * chunk :].reshape(rows, chunk, slots).astype(jnp.int32)

    def joined(near, far):
        return jnp.stack([near[:, :chunk], far], axis=1).reshape(blocks, chunk, -1)

    x = joined(tokens, met_tokens)
    picks = joined(routes, met_routes)
    picks_t = jnp.swapaxes(picks, 1, 2)
    chosen = (routes[..., None] == jnp.arange(heads, dtype=jnp.int32)).astype(f32)
    counts = lax.psum(jnp.sum(chosen, axis=(0, 1, 2)), ("dp", "mp"))

    near, far = 2 * place, 2 * (peers - 1 - place) + 1
    ids = jnp.arange(8, dtype=jnp.int32)
    sizes = jnp.sum((segment_ids[:, :, None] == ids).astype(jnp.int32), axis=1)
    own = jnp.stack(
        [lax.dynamic_slice_in_dim(segment_ids, c * chunk, chunk, 1) for c in (near, far)], axis=1
    )
    start = jnp.sum(jnp.where(ids < own[..., None], sizes[:, None, None, :], 0), axis=-1)
    last = jnp.broadcast_to(jnp.stack([near, far]), (rows, 2))
    full = jnp.minimum((start[:, :, -1] + chunk - 1) // chunk, last)
    which = jnp.broadcast_to(jnp.arange(rows, dtype=jnp.int32)[:, None], (rows, 2))
    plan = jnp.stack([which, last, start[:, :, 0] // chunk, full], axis=-1).astype(jnp.int32)
    plan = plan.reshape(-1)
    start = start.astype(jnp.int32).reshape(blocks, 1, chunk)

    n1, kv, norms = pl.pallas_call(
        functools.partial(norm_kernel, at_kv=at_kv, at_misc=at_misc, heads=heads),
        grid=(blocks,),
        in_specs=[per_block(chunk, model), fixed(weights.shape)],
        out_specs=[per_block(chunk, model), per_block(chunk, 2 * hs), fixed((8, model))],
        out_shape=[
            like((blocks, chunk, model), bf16),
            like((blocks, chunk, 2 * hs), bf16),
            like((8, model), f32),
        ],
        cost_estimate=cost(2 * count * model * LANES, 4 * MIB),
        name="norm_one",
    )(x, weights)
    kv_all = gather_each_bit(kv, "mp", 0).reshape(peers * blocks, chunk, 2 * hs)

    q, gate, gate_t = pl.pallas_call(
        functools.partial(query_kernel, at_misc=at_misc, heads=heads, slots=slots, hs=hs),
        grid=(blocks,),
        in_specs=[
            per_block(chunk, model), fixed(weights.shape), per_block(chunk, slots), per_block(slots, chunk),
        ],
        out_specs=[per_block(chunk, slim), per_block(chunk, LANES), per_block(slots, chunk)],
        out_shape=[
            like((blocks, chunk, slim), bf16),
            like((blocks, chunk, LANES), f32),
            like((blocks, slots, chunk), f32),
        ],
        compiler_params=pltpu.CompilerParams(vmem_limit_bytes=32 * MIB),
        cost_estimate=cost(2 * count * model * wide * 2, 6 * MIB),
        name="queries",
    )(n1, weights, picks, picks_t)

    out_full = gather_axis(held_out, "dp", 0)
    out_full = gather_each_bit(out_full, "mp", len(bit_groups("dp"))).reshape(model, wide)
    ff = gather_axis(jnp.concatenate([held_up, held_down], axis=1), "dp", 0)
    ff = gather_each_bit(ff.reshape(model, 2 * width), "mp", 0).reshape(peers, model, 2 * width)
    grads = joined(out_grad, swap(out_grad[:, chunk:, :]))

    attention = dict(slots=slots, hs=hs, rows=rows, peers=peers)
    total = peers * blocks
    gc, lse = pl.pallas_call(
        functools.partial(attend_kernel, **attention),
        grid_spec=pltpu.PrefetchScalarGridSpec(
            num_scalar_prefetch=1,
            grid=(blocks,),
            in_specs=[
                per_block(chunk, slim), fixed(kv_all.shape), per_block(1, chunk), per_block(slots, chunk),
            ],
            out_specs=[per_block(chunk, slim), per_block(slots, chunk)],
            scratch_shapes=[
                pltpu.VMEM((total, 2 * hs, chunk), bf16),
                pltpu.VMEM((slim, chunk), bf16),
                pltpu.VMEM((slim, chunk), f32),
                pltpu.VMEM((slots, chunk), f32),
                pltpu.VMEM((slots, chunk), f32),
                pltpu.VMEM((chunk, chunk), f32),
            ],
        ),
        out_shape=[like((blocks, chunk, slim), bf16), like((blocks, slots, chunk), f32)],
        compiler_params=pltpu.CompilerParams(vmem_limit_bytes=40 * MIB),
        cost_estimate=cost(12e9, 4 * MIB),
        name="attend",
    )(plan, q, kv_all, start, gate_t)

    outs, gm, gbr, gated, n2, hid, gbef, gatt, delta, glog, sums = pl.pallas_call(
        functools.partial(middle_kernel, heads=heads, slots=slots, hs=hs, width=width),
        grid=(blocks,),
        in_specs=[
            per_block(chunk, slim), per_block(chunk, LANES), per_block(chunk, slots),
            per_block(chunk, model), per_block(chunk, model),
            fixed(out_full.shape), fixed(ff.shape), fixed(norms.shape),
        ],
        out_specs=[
            per_block(chunk, model), per_block(chunk, model), per_block(chunk, model),
            per_block(chunk, wide), per_block(chunk, model),
            per_block(chunk, peers * width), per_block(chunk, peers * width),
            per_block(chunk, slim), per_block(slots, chunk), per_block(chunk, LANES), fixed((8, model)),
        ],
        out_shape=[
            like((blocks, chunk, model), bf16),
            like((blocks, chunk, model), f32),
            like((blocks, chunk, model), bf16),
            like((blocks, chunk, wide), bf16),
            like((blocks, chunk, model), bf16),
            like((blocks, chunk, peers * width), bf16),
            like((blocks, chunk, peers * width), bf16),
            like((blocks, chunk, slim), bf16),
            like((blocks, slots, chunk), f32),
            like((blocks, chunk, LANES), bf16),
            like((8, model), f32),
        ],
        compiler_params=pltpu.CompilerParams(vmem_limit_bytes=56 * MIB),
        cost_estimate=cost(18e9, 24 * MIB),
        name="middle",
    )(gc, gate, picks, x, grads, out_full, ff, norms)

    def flat(a):
        return a.reshape(count, -1)

    def column(w):
        return pl.BlockSpec((count, w), lambda m: (0, m))

    part = wide // peers
    ff_sum, out_sum = pl.pallas_call(
        functools.partial(weights_kernel, width=width),
        grid=(peers,),
        in_specs=[fixed((count, model))] * 3 + [column(width), column(width), column(part)],
        out_specs=[per_block(model, 2 * width), pl.BlockSpec((model, part), lambda m: (0, m))],
        out_shape=[like((peers, model, 2 * width), bf16), like((model, wide), bf16)],
        scratch_shapes=[pltpu.VMEM((model, count), bf16)] * 3,
        compiler_params=pltpu.CompilerParams(vmem_limit_bytes=48 * MIB),
        cost_estimate=cost(6e9, 20 * MIB),
        name="weight_grads",
    )(flat(n2), flat(grads), flat(gbr), flat(gbef), flat(hid), flat(gated))

    mp_bits, mp_dims = split_dims("mp", True)
    dp_bits, dp_dims = split_dims("dp", False)

    def scatter_all(a, lead):
        for group in mp_bits:
            dim = (0 if lead else len(dp_dims)) + len(mp_dims) - 1 - mp_bits.index(group)
            a = scatter_bits(a, "mp", group, dim).astype(bf16)
        for i, group in enumerate(dp_bits):
            a = scatter_bits(a, "dp", group, len(dp_dims) - 1 - i)
            if i < len(dp_bits) - 1:
                a = a.astype(bf16)
        return a

    per = w_query.shape[0]
    ff_grad = scatter_all(ff_sum.reshape(*mp_dims, *dp_dims, w_up.shape[0], 2 * width), True)
    out_grads = scatter_all(out_sum.reshape(*dp_dims, *mp_dims, per, wide), False)

    def unswapped(a):
        a = a.reshape(rows, 2, chunk, model)
        return jnp.concatenate([a[:, 0], swap(a[:, 1].astype(bf16)).astype(a.dtype)], axis=1)

    outputs = unswapped(outs)

    dq, dkv = pl.pallas_call(
        functools.partial(attend_back_kernel, **attention),
        grid_spec=pltpu.PrefetchScalarGridSpec(
            num_scalar_prefetch=1,
            grid=(blocks,),
            in_specs=[
                per_block(chunk, slim), per_block(chunk, slim), fixed(kv_all.shape), per_block(1, chunk),
                per_block(slots, chunk), per_block(slots, chunk),
            ],
            out_specs=[per_block(chunk, slim), fixed(kv_all.shape)],
            scratch_shapes=[
                pltpu.VMEM((total, 2 * hs, chunk), bf16),
                pltpu.VMEM((total, chunk, hs), bf16),
                pltpu.VMEM((slim, chunk), bf16),
                pltpu.VMEM((slim, chunk), bf16),
                pltpu.VMEM((slim, chunk), f32),
                pltpu.VMEM((total, chunk, hs), f32),
                pltpu.VMEM((total, chunk, hs), f32),
                pltpu.VMEM((chunk, chunk), f32),
            ],
        ),
        out_shape=[like((blocks, chunk, slim), bf16), like(kv_all.shape, bf16)],
        compiler_params=pltpu.CompilerParams(vmem_limit_bytes=48 * MIB),
        cost_estimate=cost(25e9, 6 * MIB),
        name="attend_back",
    )(plan, q, gatt, kv_all, start, lse, delta)

    dkv = dkv.reshape(*mp_dims, blocks * chunk, 2 * hs)
    for group in mp_bits:
        dkv = scatter_bits(dkv, "mp", group, len(mp_dims) - 1 - mp_bits.index(group)).astype(bf16)
    dkv = dkv.reshape(blocks, chunk, 2 * hs)

    wq_sum, wr_sum, dn = pl.pallas_call(
        functools.partial(query_back_kernel, at_misc=at_misc, heads=heads, slots=slots, hs=hs),
        grid=(blocks,),
        in_specs=[
            per_block(chunk, slim), per_block(chunk, slots), per_block(chunk, model),
            fixed(weights.shape), per_block(chunk, LANES),
        ],
        out_specs=[fixed((model, wide)), fixed((model, LANES)), per_block(chunk, model)],
        out_shape=[
            like((model, wide), bf16),
            like((model, LANES), f32),
            like((blocks, chunk, model), f32),
        ],
        scratch_shapes=[pltpu.VMEM((model, wide), f32), pltpu.VMEM((model, LANES), f32)],
        compiler_params=pltpu.CompilerParams(vmem_limit_bytes=40 * MIB),
        cost_estimate=cost(4e9, 10 * MIB),
        name="queries_back",
    )(dq, picks, n1, weights, glog)
    query_grad = scatter_all(wq_sum.reshape(*dp_dims, *mp_dims, per, wide), False)

    ig, small = pl.pallas_call(
        functools.partial(input_kernel, at_kv=at_kv, heads=heads),
        grid=(blocks,),
        in_specs=[
            per_block(chunk, model), per_block(chunk, 2 * hs), fixed(weights.shape),
            per_block(chunk, model), per_block(chunk, model), per_block(chunk, model),
            fixed((8, model)), fixed((model, LANES)), fixed((8, model)),
        ],
        out_specs=[per_block(chunk, model), fixed((model, 2 * LANES))],
        out_shape=[like((blocks, chunk, model), f32), like((model, 2 * LANES), bf16)],
        scratch_shapes=[pltpu.VMEM((model, 2 * hs), f32), pltpu.VMEM((8, model), f32)],
        compiler_params=pltpu.CompilerParams(vmem_limit_bytes=32 * MIB),
        cost_estimate=cost(1e9, 10 * MIB),
        name="inputs_back",
    )(dn, dkv, weights, x, n1, gm, norms, wr_sum, sums)

    tiles = small.reshape(model // per, per, 2 * LANES)
    tiles = lax.all_to_all(tiles, ("dp", "mp"), split_axis=0, concat_axis=0, tiled=True)
    smalls = jnp.sum(tiles.astype(f32), axis=0)
    return (
        outputs,
        unswapped(ig),
        counts,
        query_grad,
        smalls[:, : 2 * hs],
        out_grads,
        smalls[:, LANES : LANES + heads],
        smalls[:, LANES + heads : LANES + heads + 2],
        smalls[:, LANES + heads + 2 : LANES + heads + 4],
        ff_grad[:, :width],
        ff_grad[:, width:],
    )


def solution(mesh):
    in_specs = (
        P("dp", "mp", None),
        P("dp", None),
        P("dp", "mp", None),
        P("dp", "mp", None),
        P(("dp", "mp"), None),
        P(("dp", "mp"), None),
        P(("dp", "mp"), None),
        P(("dp", "mp"), None),
        P(("dp", "mp"), None),
        P(("dp", "mp"), None),
        P("dp", "mp"),
        P("dp", "mp"),
    )
    out_specs = (
        P("dp", "mp", None),
        P("dp", "mp", None),
        P(),
        P(("dp", "mp"), None),
        P(("dp", "mp"), None),
        P(("dp", "mp"), None),
        P(("dp", "mp"), None),
        P(("dp", "mp"), None),
        P(("dp", "mp"), None),
        P("dp", "mp"),
        P("dp", "mp"),
    )
    return jax.shard_map(shards, mesh=mesh, in_specs=in_specs, out_specs=out_specs, check_vma=False)
```

```python
import functools
import math
import jax
import jax.numpy as jnp
from jax import lax
from jax.experimental import pallas as pl
from jax.experimental.pallas import tpu as pltpu
from jax.sharding import PartitionSpec as P

epsilon = 1e-05
f32, bf16 = jnp.float32, jnp.bfloat16
NN = (((1,), (0,)), ((), ()))
NT = (((1,), (1,)), ((), ()))
LANES = 128
LOG2E = math.log2(math.e)
MIB = 2**20


def dot(left, right, dims=NN):
    return lax.dot_general(left, right, dims, preferred_element_type=f32)


def bits_of(axis):
    return (lax.axis_size(axis) - 1).bit_length()


def bit_groups(axis):
    count = bits_of(axis)
    groups, at = [], 0
    if count % 2:
        groups.append((0, 1))
        at = 1
    while at < count:
        groups.append((at, 2))
        at += 2
    return groups


def flip(x, axis, mask):
    return lax.ppermute(x, axis, [(i, i ^ mask) for i in range(lax.axis_size(axis))])


def after(x, *others):
    return lax.optimization_barrier((x, *others))[0]


def gather_bits(x, axis, group, dim, until=None):
    low, width = group
    mine = lax.axis_index(axis) >> low
    got = [flip(x, axis, k << low) for k in range(1, 2**width)]
    if until is not None:
        got = lax.optimization_barrier((*got, until))[:-1]
    shape = [1] * (x.ndim + 1)
    shape[dim] = 2**width
    way = lax.iota(jnp.int32, 2**width).reshape(shape) ^ (mine & (2**width - 1))
    pieces = [jnp.expand_dims(p, dim) for p in (x, *got)]
    for b in range(width):
        odd = (way >> b) & 1 == 1
        pieces = [jnp.where(odd, pieces[k + 1], pieces[k]) for k in range(0, len(pieces), 2)]
    return pieces[0]


def scatter_bits(x, axis, group, dim, until=None):
    low, width = group
    mine = (lax.axis_index(axis) >> low) & (2**width - 1)
    got = [
        flip(lax.dynamic_index_in_dim(x, mine ^ k, dim, keepdims=False), axis, k << low)
        for k in range(1, 2**width)
    ]
    if until is not None:
        got = lax.optimization_barrier((*got, until))[:-1]
    total = lax.dynamic_index_in_dim(x, mine, dim, keepdims=False).astype(f32)
    for g in got:
        total = total + g.astype(f32)
    return total


def halves(row_first, row_second, like):
    lane = lax.broadcasted_iota(jnp.int32, like, 1)
    return jnp.where(lane < LANES // 2, row_first, row_second)


def slot_experts(routes, pairs):
    shape = (routes.shape[0], LANES)
    return [halves(routes[:, 2 * j : 2 * j + 1], routes[:, 2 * j + 1 : 2 * j + 2], shape) for j in range(pairs)]


def turn_half(x):
    return pltpu.roll(x, LANES // 2, 1)


def compact(wide, experts, head_pairs):
    lane = lax.broadcasted_iota(jnp.int32, experts[0].shape, 1)
    high = (lane >= LANES // 2).astype(jnp.int32)
    straight = [e - high for e in experts]
    crossed = [e + high for e in experts]
    found = [jnp.zeros(experts[0].shape, f32) for _ in experts]
    for i in range(head_pairs):
        block = wide(i)
        turned = turn_half(block)
        for j in range(len(experts)):
            found[j] = jnp.where(straight[j] == 2 * i, block, found[j])
            found[j] = jnp.where(crossed[j] == 2 * i + 1, turned, found[j])
    return found


def expand(narrow, experts, head_pairs):
    lane = lax.broadcasted_iota(jnp.int32, experts[0].shape, 1)
    high = (lane >= LANES // 2).astype(jnp.int32)
    sources = []
    for block, e in zip(narrow, experts):
        sources.append((e - high, block))
        sources.append((turn_half(e) - high, turn_half(block)))
    wide = []
    for i in range(head_pairs):
        out = jnp.zeros(experts[0].shape, f32)
        for e, block in sources:
            out = jnp.where(e == 2 * i, block, out)
        wide.append(out.astype(bf16))
    return jnp.concatenate(wide, axis=1)


def split_core(value, core, per, send_ref, keep_ref):
    rows, columns = value.shape
    if per % 16 == 0:
        parts = value.reshape(rows // (2 * per), 2, per, columns)
        first, second = parts[:, 0], parts[:, 1]
        send = jnp.where(core == 0, second, first).reshape(rows // 2, columns)
        keep = jnp.where(core == 0, first, second).reshape(rows // 2, columns)
        send_ref[...], keep_ref[...] = send.astype(bf16), keep.astype(bf16)
        return
    shape = (rows // 2, rows)
    target, source = (lax.broadcasted_iota(jnp.int32, shape, i) for i in range(2))
    start = target // per * (2 * per) + target % per
    for ref, side in ((send_ref, 1 - core), (keep_ref, core)):
        chosen = (source == start + side * per).astype(bf16)
        ref[...] = dot(chosen, value.astype(bf16)).astype(bf16)


def normed_parts(values):
    mean = jnp.mean(values, axis=1, keepdims=True)
    centred = values - mean
    rstd = lax.rsqrt(jnp.mean(centred * centred, axis=1, keepdims=True) + epsilon)
    return centred * rstd, rstd


def norm_back(grad, normed, rstd, gain):
    scaled = grad * gain
    return rstd * (
        scaled
        - jnp.mean(scaled, axis=1, keepdims=True)
        - normed * jnp.mean(scaled * normed, axis=1, keepdims=True)
    )


def norm_kernel(x_ref, w_ref, n_ref, kv_ref, norms_ref, *, at_kv, at_misc, heads):
    misc = w_ref[:, at_misc : at_misc + LANES].astype(f32).T
    norms = misc[heads : heads + 8, :]
    norms = jnp.concatenate(
        [norms[0:2] + norms[2:4], norms[4:6] + norms[6:8], jnp.zeros_like(norms[0:4])], axis=0
    )
    norms_ref[...] = norms
    normed, _ = normed_parts(x_ref[0].astype(f32))
    low = (normed * norms[0:1] + norms[2:3]).astype(bf16)
    n_ref[0] = low
    kv_ref[0] = dot(low, w_ref[:, at_kv : at_kv + LANES]).astype(bf16)


def query_kernel(
    n_ref, w_ref, routes_ref, routes_t_ref, q_ref, gate_ref, gate_t_ref, *, at_misc, heads, slots, hs
):
    low = n_ref[0]
    head_pairs = heads // 2
    queries = dot(low, w_ref[:, : heads * hs]) * (hs**-0.5 * LOG2E)
    experts = slot_experts(routes_ref[0], slots // 2)
    found = compact(lambda i: queries[:, i * LANES : (i + 1) * LANES], experts, head_pairs)
    q_ref[0] = jnp.concatenate([f.astype(bf16) for f in found], axis=1)
    logits = dot(low, w_ref[:, at_misc : at_misc + LANES]).T[:heads, :]
    expert = lax.broadcasted_iota(jnp.int32, logits.shape, 0)
    routes_t = routes_t_ref[0]
    picked = [
        jnp.sum(jnp.where(expert == routes_t[s : s + 1, :], logits, 0.0), axis=0, keepdims=True)
        for s in range(slots)
    ]
    chosen = jnp.concatenate(picked, axis=0)
    lifted = jnp.exp(chosen - jnp.max(chosen, axis=0, keepdims=True))
    gate = lifted / jnp.sum(lifted, axis=0, keepdims=True)
    gate_t_ref[0] = gate
    padded = jnp.concatenate([gate, jnp.zeros((LANES - slots, gate.shape[1]), f32)], axis=0)
    gate_ref[0] = padded.T


def key_bias(first_key, first_query, start, keys, queries):
    key = first_key + lax.broadcasted_iota(jnp.int32, (keys, queries), 0)
    query = first_query + lax.broadcasted_iota(jnp.int32, (keys, queries), 1)
    return jnp.where((key <= query) & (key >= start), 0.0, -1e30)


def kv_place(row, chunk, single, rows, peers):
    half, owner = chunk % 2, chunk // 2
    owner = jnp.where((half == 1) & (row == single), peers - 1 - owner, owner)
    return owner * (2 * rows) + row * 2 + half


def over_keys(plan, start_ref, bias, block, keys, queries):
    b = pl.program_id(0)
    row, last, first, full = plan[4 * b], plan[4 * b + 1], plan[4 * b + 2], plan[4 * b + 3]

    def masked(i, carry):
        chunk = jnp.where(i == 0, last, first + i - 1)
        bias[...] = key_bias(chunk * keys, last * keys, start_ref[0], keys, queries)
        block(row, chunk, True)
        return carry

    def plain(chunk, carry):
        block(row, chunk, False)
        return carry

    lax.fori_loop(0, 1 + full - first, masked, 0)
    lax.fori_loop(full, last, plain, 0)


def attend_kernel(
    plan, q_ref, kv_ref, start_ref, gate_ref, out_ref, lse_ref, kvt, qt, acc, top, tot, bias, *, slots, hs, rows, peers
):
    queries, keys = q_ref.shape[1], kv_ref.shape[1]

    @pl.when(pl.program_id(0) == 0)
    def _():
        for i in range(kv_ref.shape[0]):
            kvt[i] = kv_ref[i].T

    qt[...] = q_ref[0].T
    acc[...] = jnp.zeros_like(acc)
    top[...] = jnp.full_like(top, -1e30)
    tot[...] = jnp.zeros_like(tot)
    part = [slice(h * hs, (h + 1) * hs) for h in range(slots)]

    def block(row, chunk, masked):
        at = kv_place(row, chunk, plan[8 * rows], rows, peers)
        k = kv_ref[at][:, :hs]
        vt = kvt[at, hs : 2 * hs, :]
        tops, tots = top[...], tot[...]
        scores = [dot(k, qt[part[h], :]) for h in range(slots)]
        if masked:
            scores = [s + bias[...] for s in scores]
        highest = [
            jnp.maximum(tops[h : h + 1], jnp.max(scores[h], axis=0, keepdims=True)) for h in range(slots)
        ]
        probs = [jnp.exp2(scores[h] - highest[h]) for h in range(slots)]
        shrink = [jnp.exp2(tops[h : h + 1] - highest[h]) for h in range(slots)]
        totals = [
            tots[h : h + 1] * shrink[h] + jnp.sum(probs[h], axis=0, keepdims=True) for h in range(slots)
        ]
        for h in range(slots):
            acc[part[h], :] = acc[part[h], :] * shrink[h] + dot(vt, probs[h].astype(bf16))
        top[...] = jnp.concatenate(highest, axis=0)
        tot[...] = jnp.concatenate(totals, axis=0)

    over_keys(plan, start_ref, bias, block, keys, queries)
    for h in range(slots):
        acc[part[h], :] = acc[part[h], :] * (gate_ref[0, h : h + 1, :] / tot[h : h + 1, :])
    lse_ref[0] = top[...] + jnp.log2(tot[...])
    out_ref[0] = acc[...].astype(bf16).T


def attend_back_kernel(
    plan, q_ref, g_ref, kv_ref, start_ref, lse_ref, delta_ref, dq_ref, send_ref, keep_ref,
    kvt, v_rows, qt, gt, dqt, dk, dv, bias, *, slots, hs, rows, peers,
):
    queries, keys = q_ref.shape[1], kv_ref.shape[1]
    b = pl.program_id(0)

    @pl.when(b == 0)
    def _():
        for i in range(kv_ref.shape[0]):
            kvt[i] = kv_ref[i].T
            v_rows[i] = kv_ref[i][:, hs:]
        dk[...] = jnp.zeros_like(dk)
        dv[...] = jnp.zeros_like(dv)

    qt[...] = q_ref[0].T
    gt[...] = g_ref[0].T
    dqt[...] = jnp.zeros_like(dqt)
    part = [slice(h * hs, (h + 1) * hs) for h in range(slots)]

    def block(row, chunk, masked):
        at = kv_place(row, chunk, plan[8 * rows], rows, peers)
        k = kv_ref[at][:, :hs]
        v = v_rows[at]
        kt = kvt[at, :hs, :]
        scores = [dot(k, qt[part[h], :]) for h in range(slots)]
        grads = [dot(v, gt[part[h], :]) for h in range(slots)]
        if masked:
            scores = [s + bias[...] for s in scores]
        probs = [jnp.exp2(scores[h] - lse_ref[0, h : h + 1, :]) for h in range(slots)]
        ds = [(probs[h] * (grads[h] - delta_ref[0, h : h + 1, :])).astype(bf16) for h in range(slots)]
        low = [p.astype(bf16) for p in probs]
        for h in range(slots):
            dqt[part[h], :] += dot(kt, ds[h])
        dk[at] += sum(dot(ds[h], qt[part[h], :], NT) for h in range(slots))
        dv[at] += sum(dot(low[h], gt[part[h], :], NT) for h in range(slots))

    over_keys(plan, start_ref, bias, block, keys, queries)
    dq_ref[0] = (dqt[...] * hs**-0.5).astype(bf16).T

    @pl.when(b == pl.num_programs(0) - 1)
    def _():
        core, each = plan[8 * rows + 1], kv_ref.shape[0] // peers
        for i in range(send_ref.shape[0]):
            at = i + each * (i // each)
            for ref, place in ((send_ref, at + each * (1 - core)), (keep_ref, at + each * core)):
                ref[i] = jnp.concatenate([dk[place] * (1.0 / LOG2E), dv[place]], axis=1).astype(bf16)


def forward_kernel(
    gc_ref, routes_ref, x_ref, og_ref, wo_ref, ff_ref, norms_ref,
    gated_ref, mid_ref, out_ref, back_ref, sum_ref, n2t, ogt, hid, gbef,
    *, heads, slots, width, blocks,
):
    step = pl.program_id(0)
    tokens, model = x_ref.shape[1], x_ref.shape[2]
    peers = ff_ref.shape[1]

    @pl.when(step < blocks)
    def _():
        pairs = slots // 2
        experts = slot_experts(routes_ref[0], pairs)
        gc = [gc_ref[0][:, j * LANES : (j + 1) * LANES].astype(f32) for j in range(pairs)]
        gated = expand(gc, experts, heads // 2)
        gated_ref[0] = gated
        middle = x_ref[0].astype(f32) + dot(gated, wo_ref[:, : gated.shape[1]], NT)
        mid_ref[0] = middle
        vhat, _ = normed_parts(middle)
        low = (vhat * norms_ref[1:2, :] + norms_ref[3:4, :]).astype(bf16)
        og = og_ref[0]
        n2t[step] = low.T
        ogt[step] = og.T
        out = middle
        back = jnp.zeros_like(out)
        slope = math.sqrt(2.0 / math.pi)
        for c in range(peers):
            up, down = (ff_ref[:, c, :, at : at + width].reshape(model, width) for at in (0, width))
            v = dot(low, up)
            square = v * v
            bent = jnp.tanh(slope * v * (1.0 + 0.044715 * square))
            rise = 0.5 * (1.0 + bent)
            hidden = (v * rise).astype(bf16)
            slant = rise + 0.5 * v * (1.0 - bent * bent) * (slope + 3.0 * slope * 0.044715 * square)
            before = (dot(og, down) * slant).astype(bf16)
            out = out + dot(hidden, down, NT)
            back = back + dot(before, up, NT)
            hid[c, step] = hidden
            gbef[c, step] = before
        out_ref[0] = out.astype(bf16)
        back_ref[0] = back

    @pl.when(step >= blocks)
    def _():
        c = step - blocks
        up = sum(dot(n2t[b], gbef[c, b]) for b in range(blocks))
        down = sum(dot(ogt[b], hid[c, b]) for b in range(blocks))
        shape = (sum_ref.shape[1], sum_ref.shape[2] // 2, sum_ref.shape[3])
        sum_ref[0] = jnp.concatenate([up.reshape(shape), down.reshape(shape)], axis=1).astype(bf16)


def branch_back_kernel(
    core, back_ref, mid_ref, og_ref, gc_ref, gate_ref, routes_ref, wo_ref, norms_ref, gated_ref,
    gm_ref, gatt_ref, delta_ref, glog_ref, sums_ref, send_ref, keep_ref, gbrt,
    *, heads, slots, hs, blocks, per,
):
    step = pl.program_id(0)

    @pl.when(step < blocks)
    def _():
        branch_back_block(
            step, back_ref, mid_ref, og_ref, gc_ref, gate_ref, routes_ref, wo_ref, norms_ref,
            gm_ref, gatt_ref, delta_ref, glog_ref, sums_ref, gbrt, heads, slots, hs,
        )

    @pl.when(step >= blocks)
    def _():
        total = sum(dot(gbrt[b], gated_ref[b]) for b in range(blocks))
        split_core(total, core[0], per, send_ref, keep_ref)


def branch_back_block(
    step, back_ref, mid_ref, og_ref, gc_ref, gate_ref, routes_ref, wo_ref, norms_ref,
    gm_ref, gatt_ref, delta_ref, glog_ref, sums_ref, gbrt, heads, slots, hs,
):
    tokens, model = mid_ref.shape[1], mid_ref.shape[2]
    head_pairs, pairs = heads // 2, slots // 2
    experts = slot_experts(routes_ref[0], pairs)
    back = back_ref[0]
    vhat, rstd = normed_parts(mid_ref[0])
    gm = og_ref[0].astype(f32) + norm_back(back, vhat, rstd, norms_ref[1:2, :])
    gm_ref[0] = gm

    @pl.when(step == 0)
    def _():
        sums_ref[...] = jnp.zeros_like(sums_ref)

    sums_ref[0:1, :] += jnp.sum(back * vhat, axis=0, keepdims=True)
    sums_ref[1:2, :] += jnp.sum(back, axis=0, keepdims=True)
    gbr = gm.astype(bf16)
    gbrt[step] = gbr.T
    wide = dot(gbr, wo_ref[:, : heads * hs])
    found = compact(lambda i: wide[:, i * LANES : (i + 1) * LANES], experts, head_pairs)
    gate = gate_ref[0]
    shape = (tokens, LANES)
    attended, products = [], []
    for j in range(pairs):
        spread = halves(gate[:, 2 * j : 2 * j + 1], gate[:, 2 * j + 1 : 2 * j + 2], shape)
        attended.append((found[j] * spread).astype(bf16))
        products.append(found[j] * gc_ref[0][:, j * LANES : (j + 1) * LANES].astype(f32))
    gatt_ref[0] = jnp.concatenate(attended, axis=1)
    product = jnp.concatenate(products, axis=1)
    owner = lax.broadcasted_iota(jnp.int32, (slots * hs, LANES), 0) // hs
    ones = (owner == lax.broadcasted_iota(jnp.int32, (slots * hs, LANES), 1)).astype(bf16)
    coarse = product.astype(bf16)
    fine = (product - coarse.astype(f32)).astype(bf16)
    inner = dot(coarse, ones) + dot(fine, ones)
    delta_ref[0] = inner.T[:slots, :]
    logit = inner - gate * jnp.sum(inner, axis=1, keepdims=True)
    lane = lax.broadcasted_iota(jnp.int32, shape, 1)
    spread_out = jnp.zeros(shape, f32)
    routes = routes_ref[0]
    for s in range(slots):
        spread_out = jnp.where(lane == routes[:, s : s + 1], logit[:, s : s + 1], spread_out)
    glog_ref[0] = spread_out.astype(bf16)


def query_weights_kernel(
    core, dq_ref, routes_ref, n_ref, send_ref, keep_ref, wide_ref, acc, *, heads, slots, per
):
    pairs = slots // 2
    experts = slot_experts(routes_ref[0], pairs)
    dq = [dq_ref[0][:, j * LANES : (j + 1) * LANES].astype(f32) for j in range(pairs)]
    wide = expand(dq, experts, heads // 2)
    wide_ref[0] = wide

    @pl.when(pl.program_id(0) == 0)
    def _():
        acc[...] = jnp.zeros_like(acc)

    acc[...] += dot(n_ref[0].T, wide)

    @pl.when(pl.program_id(0) == pl.num_programs(0) - 1)
    def _():
        split_core(acc[...], core[0], per, send_ref, keep_ref)


def input_kernel(
    wide_ref, glog_ref, dkv_ref, w_ref, x_ref, n_ref, gm_ref, norms_ref, sums_ref,
    ig_ref, small_ref, acck, accr, sums, *, at_kv, at_misc, heads,
):
    dkv, glog = dkv_ref[0], glog_ref[0]
    dn = (
        dot(wide_ref[0], w_ref[:, :at_kv], NT)
        + dot(dkv, w_ref[:, at_kv:at_misc], NT)
        + dot(glog, w_ref[:, at_misc : at_misc + LANES], NT)
    )
    vhat, rstd = normed_parts(x_ref[0].astype(f32))
    ig_ref[0] = gm_ref[0] + norm_back(dn, vhat, rstd, norms_ref[0:1, :])

    @pl.when(pl.program_id(0) == 0)
    def _():
        acck[...] = jnp.zeros_like(acck)
        accr[...] = jnp.zeros_like(accr)
        sums[...] = jnp.zeros_like(sums)

    nt = n_ref[0].T
    acck[...] += dot(nt, dkv)
    accr[...] += dot(nt, glog)
    sums[0:1, :] += jnp.sum(dn * vhat, axis=0, keepdims=True)
    sums[1:2, :] += jnp.sum(dn, axis=0, keepdims=True)

    @pl.when(pl.program_id(0) == pl.num_programs(0) - 1)
    def _():
        second = sums_ref[...]
        model = second.shape[1]
        rows = jnp.concatenate(
            [
                jnp.zeros((heads, model), f32),
                sums[0:1, :], second[0:1, :], sums[1:2, :], second[1:2, :],
                jnp.zeros((LANES - heads - 4, model), f32),
            ],
            axis=0,
        )
        small_ref[:, :LANES] = acck[...].astype(bf16)
        small_ref[:, LANES:] = (accr[...] + rows.T).astype(bf16)


def fixed(shape):
    return pl.BlockSpec(shape, lambda b, *_: (0,) * len(shape))


def per_block(*shape):
    return pl.BlockSpec((1, *shape), lambda b, *_: (b,) + (0,) * len(shape))


def like(shape, kind):
    return jax.ShapeDtypeStruct(shape, kind)


def cost(flops, size, exps=0):
    return pl.CostEstimate(flops=int(flops), bytes_accessed=int(size), transcendentals=int(exps))


def shards(
    tokens, segment_ids, routes, out_grad, w_query, w_keyval, w_output, w_router,
    norm_gains, norm_biases, w_up, w_down,
):
    rows, local, model = tokens.shape
    peers = lax.axis_size("mp")
    slots = routes.shape[2]
    heads = w_router.shape[1]
    hs = w_keyval.shape[1] // 2
    width = w_up.shape[1]
    chunk = local // 2
    blocks = rows * 2
    count = rows * local
    place = lax.axis_index("mp")
    wide = heads * hs
    slim = slots * hs
    at_kv, at_misc = wide, wide + 2 * hs

    def two(v):
        high = lax.reduce_precision(v, 8, 7)
        return [high.astype(bf16), (v - high).astype(bf16)]

    pads = jnp.zeros((w_query.shape[0], LANES - heads - 8), bf16)
    first = jnp.concatenate(
        [w_query, w_keyval, w_router, *two(norm_gains), *two(norm_biases), pads], axis=1
    )
    dp_groups = bit_groups("dp")
    far_groups, near_group = dp_groups[1:], dp_groups[0]
    depth = len(dp_groups)

    def far_stage(a, until=None):
        for i, group in enumerate(reversed(far_groups)):
            a = gather_bits(a, "dp", group, i, until)
        return a

    both = jnp.concatenate([w_up, w_down], axis=1)
    feed = lax.all_gather(both, ("dp", "mp"), axis=0, tiled=False)
    feed = feed.reshape(lax.axis_size("dp"), peers, *both.shape)
    y_bit, core_bit = (1, 1), (0, 1)
    first = far_stage(first)
    chosen = after(routes, first)
    chosen = (chosen[..., None] == jnp.arange(heads, dtype=jnp.int32)).astype(f32)
    held = jnp.sum(chosen, axis=(0, 1, 2))
    held_high = lax.reduce_precision(held, 8, 7)
    held = jnp.concatenate([held_high, held - held_high, jnp.zeros(LANES - 2 * heads, f32)])
    held = jnp.broadcast_to(held.astype(bf16), (w_output.shape[0], LANES))
    first_y = gather_bits(first, "mp", y_bit, depth - 1)
    proj = far_stage(after(jnp.concatenate([w_output, held], axis=1), first), first_y)
    first_x = gather_bits(first_y, "dp", near_group, depth - 1)
    first = gather_bits(first_x, "mp", core_bit, depth + 1)
    proj = gather_bits(after(proj, first_y), "mp", y_bit, depth - 1, first)
    weights = first.reshape(model, at_misc + LANES)

    single = jnp.argmax(segment_ids[:, -1] == 0).astype(jnp.int32)

    def swapped(a, start=None, until=None):
        kind = a.dtype
        if start is not None:
            a = after(a, start)
        a = a.reshape(rows, 2, chunk, -1)
        piece = lax.dynamic_index_in_dim(a[:, 1], single, 0, keepdims=False)
        piece = flip(piece.astype(bf16), "mp", peers - 1)
        if until is not None:
            piece = after(piece, until)
        return lax.dynamic_update_slice(a, piece.astype(kind)[None, None], (single, 1, 0, 0))

    def blocked(a):
        return a.reshape(blocks, chunk, -1)

    x = blocked(swapped(tokens))
    picks = blocked(swapped(routes, first_y, first_x))
    picks_t = jnp.swapaxes(picks, 1, 2)
    segments = after(segment_ids, first_x)
    near, far = 2 * place, 2 * (peers - 1 - place) + 1
    one = jnp.arange(rows, dtype=jnp.int32) == single
    last = jnp.stack(
        [jnp.full((rows,), near, jnp.int32), jnp.where(one, far, near + 1).astype(jnp.int32)], axis=1
    )
    ids = jnp.arange(8, dtype=jnp.int32)
    sizes = jnp.sum((segments[:, :, None] == ids).astype(jnp.int32), axis=1)
    own = jnp.stack(
        [
            jnp.stack(
                [lax.dynamic_slice(segments, (r, last[r, i] * chunk), (1, chunk))[0] for i in range(2)]
            )
            for r in range(rows)
        ]
    )
    start = jnp.sum(jnp.where(ids < own[..., None], sizes[:, None, None, :], 0), axis=-1)
    full = jnp.minimum((start[:, :, -1] + chunk - 1) // chunk, last)
    which = jnp.broadcast_to(jnp.arange(rows, dtype=jnp.int32)[:, None], (rows, 2))
    plan = jnp.stack([which, last, start[:, :, 0] // chunk, full], axis=-1).astype(jnp.int32)
    plan = jnp.concatenate([plan.reshape(-1), single[None], (place & 1).astype(jnp.int32)[None]])
    start = start.astype(jnp.int32).reshape(blocks, 1, chunk)

    n1, kv, norms = pl.pallas_call(
        functools.partial(norm_kernel, at_kv=at_kv, at_misc=at_misc, heads=heads),
        grid=(blocks,),
        in_specs=[per_block(chunk, model), fixed(weights.shape)],
        out_specs=[per_block(chunk, model), per_block(chunk, 2 * hs), fixed((8, model))],
        out_shape=[
            like((blocks, chunk, model), bf16),
            like((blocks, chunk, 2 * hs), bf16),
            like((8, model), f32),
        ],
        cost_estimate=cost(2 * count * model * LANES, 4 * MIB),
        name="norm_one",
    )(x, weights)
    kv_half = gather_bits(kv, "mp", y_bit, 0)
    kv_all = gather_bits(kv_half, "mp", core_bit, 1).reshape(peers * blocks, chunk, 2 * hs)
    proj = gather_bits(after(proj, weights), "dp", near_group, depth - 1, kv_half)

    q, gate, gate_t = pl.pallas_call(
        functools.partial(query_kernel, at_misc=at_misc, heads=heads, slots=slots, hs=hs),
        grid=(blocks,),
        in_specs=[
            per_block(chunk, model), fixed(weights.shape), per_block(chunk, slots), per_block(slots, chunk),
        ],
        out_specs=[per_block(chunk, slim), per_block(chunk, LANES), per_block(slots, chunk)],
        out_shape=[
            like((blocks, chunk, slim), bf16),
            like((blocks, chunk, LANES), f32),
            like((blocks, slots, chunk), f32),
        ],
        compiler_params=pltpu.CompilerParams(vmem_limit_bytes=24 * MIB),
        cost_estimate=cost(2 * count * model * wide * 2, 6 * MIB),
        name="queries",
    )(n1, weights, picks, picks_t)

    attention = dict(slots=slots, hs=hs, rows=rows, peers=peers)
    total = peers * blocks
    gc, lse = pl.pallas_call(
        functools.partial(attend_kernel, **attention),
        grid_spec=pltpu.PrefetchScalarGridSpec(
            num_scalar_prefetch=1,
            grid=(blocks,),
            in_specs=[
                per_block(chunk, slim), fixed(kv_all.shape), per_block(1, chunk), per_block(slots, chunk),
            ],
            out_specs=[per_block(chunk, slim), per_block(slots, chunk)],
            scratch_shapes=[
                pltpu.VMEM((total, 2 * hs, chunk), bf16),
                pltpu.VMEM((slim, chunk), bf16),
                pltpu.VMEM((slim, chunk), f32),
                pltpu.VMEM((slots, chunk), f32),
                pltpu.VMEM((slots, chunk), f32),
                pltpu.VMEM((chunk, chunk), f32),
            ],
        ),
        out_shape=[like((blocks, chunk, slim), bf16), like((blocks, slots, chunk), f32)],
        compiler_params=pltpu.CompilerParams(vmem_limit_bytes=24 * MIB),
        cost_estimate=cost(12e9, 4 * MIB),
        name="attend",
    )(plan, q, kv_all, start, gate_t)

    proj = gather_bits(proj, "mp", core_bit, depth + 1, gc).reshape(model, wide + LANES)
    grads = blocked(swapped(out_grad, kv_half, gc))
    core = (place & 1).astype(jnp.int32)[None]
    pair = peers // 2
    per = w_query.shape[0]

    def early(*shape):
        return pl.BlockSpec((1, *shape), lambda b, *_: (jnp.minimum(b, blocks - 1),) + (0,) * len(shape))

    def once(shape):
        return pl.BlockSpec(shape, lambda b, *_: (0,) * len(shape), pipeline_mode=pl.Buffered(1))

    feed_shape = (lax.axis_size("dp"), 2 * w_up.shape[0], width)
    gated, mid, outs, back, feed_sum = pl.pallas_call(
        functools.partial(forward_kernel, heads=heads, slots=slots, width=width, blocks=blocks),
        grid=(blocks + peers,),
        in_specs=[
            early(chunk, slim), early(chunk, slots), early(chunk, model), early(chunk, model),
            once(proj.shape), once(feed.shape), once(norms.shape),
        ],
        out_specs=[
            early(chunk, wide), early(chunk, model), early(chunk, model), early(chunk, model),
            pl.BlockSpec((1, *feed_shape), lambda b: (jnp.maximum(b - blocks, 0), 0, 0, 0)),
        ],
        scratch_shapes=[
            pltpu.VMEM((blocks, model, chunk), bf16),
            pltpu.VMEM((blocks, model, chunk), bf16),
            pltpu.VMEM((peers, blocks, chunk, width), bf16),
            pltpu.VMEM((peers, blocks, chunk, width), bf16),
        ],
        out_shape=[
            like((blocks, chunk, wide), bf16),
            like((blocks, chunk, model), f32),
            like((blocks, chunk, model), bf16),
            like((blocks, chunk, model), f32),
            like((peers, *feed_shape), bf16),
        ],
        compiler_params=pltpu.CompilerParams(vmem_limit_bytes=60 * MIB),
        cost_estimate=cost(24e9, 24 * MIB),
        name="forward",
    )(gc, picks, x, grads, proj, feed, norms)

    part, parts = model, wide // model

    def late_columns(b, core):
        return 0, jnp.maximum(b - blocks, 0)

    gm, gatt, delta, glog, sums, out_send, out_keep = pl.pallas_call(
        functools.partial(branch_back_kernel, heads=heads, slots=slots, hs=hs, blocks=blocks, per=per),
        grid_spec=pltpu.PrefetchScalarGridSpec(
            num_scalar_prefetch=1,
            grid=(blocks + parts,),
            in_specs=[
                early(chunk, model), early(chunk, model), early(chunk, model),
                early(chunk, slim), early(chunk, LANES), early(chunk, slots),
                once(proj.shape), once(norms.shape),
                pl.BlockSpec((blocks, chunk, part), lambda b, core: (0, *late_columns(b, core))),
            ],
            out_specs=[
                early(chunk, model), early(chunk, slim),
                early(slots, chunk), early(chunk, LANES), fixed((8, model)),
                pl.BlockSpec((model // 2, part), late_columns),
                pl.BlockSpec((model // 2, part), late_columns),
            ],
            scratch_shapes=[pltpu.VMEM((blocks, model, chunk), bf16)],
        ),
        out_shape=[
            like((blocks, chunk, model), f32),
            like((blocks, chunk, slim), bf16),
            like((blocks, slots, chunk), f32),
            like((blocks, chunk, LANES), bf16),
            like((8, model), f32),
            like((model // 2, wide), bf16),
            like((model // 2, wide), bf16),
        ],
        compiler_params=pltpu.CompilerParams(vmem_limit_bytes=60 * MIB),
        cost_estimate=cost(8e9, 14 * MIB),
        name="branch_back",
    )(core, back, mid, grads, gc, gate, picks, proj, norms, gated)

    def low_bits(a, axis, group, dim, until=None):
        return scatter_bits(a, axis, group, dim, until).astype(bf16)

    def across(send, keep, until):
        got = flip(send, "mp", 1)
        if until is not None:
            got = after(got, until)
        return (keep.astype(f32) + got.astype(f32)).astype(bf16)

    def far_scatter(a, until=None):
        for i, group in enumerate(far_groups):
            a = scatter_bits(a, "dp", group, depth - 2 - i, until)
            if i < len(far_groups) - 1:
                a = a.astype(bf16)
        return a

    def across(send, keep, until):
        got = flip(send, "mp", 1)
        if until is not None:
            got = after(got, until)
        return (keep.astype(f32) + got.astype(f32)).astype(bf16)

    groups = [2**bits for _, bits in reversed(dp_groups)]
    feed_part = lax.psum_scatter(feed_sum, "mp", scatter_dimension=0, tiled=False)
    feed_part = feed_part.reshape(*groups, *feed_shape[1:])
    half_kv = (total // 2, chunk, 2 * hs)
    dq, dkv_send, dkv_keep = pl.pallas_call(
        functools.partial(attend_back_kernel, **attention),
        grid_spec=pltpu.PrefetchScalarGridSpec(
            num_scalar_prefetch=1,
            grid=(blocks,),
            in_specs=[
                per_block(chunk, slim), per_block(chunk, slim), fixed(kv_all.shape), per_block(1, chunk),
                per_block(slots, chunk), per_block(slots, chunk),
            ],
            out_specs=[per_block(chunk, slim), fixed(half_kv), fixed(half_kv)],
            scratch_shapes=[
                pltpu.VMEM((total, 2 * hs, chunk), bf16),
                pltpu.VMEM((total, chunk, hs), bf16),
                pltpu.VMEM((slim, chunk), bf16),
                pltpu.VMEM((slim, chunk), bf16),
                pltpu.VMEM((slim, chunk), f32),
                pltpu.VMEM((total, chunk, hs), f32),
                pltpu.VMEM((total, chunk, hs), f32),
                pltpu.VMEM((chunk, chunk), f32),
            ],
        ),
        out_shape=[like((blocks, chunk, slim), bf16), like(half_kv, bf16), like(half_kv, bf16)],
        compiler_params=pltpu.CompilerParams(vmem_limit_bytes=32 * MIB),
        cost_estimate=cost(25e9, 6 * MIB),
        name="attend_back",
    )(plan, q, gatt, kv_all, start, lse, delta)

    outputs = swapped(outs, gatt, dq).reshape(rows, local, model)
    wq_send, wq_keep, spread = pl.pallas_call(
        functools.partial(query_weights_kernel, heads=heads, slots=slots, per=per),
        grid_spec=pltpu.PrefetchScalarGridSpec(
            num_scalar_prefetch=1,
            grid=(blocks,),
            in_specs=[per_block(chunk, slim), per_block(chunk, slots), per_block(chunk, model)],
            out_specs=[
                fixed((model // 2, wide)), fixed((model // 2, wide)), per_block(chunk, wide),
            ],
            scratch_shapes=[pltpu.VMEM((model, wide), f32)],
        ),
        out_shape=[
            like((model // 2, wide), bf16),
            like((model // 2, wide), bf16),
            like((blocks, chunk, wide), bf16),
        ],
        compiler_params=pltpu.CompilerParams(vmem_limit_bytes=28 * MIB),
        cost_estimate=cost(4e9, 10 * MIB),
        name="query_weights",
    )(core, dq, picks, n1)
    feed_part = low_bits(after(feed_part, dq), "dp", near_group, depth - 1, wq_send)
    out_part = across(out_send, out_keep, dq).reshape(*groups, 2, per, wide)
    out_part = low_bits(out_part, "mp", y_bit, depth, wq_send)
    dkv = across(dkv_send, dkv_keep, wq_send).reshape(pair, blocks * chunk, 2 * hs)
    dkv = low_bits(dkv, "mp", y_bit, 0).reshape(blocks, chunk, 2 * hs)
    query_part = across(wq_send, wq_keep, None).reshape(*groups, 2, per, wide)

    ig, small = pl.pallas_call(
        functools.partial(input_kernel, at_kv=at_kv, at_misc=at_misc, heads=heads),
        grid=(blocks,),
        in_specs=[
            per_block(chunk, wide), per_block(chunk, LANES), per_block(chunk, 2 * hs),
            fixed(weights.shape), per_block(chunk, model), per_block(chunk, model),
            per_block(chunk, model), fixed((8, model)), fixed((8, model)),
        ],
        out_specs=[per_block(chunk, model), fixed((model, 2 * LANES))],
        out_shape=[like((blocks, chunk, model), f32), like((model, 2 * LANES), bf16)],
        scratch_shapes=[
            pltpu.VMEM((model, 2 * hs), f32), pltpu.VMEM((model, LANES), f32), pltpu.VMEM((8, model), f32),
        ],
        compiler_params=pltpu.CompilerParams(vmem_limit_bytes=28 * MIB),
        cost_estimate=cost(4e9, 12 * MIB),
        name="inputs_back",
    )(after(spread, query_part), glog, dkv, weights, x, n1, gm, norms, sums)

    feed_grad = far_scatter(feed_part, ig)
    query_part = low_bits(query_part, "mp", y_bit, depth, ig)
    joint = jnp.concatenate([query_part, out_part], axis=-1)
    joint = low_bits(joint, "dp", near_group, depth - 1)
    tiles = after(small, query_part).reshape(model // per, per, 2 * LANES)
    tiles = lax.all_to_all(tiles, ("dp", "mp"), split_axis=0, concat_axis=0, tiled=True)
    smalls = jnp.sum(tiles.astype(f32), axis=0)
    up_rows = w_up.shape[0]
    joint = far_scatter(joint)
    input_grad = swapped(ig).reshape(rows, local, model)
    tallies = jnp.sum(proj.reshape(-1, per, wide + LANES)[:, 0, wide:].astype(f32), axis=0)
    counts = tallies[:heads] + tallies[heads : 2 * heads]
    return (
        outputs,
        input_grad,
        counts,
        joint[:, :wide],
        smalls[:, : 2 * hs],
        joint[:, wide:],
        smalls[:, LANES : LANES + heads],
        smalls[:, LANES + heads : LANES + heads + 2],
        smalls[:, LANES + heads + 2 : LANES + heads + 4],
        feed_grad[:up_rows],
        feed_grad[up_rows:],
    )


def solution(mesh):
    in_specs = (
        P("dp", "mp", None),
        P("dp", None),
        P("dp", "mp", None),
        P("dp", "mp", None),
        P(("dp", "mp"), None),
        P(("dp", "mp"), None),
        P(("dp", "mp"), None),
        P(("dp", "mp"), None),
        P(("dp", "mp"), None),
        P(("dp", "mp"), None),
        P("dp", "mp"),
        P("dp", "mp"),
    )
    out_specs = (
        P("dp", "mp", None),
        P("dp", "mp", None),
        P(),
        P(("dp", "mp"), None),
        P(("dp", "mp"), None),
        P(("dp", "mp"), None),
        P(("dp", "mp"), None),
        P(("dp", "mp"), None),
        P(("dp", "mp"), None),
        P("dp", "mp"),
        P("dp", "mp"),
    )
    return jax.shard_map(shards, mesh=mesh, in_specs=in_specs, out_specs=out_specs, check_vma=False)
```

```python
import functools
import math
import jax
import jax.numpy as jnp
from jax import lax
from jax.experimental import pallas as pl
from jax.experimental.pallas import tpu as pltpu
from jax.sharding import PartitionSpec as P

epsilon = 1e-05
f32, bf16 = jnp.float32, jnp.bfloat16
NN = (((1,), (0,)), ((), ()))
NT = (((1,), (1,)), ((), ()))
LANES = 128
LOG2E = math.log2(math.e)
MIB = 2**20


def dot(left, right, dims=NN):
    return lax.dot_general(left, right, dims, preferred_element_type=f32)


def bits_of(axis):
    return (lax.axis_size(axis) - 1).bit_length()


def bit_groups(axis):
    count = bits_of(axis)
    groups, at = [], 0
    if count % 2:
        groups.append((0, 1))
        at = 1
    while at < count:
        groups.append((at, 2))
        at += 2
    return groups


def flip(x, axis, mask):
    return lax.ppermute(x, axis, [(i, i ^ mask) for i in range(lax.axis_size(axis))])


def after(x, *others):
    return lax.optimization_barrier((x, *others))[0]


def gather_bits(x, axis, group, dim, until=None):
    low, width = group
    mine = lax.axis_index(axis) >> low
    got = [flip(x, axis, k << low) for k in range(1, 2**width)]
    if until is not None:
        got = lax.optimization_barrier((*got, until))[:-1]
    shape = [1] * (x.ndim + 1)
    shape[dim] = 2**width
    way = lax.iota(jnp.int32, 2**width).reshape(shape) ^ (mine & (2**width - 1))
    pieces = [jnp.expand_dims(p, dim) for p in (x, *got)]
    for b in range(width):
        odd = (way >> b) & 1 == 1
        pieces = [jnp.where(odd, pieces[k + 1], pieces[k]) for k in range(0, len(pieces), 2)]
    return pieces[0]


def scatter_start(x, axis, group, dim):
    low, width = group
    mine = (lax.axis_index(axis) >> low) & (2**width - 1)
    sent = [
        lax.dynamic_index_in_dim(x, mine ^ k, dim, keepdims=False) for k in range(1, 2**width)
    ]
    got = [flip(a, axis, k << low) for k, a in enumerate(sent, 1)]
    return lax.dynamic_index_in_dim(x, mine, dim, keepdims=False), got, sent


def scatter_end(started, until=None):
    total, got, _ = started
    if until is not None:
        got = lax.optimization_barrier((*got, until))[:-1]
    total = total.astype(f32)
    for g in got:
        total = total + g.astype(f32)
    return total


def scatter_bits(x, axis, group, dim, until=None):
    return scatter_end(scatter_start(x, axis, group, dim), until)


def halves(row_first, row_second, like):
    lane = lax.broadcasted_iota(jnp.int32, like, 1)
    return jnp.where(lane < LANES // 2, row_first, row_second)


def slot_experts(routes, pairs):
    shape = (routes.shape[0], LANES)
    return [halves(routes[:, 2 * j : 2 * j + 1], routes[:, 2 * j + 1 : 2 * j + 2], shape) for j in range(pairs)]


def turn_half(x):
    return pltpu.roll(x, LANES // 2, 1)


def compact(wide, experts, head_pairs):
    lane = lax.broadcasted_iota(jnp.int32, experts[0].shape, 1)
    high = (lane >= LANES // 2).astype(jnp.int32)
    straight = [(e - high).astype(jnp.int16) for e in experts]
    crossed = [(e + high).astype(jnp.int16) for e in experts]
    found = [jnp.zeros(experts[0].shape, bf16) for _ in experts]
    for i in range(head_pairs):
        block = wide(i)
        turned = turn_half(block).astype(bf16)
        block = block.astype(bf16)
        for j in range(len(experts)):
            found[j] = jnp.where(straight[j] == jnp.int16(2 * i), block, found[j])
            found[j] = jnp.where(crossed[j] == jnp.int16(2 * i + 1), turned, found[j])
    return found


def expand(narrow, experts, head_pairs):
    lane = lax.broadcasted_iota(jnp.int32, experts[0].shape, 1)
    high = (lane >= LANES // 2).astype(jnp.int32)
    sources = []
    for block, e in zip(narrow, experts):
        sources.append(((e - high).astype(jnp.int16), block.astype(bf16)))
        sources.append(((turn_half(e) - high).astype(jnp.int16), turn_half(block).astype(bf16)))
    wide = []
    for i in range(head_pairs):
        out = jnp.zeros(experts[0].shape, bf16)
        for e, block in sources:
            out = jnp.where(e == jnp.int16(2 * i), block, out)
        wide.append(out)
    return jnp.concatenate(wide, axis=1)


def split_core(value, core, per, send_ref, keep_ref):
    rows, columns = value.shape
    if per % 16 == 0:
        parts = value.reshape(rows // (2 * per), 2, per, columns)
        first, second = parts[:, 0], parts[:, 1]
        send = jnp.where(core == 0, second, first).reshape(rows // 2, columns)
        keep = jnp.where(core == 0, first, second).reshape(rows // 2, columns)
        send_ref[...], keep_ref[...] = send.astype(bf16), keep.astype(bf16)
        return
    shape = (rows // 2, rows)
    target, source = (lax.broadcasted_iota(jnp.int32, shape, i) for i in range(2))
    start = target // per * (2 * per) + target % per
    for ref, side in ((send_ref, 1 - core), (keep_ref, core)):
        chosen = (source == start + side * per).astype(bf16)
        ref[...] = dot(chosen, value.astype(bf16)).astype(bf16)


def normed_parts(values):
    mean = jnp.mean(values, axis=1, keepdims=True)
    centred = values - mean
    rstd = lax.rsqrt(jnp.mean(centred * centred, axis=1, keepdims=True) + epsilon)
    return centred * rstd, rstd


def norm_back(grad, normed, rstd, gain):
    scaled = grad * gain
    return rstd * (
        scaled
        - jnp.mean(scaled, axis=1, keepdims=True)
        - normed * jnp.mean(scaled * normed, axis=1, keepdims=True)
    )


def norm_kernel(x_ref, w_ref, n_ref, kv_ref, norms_ref, *, heads):
    misc = w_ref[:, -LANES:].astype(f32).T
    norms = misc[heads : heads + 8, :]
    norms = jnp.concatenate(
        [norms[0:2] + norms[2:4], norms[4:6] + norms[6:8], jnp.zeros_like(norms[0:4])], axis=0
    )
    norms_ref[...] = norms
    normed, _ = normed_parts(x_ref[0].astype(f32))
    low = (normed * norms[0:1] + norms[2:3]).astype(bf16)
    n_ref[0] = low
    kv_ref[0] = dot(low, w_ref[:, : kv_ref.shape[2]]).astype(bf16)


def query_kernel(
    n_ref, w_ref, few_ref, routes_ref, routes_t_ref, q_ref, gate_ref, gate_t_ref, *, heads, slots, hs
):
    low = n_ref[0]
    head_pairs = heads // 2
    queries = dot(low, w_ref[...]) * (hs**-0.5 * LOG2E)
    experts = slot_experts(routes_ref[0], slots // 2)
    found = compact(lambda i: queries[:, i * LANES : (i + 1) * LANES], experts, head_pairs)
    q_ref[0] = jnp.concatenate(found, axis=1)
    logits = dot(low, few_ref[:, -LANES:]).T[:heads, :]
    expert = lax.broadcasted_iota(jnp.int32, logits.shape, 0)
    routes_t = routes_t_ref[0]
    picked = [
        jnp.sum(jnp.where(expert == routes_t[s : s + 1, :], logits, 0.0), axis=0, keepdims=True)
        for s in range(slots)
    ]
    chosen = jnp.concatenate(picked, axis=0)
    lifted = jnp.exp(chosen - jnp.max(chosen, axis=0, keepdims=True))
    gate = lifted / jnp.sum(lifted, axis=0, keepdims=True)
    gate_t_ref[0] = gate
    padded = jnp.concatenate([gate, jnp.zeros((LANES - slots, gate.shape[1]), f32)], axis=0)
    gate_ref[0] = padded.T


def key_bias(first_key, first_query, start, keys, queries):
    key = first_key + lax.broadcasted_iota(jnp.int32, (keys, queries), 0)
    query = first_query + lax.broadcasted_iota(jnp.int32, (keys, queries), 1)
    return jnp.where((key <= query) & (key >= start), 0.0, -1e30)


def kv_place(row, chunk, single, rows, peers):
    half, owner = chunk % 2, chunk // 2
    owner = jnp.where((half == 1) & (row == single), peers - 1 - owner, owner)
    return owner * (2 * rows) + row * 2 + half


def over_keys(plan, start_ref, bias, block, keys, queries):
    b = pl.program_id(0)
    row, last, first, full = plan[4 * b], plan[4 * b + 1], plan[4 * b + 2], plan[4 * b + 3]

    def masked(i, carry):
        chunk = jnp.where(i == 0, last, first + i - 1)
        bias[...] = key_bias(chunk * keys, last * keys, start_ref[0], keys, queries)
        block(row, chunk, True)
        return carry

    def plain(chunk, carry):
        block(row, chunk, False)
        return carry

    lax.fori_loop(0, 1 + full - first, masked, 0)
    lax.fori_loop(full, last, plain, 0)


def attend_kernel(
    plan, q_ref, kv_ref, start_ref, gate_ref, out_ref, lse_ref, kvt, qt, acc, top, tot, bias, *, slots, hs, rows, peers
):
    queries, keys = q_ref.shape[1], kv_ref.shape[1]

    @pl.when(pl.program_id(0) == 0)
    def _():
        for i in range(kv_ref.shape[0]):
            kvt[i] = kv_ref[i].T

    qt[...] = q_ref[0].T
    acc[...] = jnp.zeros_like(acc)
    top[...] = jnp.full_like(top, -1e30)
    tot[...] = jnp.zeros_like(tot)
    part = [slice(h * hs, (h + 1) * hs) for h in range(slots)]

    def block(row, chunk, masked):
        at = kv_place(row, chunk, plan[8 * rows], rows, peers)
        k = kv_ref[at][:, :hs]
        vt = kvt[at, hs : 2 * hs, :]
        tops, tots = top[...], tot[...]
        scores = [dot(k, qt[part[h], :]) for h in range(slots)]
        if masked:
            scores = [s + bias[...] for s in scores]
        highest = [
            jnp.maximum(tops[h : h + 1], jnp.max(scores[h], axis=0, keepdims=True)) for h in range(slots)
        ]
        probs = [jnp.exp2(scores[h] - highest[h]) for h in range(slots)]
        shrink = [jnp.exp2(tops[h : h + 1] - highest[h]) for h in range(slots)]
        totals = [
            tots[h : h + 1] * shrink[h] + jnp.sum(probs[h], axis=0, keepdims=True) for h in range(slots)
        ]
        for h in range(slots):
            acc[part[h], :] = acc[part[h], :] * shrink[h] + dot(vt, probs[h].astype(bf16))
        top[...] = jnp.concatenate(highest, axis=0)
        tot[...] = jnp.concatenate(totals, axis=0)

    over_keys(plan, start_ref, bias, block, keys, queries)
    for h in range(slots):
        acc[part[h], :] = acc[part[h], :] * (gate_ref[0, h : h + 1, :] / tot[h : h + 1, :])
    lse_ref[0] = top[...] + jnp.log2(tot[...])
    out_ref[0] = acc[...].astype(bf16).T


def attend_back_kernel(
    plan, q_ref, g_ref, kv_ref, start_ref, lse_ref, delta_ref, dq_ref, send_ref, keep_ref,
    kvt, v_rows, qt, gt, dqt, dk, dv, bias, *, slots, hs, rows, peers,
):
    queries, keys = q_ref.shape[1], kv_ref.shape[1]
    b = pl.program_id(0)

    @pl.when(b == 0)
    def _():
        for i in range(kv_ref.shape[0]):
            kvt[i] = kv_ref[i].T
            v_rows[i] = kv_ref[i][:, hs:]
        dk[...] = jnp.zeros_like(dk)
        dv[...] = jnp.zeros_like(dv)

    qt[...] = q_ref[0].T
    gt[...] = g_ref[0].T
    dqt[...] = jnp.zeros_like(dqt)
    part = [slice(h * hs, (h + 1) * hs) for h in range(slots)]

    def block(row, chunk, masked):
        at = kv_place(row, chunk, plan[8 * rows], rows, peers)
        k = kv_ref[at][:, :hs]
        v = v_rows[at]
        kt = kvt[at, :hs, :]
        scores = [dot(k, qt[part[h], :]) for h in range(slots)]
        grads = [dot(v, gt[part[h], :]) for h in range(slots)]
        if masked:
            scores = [s + bias[...] for s in scores]
        probs = [jnp.exp2(scores[h] - lse_ref[0, h : h + 1, :]) for h in range(slots)]
        ds = [(probs[h] * (grads[h] - delta_ref[0, h : h + 1, :])).astype(bf16) for h in range(slots)]
        low = [p.astype(bf16) for p in probs]
        for h in range(slots):
            dqt[part[h], :] += dot(kt, ds[h])
        dk[at] += sum(dot(ds[h], qt[part[h], :], NT) for h in range(slots))
        dv[at] += sum(dot(low[h], gt[part[h], :], NT) for h in range(slots))

    over_keys(plan, start_ref, bias, block, keys, queries)
    dq_ref[0] = (dqt[...] * hs**-0.5).astype(bf16).T

    @pl.when(b == pl.num_programs(0) - 1)
    def _():
        core, each = plan[8 * rows + 1], kv_ref.shape[0] // peers
        for i in range(send_ref.shape[0]):
            at = i + each * (i // each)
            for ref, place in ((send_ref, at + each * (1 - core)), (keep_ref, at + each * core)):
                ref[i] = jnp.concatenate([dk[place] * (1.0 / LOG2E), dv[place]], axis=1).astype(bf16)


def forward_kernel(
    moved, gc_ref, routes_ref, x_ref, og_ref, wo_ref, ff_ref, norms_ref,
    gated_ref, mid_ref, out_ref, far_ref, back_ref, sum_ref, n2t, ogt, hid, gbef,
    *, heads, slots, width, blocks,
):
    step = pl.program_id(0)
    tokens, model = x_ref.shape[1], x_ref.shape[2]
    peers = ff_ref.shape[1]

    @pl.when(step < blocks)
    def _():
        pairs = slots // 2
        experts = slot_experts(routes_ref[0], pairs)
        gc = [gc_ref[0][:, j * LANES : (j + 1) * LANES].astype(f32) for j in range(pairs)]
        gated = expand(gc, experts, heads // 2)
        gated_ref[0] = gated
        middle = x_ref[0].astype(f32) + dot(gated, wo_ref[:, : gated.shape[1]], NT)
        mid_ref[0] = middle
        vhat, _ = normed_parts(middle)
        low = (vhat * norms_ref[1:2, :] + norms_ref[3:4, :]).astype(bf16)
        og = og_ref[0]
        n2t[step] = low.T
        ogt[step] = og.T
        out = middle
        back = jnp.zeros_like(out)
        slope = math.sqrt(2.0 / math.pi)
        for c in range(peers):
            up, down = (ff_ref[:, c, :, at : at + width].reshape(model, width) for at in (0, width))
            v = dot(low, up)
            square = v * v
            bent = jnp.tanh(slope * v * (1.0 + 0.044715 * square))
            rise = 0.5 * (1.0 + bent)
            hidden = (v * rise).astype(bf16)
            slant = rise + 0.5 * v * (1.0 - bent * bent) * (slope + 3.0 * slope * 0.044715 * square)
            before = (dot(og, down) * slant).astype(bf16)
            out = out + dot(hidden, down, NT)
            back = back + dot(before, up, NT)
            hid[c, step] = hidden
            gbef[c, step] = before
        out_ref[0] = out.astype(bf16)
        back_ref[0] = back

        @pl.when(step == moved[0])
        def _():
            far_ref[...] = out.astype(bf16)

    @pl.when(step >= blocks)
    def _():
        c = step - blocks
        up = sum(dot(n2t[b], gbef[c, b]) for b in range(blocks))
        down = sum(dot(ogt[b], hid[c, b]) for b in range(blocks))
        shape = (sum_ref.shape[1], sum_ref.shape[2] // 2, sum_ref.shape[3])
        sum_ref[0] = jnp.concatenate([up.reshape(shape), down.reshape(shape)], axis=1).astype(bf16)


def branch_back_kernel(
    core, back_ref, mid_ref, og_ref, gc_ref, gate_ref, routes_ref, wo_ref, norms_ref, gated_ref,
    gm_ref, gatt_ref, delta_ref, glog_ref, sums_ref, send_ref, keep_ref, gbrt,
    *, heads, slots, hs, blocks, per,
):
    step = pl.program_id(0)

    @pl.when(step < blocks)
    def _():
        branch_back_block(
            step, back_ref, mid_ref, og_ref, gc_ref, gate_ref, routes_ref, wo_ref, norms_ref,
            gm_ref, gatt_ref, delta_ref, glog_ref, sums_ref, gbrt, heads, slots, hs,
        )

    @pl.when(step >= blocks)
    def _():
        total = sum(dot(gbrt[b], gated_ref[b]) for b in range(blocks))
        split_core(total, core[0], per, send_ref, keep_ref)

        @pl.when(step == blocks)
        def _():
            held = jnp.sum(wo_ref[:, heads * hs :].astype(f32), axis=0, keepdims=True)
            sums_ref[2:3, :LANES] = held * (1.0 / per)


def branch_back_block(
    step, back_ref, mid_ref, og_ref, gc_ref, gate_ref, routes_ref, wo_ref, norms_ref,
    gm_ref, gatt_ref, delta_ref, glog_ref, sums_ref, gbrt, heads, slots, hs,
):
    tokens, model = mid_ref.shape[1], mid_ref.shape[2]
    head_pairs, pairs = heads // 2, slots // 2
    experts = slot_experts(routes_ref[0], pairs)
    back = back_ref[0]
    vhat, rstd = normed_parts(mid_ref[0])
    gm = og_ref[0].astype(f32) + norm_back(back, vhat, rstd, norms_ref[1:2, :])
    gm_ref[0] = gm

    @pl.when(step == 0)
    def _():
        sums_ref[...] = jnp.zeros_like(sums_ref)

    sums_ref[0:1, :] += jnp.sum(back * vhat, axis=0, keepdims=True)
    sums_ref[1:2, :] += jnp.sum(back, axis=0, keepdims=True)
    gbr = gm.astype(bf16)
    gbrt[step] = gbr.T
    wide = dot(gbr, wo_ref[:, : heads * hs])
    found = compact(lambda i: wide[:, i * LANES : (i + 1) * LANES], experts, head_pairs)
    found = [f.astype(f32) for f in found]
    gate = gate_ref[0]
    shape = (tokens, LANES)
    attended, products = [], []
    for j in range(pairs):
        spread = halves(gate[:, 2 * j : 2 * j + 1], gate[:, 2 * j + 1 : 2 * j + 2], shape)
        attended.append((found[j] * spread).astype(bf16))
        products.append(found[j] * gc_ref[0][:, j * LANES : (j + 1) * LANES].astype(f32))
    gatt_ref[0] = jnp.concatenate(attended, axis=1)
    product = jnp.concatenate(products, axis=1)
    owner = lax.broadcasted_iota(jnp.int32, (slots * hs, LANES), 0) // hs
    ones = (owner == lax.broadcasted_iota(jnp.int32, (slots * hs, LANES), 1)).astype(bf16)
    coarse = product.astype(bf16)
    fine = (product - coarse.astype(f32)).astype(bf16)
    inner = dot(coarse, ones) + dot(fine, ones)
    delta_ref[0] = inner.T[:slots, :]
    logit = inner - gate * jnp.sum(inner, axis=1, keepdims=True)
    lane = lax.broadcasted_iota(jnp.int32, shape, 1)
    spread_out = jnp.zeros(shape, f32)
    routes = routes_ref[0]
    for s in range(slots):
        spread_out = jnp.where(lane == routes[:, s : s + 1], logit[:, s : s + 1], spread_out)
    glog_ref[0] = spread_out.astype(bf16)


def query_weights_kernel(
    core, dq_ref, routes_ref, n_ref, send_ref, keep_ref, wide_ref, acc, *, heads, slots, per
):
    pairs = slots // 2
    experts = slot_experts(routes_ref[0], pairs)
    dq = [dq_ref[0][:, j * LANES : (j + 1) * LANES].astype(f32) for j in range(pairs)]
    wide = expand(dq, experts, heads // 2)
    wide_ref[0] = wide

    @pl.when(pl.program_id(0) == 0)
    def _():
        acc[...] = jnp.zeros_like(acc)

    acc[...] += dot(n_ref[0].T, wide)

    @pl.when(pl.program_id(0) == pl.num_programs(0) - 1)
    def _():
        split_core(acc[...], core[0], per, send_ref, keep_ref)


def input_kernel(
    core, wide_ref, glog_ref, dkv_ref, w_ref, few_ref, x_ref, n_ref, gm_ref, norms_ref, sums_ref,
    ig_ref, far_ref, send_ref, keep_ref, acck, accr, sums, *, heads, per,
):
    dkv, glog = dkv_ref[0], glog_ref[0]
    dn = (
        dot(wide_ref[0], w_ref[...], NT)
        + dot(dkv, few_ref[:, : dkv.shape[1]], NT)
        + dot(glog, few_ref[:, -LANES:], NT)
    )
    vhat, rstd = normed_parts(x_ref[0].astype(f32))
    ig = gm_ref[0] + norm_back(dn, vhat, rstd, norms_ref[0:1, :])
    ig_ref[0] = ig

    @pl.when(pl.program_id(0) == core[1])
    def _():
        far_ref[...] = ig.astype(bf16)

    @pl.when(pl.program_id(0) == 0)
    def _():
        acck[...] = jnp.zeros_like(acck)
        accr[...] = jnp.zeros_like(accr)
        sums[...] = jnp.zeros_like(sums)

    nt = n_ref[0].T
    acck[...] += dot(nt, dkv)
    accr[...] += dot(nt, glog)
    sums[0:1, :] += jnp.sum(dn * vhat, axis=0, keepdims=True)
    sums[1:2, :] += jnp.sum(dn, axis=0, keepdims=True)

    @pl.when(pl.program_id(0) == pl.num_programs(0) - 1)
    def _():
        second = sums_ref[...]
        model = second.shape[1]
        rows = jnp.concatenate(
            [
                jnp.zeros((heads, model), f32),
                sums[0:1, :], second[0:1, :], sums[1:2, :], second[1:2, :],
                jnp.zeros((LANES - heads - 4, model), f32),
            ],
            axis=0,
        )
        small = jnp.concatenate([acck[...], accr[...] + rows.T], axis=1)
        split_core(small, core[0], per, send_ref, keep_ref)


def fixed(shape):
    return pl.BlockSpec(shape, lambda b, *_: (0,) * len(shape))


def per_block(*shape):
    return pl.BlockSpec((1, *shape), lambda b, *_: (b,) + (0,) * len(shape))


def like(shape, kind):
    return jax.ShapeDtypeStruct(shape, kind)


def cost(flops, size, exps=0):
    return pl.CostEstimate(flops=int(flops), bytes_accessed=int(size), transcendentals=int(exps))


def shards(
    tokens, segment_ids, routes, out_grad, w_query, w_keyval, w_output, w_router,
    norm_gains, norm_biases, w_up, w_down,
):
    rows, local, model = tokens.shape
    peers = lax.axis_size("mp")
    slots = routes.shape[2]
    heads = w_router.shape[1]
    hs = w_keyval.shape[1] // 2
    width = w_up.shape[1]
    chunk = local // 2
    blocks = rows * 2
    count = rows * local
    place = lax.axis_index("mp")
    wide = heads * hs
    slim = slots * hs

    def two(v):
        high = lax.reduce_precision(v, 8, 7)
        return [high.astype(bf16), (v - high).astype(bf16)]

    pads = jnp.zeros((w_query.shape[0], LANES - heads - 8), bf16)
    first = jnp.concatenate(
        [w_query, w_keyval, w_router, *two(norm_gains), *two(norm_biases), pads], axis=1
    )
    dp_groups = bit_groups("dp")
    far_groups, near_group = dp_groups[1:], dp_groups[0]
    depth = len(dp_groups)

    def far_stage(a, until=None):
        for i, group in enumerate(reversed(far_groups)):
            a = gather_bits(a, "dp", group, i, until)
        return a

    both = jnp.concatenate([w_up, w_down], axis=1)
    feed = lax.all_gather(both, ("dp", "mp"), axis=0, tiled=False)
    feed = feed.reshape(lax.axis_size("dp"), peers, *both.shape)
    y_bit, core_bit = (1, 1), (0, 1)
    first = far_stage(first)
    chosen = after(routes, first)
    chosen = (chosen[..., None] == jnp.arange(heads, dtype=jnp.int32)).astype(f32)
    held = jnp.sum(chosen, axis=(0, 1, 2))
    held_high = lax.reduce_precision(held, 8, 7)
    held = jnp.concatenate([held_high, held - held_high, jnp.zeros(LANES - 2 * heads, f32)])
    held = jnp.broadcast_to(held.astype(bf16), (w_output.shape[0], LANES))
    first_y = gather_bits(first, "mp", y_bit, depth - 1)
    proj = far_stage(after(jnp.concatenate([w_output, held], axis=1), first), first_y)
    few = gather_bits(first_y[..., wide:], "dp", near_group, depth - 1)
    many = after(first_y[..., :wide], few)
    few = gather_bits(few, "mp", core_bit, depth + 1).reshape(model, 2 * hs + LANES)
    first_x = few
    proj = gather_bits(after(proj, first_y), "mp", y_bit, depth - 1, few)

    single = jnp.argmax(segment_ids[:, -1] == 0).astype(jnp.int32)

    def swapped(a, start=None, until=None):
        kind = a.dtype
        if start is not None:
            a = after(a, start)
        a = a.reshape(rows, 2, chunk, -1)
        piece = lax.dynamic_index_in_dim(a[:, 1], single, 0, keepdims=False)
        piece = flip(piece.astype(bf16), "mp", peers - 1)
        if until is not None:
            piece = after(piece, until)
        return lax.dynamic_update_slice(a, piece.astype(kind)[None, None], (single, 1, 0, 0))

    def blocked(a):
        return a.reshape(blocks, chunk, -1)

    x = blocked(swapped(tokens))
    picks = blocked(swapped(routes, first_y, first_x))
    picks_t = jnp.swapaxes(picks, 1, 2)
    segments = after(segment_ids, first_y)
    near, far = 2 * place, 2 * (peers - 1 - place) + 1
    one = jnp.arange(rows, dtype=jnp.int32) == single
    last = jnp.stack(
        [jnp.full((rows,), near, jnp.int32), jnp.where(one, far, near + 1).astype(jnp.int32)], axis=1
    )
    ids = jnp.arange(8, dtype=jnp.int32)
    sizes = jnp.sum((segments[:, :, None] == ids).astype(jnp.int32), axis=1)
    own = jnp.stack(
        [
            jnp.stack(
                [lax.dynamic_slice(segments, (r, last[r, i] * chunk), (1, chunk))[0] for i in range(2)]
            )
            for r in range(rows)
        ]
    )
    start = jnp.sum(jnp.where(ids < own[..., None], sizes[:, None, None, :], 0), axis=-1)
    full = jnp.minimum((start[:, :, -1] + chunk - 1) // chunk, last)
    which = jnp.broadcast_to(jnp.arange(rows, dtype=jnp.int32)[:, None], (rows, 2))
    plan = jnp.stack([which, last, start[:, :, 0] // chunk, full], axis=-1).astype(jnp.int32)
    plan = jnp.concatenate([plan.reshape(-1), single[None], (place & 1).astype(jnp.int32)[None]])
    start = start.astype(jnp.int32).reshape(blocks, 1, chunk)

    n1, kv, norms = pl.pallas_call(
        functools.partial(norm_kernel, heads=heads),
        grid=(blocks,),
        in_specs=[per_block(chunk, model), fixed(few.shape)],
        out_specs=[per_block(chunk, model), per_block(chunk, 2 * hs), fixed((8, model))],
        out_shape=[
            like((blocks, chunk, model), bf16),
            like((blocks, chunk, 2 * hs), bf16),
            like((8, model), f32),
        ],
        cost_estimate=cost(2 * count * model * LANES, 4 * MIB),
        name="norm_one",
    )(x, few)
    many = gather_bits(many, "dp", near_group, depth - 1, kv)
    weights = gather_bits(many, "mp", core_bit, depth + 1).reshape(model, wide)
    kv_half = gather_bits(kv, "mp", y_bit, 0, weights)
    kv_all = gather_bits(kv_half, "mp", core_bit, 1).reshape(peers * blocks, chunk, 2 * hs)

    q, gate, gate_t = pl.pallas_call(
        functools.partial(query_kernel, heads=heads, slots=slots, hs=hs),
        grid=(blocks,),
        in_specs=[
            per_block(chunk, model), fixed(weights.shape), fixed(few.shape),
            per_block(chunk, slots), per_block(slots, chunk),
        ],
        out_specs=[per_block(chunk, slim), per_block(chunk, LANES), per_block(slots, chunk)],
        out_shape=[
            like((blocks, chunk, slim), bf16),
            like((blocks, chunk, LANES), f32),
            like((blocks, slots, chunk), f32),
        ],
        compiler_params=pltpu.CompilerParams(vmem_limit_bytes=24 * MIB),
        cost_estimate=cost(2 * count * model * wide * 2, 6 * MIB),
        name="queries",
    )(after(n1, kv_half), weights, few, picks, picks_t)

    proj = gather_bits(after(proj, many), "dp", near_group, depth - 1, q)
    attention = dict(slots=slots, hs=hs, rows=rows, peers=peers)
    total = peers * blocks
    gc, lse = pl.pallas_call(
        functools.partial(attend_kernel, **attention),
        grid_spec=pltpu.PrefetchScalarGridSpec(
            num_scalar_prefetch=1,
            grid=(blocks,),
            in_specs=[
                per_block(chunk, slim), fixed(kv_all.shape), per_block(1, chunk), per_block(slots, chunk),
            ],
            out_specs=[per_block(chunk, slim), per_block(slots, chunk)],
            scratch_shapes=[
                pltpu.VMEM((total, 2 * hs, chunk), bf16),
                pltpu.VMEM((slim, chunk), bf16),
                pltpu.VMEM((slim, chunk), f32),
                pltpu.VMEM((slots, chunk), f32),
                pltpu.VMEM((slots, chunk), f32),
                pltpu.VMEM((chunk, chunk), f32),
            ],
        ),
        out_shape=[like((blocks, chunk, slim), bf16), like((blocks, slots, chunk), f32)],
        compiler_params=pltpu.CompilerParams(vmem_limit_bytes=24 * MIB),
        cost_estimate=cost(12e9, 4 * MIB),
        name="attend",
    )(plan, q, kv_all, start, gate_t)

    proj = gather_bits(proj, "mp", core_bit, depth + 1, gc).reshape(model, wide + LANES)
    grads = blocked(swapped(out_grad, q, gc))
    core = (place & 1).astype(jnp.int32)[None]
    moved = 2 * single[None] + 1
    core_moved = jnp.concatenate([core, moved])
    pair = peers // 2
    per = w_query.shape[0]

    def early(*shape):
        return pl.BlockSpec((1, *shape), lambda b, *_: (jnp.minimum(b, blocks - 1),) + (0,) * len(shape))

    def once(shape):
        return pl.BlockSpec(shape, lambda b, *_: (0,) * len(shape), pipeline_mode=pl.Buffered(1))

    feed_shape = (lax.axis_size("dp"), 2 * w_up.shape[0], width)
    gated, mid, outs, outs_far, back, feed_sum = pl.pallas_call(
        functools.partial(forward_kernel, heads=heads, slots=slots, width=width, blocks=blocks),
        grid_spec=pltpu.PrefetchScalarGridSpec(
            num_scalar_prefetch=1,
            grid=(blocks + peers,),
            in_specs=[
                early(chunk, slim), early(chunk, slots), early(chunk, model), early(chunk, model),
                once(proj.shape), once(feed.shape), once(norms.shape),
            ],
            out_specs=[
                early(chunk, wide), early(chunk, model), early(chunk, model), fixed((chunk, model)),
                early(chunk, model),
                pl.BlockSpec((1, *feed_shape), lambda b, *_: (jnp.maximum(b - blocks, 0), 0, 0, 0)),
            ],
            scratch_shapes=[
                pltpu.VMEM((blocks, model, chunk), bf16),
                pltpu.VMEM((blocks, model, chunk), bf16),
                pltpu.VMEM((peers, blocks, chunk, width), bf16),
                pltpu.VMEM((peers, blocks, chunk, width), bf16),
            ],
        ),
        out_shape=[
            like((blocks, chunk, wide), bf16),
            like((blocks, chunk, model), f32),
            like((blocks, chunk, model), bf16),
            like((chunk, model), bf16),
            like((blocks, chunk, model), f32),
            like((peers, *feed_shape), bf16),
        ],
        compiler_params=pltpu.CompilerParams(vmem_limit_bytes=60 * MIB),
        cost_estimate=cost(24e9, 24 * MIB),
        name="forward",
    )(moved, gc, picks, x, grads, proj, feed, norms)

    part, parts = model, wide // model

    def late_columns(b, core):
        return 0, jnp.maximum(b - blocks, 0)

    gm, gatt, delta, glog, sums, out_send, out_keep = pl.pallas_call(
        functools.partial(branch_back_kernel, heads=heads, slots=slots, hs=hs, blocks=blocks, per=per),
        grid_spec=pltpu.PrefetchScalarGridSpec(
            num_scalar_prefetch=1,
            grid=(blocks + parts,),
            in_specs=[
                early(chunk, model), early(chunk, model), early(chunk, model),
                early(chunk, slim), early(chunk, LANES), early(chunk, slots),
                once(proj.shape), once(norms.shape),
                pl.BlockSpec((blocks, chunk, part), lambda b, core: (0, *late_columns(b, core))),
            ],
            out_specs=[
                early(chunk, model), early(chunk, slim),
                early(slots, chunk), early(chunk, LANES), fixed((8, model)),
                pl.BlockSpec((model // 2, part), late_columns),
                pl.BlockSpec((model // 2, part), late_columns),
            ],
            scratch_shapes=[pltpu.VMEM((blocks, model, chunk), bf16)],
        ),
        out_shape=[
            like((blocks, chunk, model), f32),
            like((blocks, chunk, slim), bf16),
            like((blocks, slots, chunk), f32),
            like((blocks, chunk, LANES), bf16),
            like((8, model), f32),
            like((model // 2, wide), bf16),
            like((model // 2, wide), bf16),
        ],
        compiler_params=pltpu.CompilerParams(vmem_limit_bytes=60 * MIB),
        cost_estimate=cost(8e9, 14 * MIB),
        name="branch_back",
    )(core, back, mid, grads, gc, gate, picks, proj, norms, gated)

    def low_bits(a, axis, group, dim, until=None):
        return scatter_bits(a, axis, group, dim, until).astype(bf16)

    def across(send, keep, until):
        got = flip(send, "mp", 1)
        if until is not None:
            got = after(got, until)
        return (keep.astype(f32) + got.astype(f32)).astype(bf16)

    def far_scatter(a, until=None):
        for i, group in enumerate(far_groups):
            a = scatter_bits(a, "dp", group, depth - 2 - i, until)
            if i < len(far_groups) - 1:
                a = a.astype(bf16)
        return a

    def across(send, keep, until):
        got = flip(send, "mp", 1)
        if until is not None:
            got = after(got, until)
        return (keep.astype(f32) + got.astype(f32)).astype(bf16)

    groups = [2**bits for _, bits in reversed(dp_groups)]
    feed_part = lax.psum_scatter(feed_sum, "mp", scatter_dimension=0, tiled=False)
    feed_part = feed_part.reshape(*groups, *feed_shape[1:])
    half_kv = (total // 2, chunk, 2 * hs)
    dq, dkv_send, dkv_keep = pl.pallas_call(
        functools.partial(attend_back_kernel, **attention),
        grid_spec=pltpu.PrefetchScalarGridSpec(
            num_scalar_prefetch=1,
            grid=(blocks,),
            in_specs=[
                per_block(chunk, slim), per_block(chunk, slim), fixed(kv_all.shape), per_block(1, chunk),
                per_block(slots, chunk), per_block(slots, chunk),
            ],
            out_specs=[per_block(chunk, slim), fixed(half_kv), fixed(half_kv)],
            scratch_shapes=[
                pltpu.VMEM((total, 2 * hs, chunk), bf16),
                pltpu.VMEM((total, chunk, hs), bf16),
                pltpu.VMEM((slim, chunk), bf16),
                pltpu.VMEM((slim, chunk), bf16),
                pltpu.VMEM((slim, chunk), f32),
                pltpu.VMEM((total, chunk, hs), f32),
                pltpu.VMEM((total, chunk, hs), f32),
                pltpu.VMEM((chunk, chunk), f32),
            ],
        ),
        out_shape=[like((blocks, chunk, slim), bf16), like(half_kv, bf16), like(half_kv, bf16)],
        compiler_params=pltpu.CompilerParams(vmem_limit_bytes=32 * MIB),
        cost_estimate=cost(25e9, 6 * MIB),
        name="attend_back",
    )(plan, q, gatt, kv_all, start, lse, delta)

    feed_near = scatter_start(feed_part, "dp", near_group, depth - 1)
    dkv = across(dkv_send, dkv_keep, None).reshape(pair, blocks * chunk, 2 * hs)
    dkv_y = scatter_start(dkv, "mp", y_bit, 0)
    dq = after(dq, *feed_near[2], *dkv_y[2])
    wq_send, wq_keep, spread = pl.pallas_call(
        functools.partial(query_weights_kernel, heads=heads, slots=slots, per=per),
        grid_spec=pltpu.PrefetchScalarGridSpec(
            num_scalar_prefetch=1,
            grid=(blocks,),
            in_specs=[per_block(chunk, slim), per_block(chunk, slots), per_block(chunk, model)],
            out_specs=[
                fixed((model // 2, wide)), fixed((model // 2, wide)), per_block(chunk, wide),
            ],
            scratch_shapes=[pltpu.VMEM((model, wide), f32)],
        ),
        out_shape=[
            like((model // 2, wide), bf16),
            like((model // 2, wide), bf16),
            like((blocks, chunk, wide), bf16),
        ],
        compiler_params=pltpu.CompilerParams(vmem_limit_bytes=60 * MIB),
        cost_estimate=cost(4e9, 10 * MIB),
        name="query_weights",
    )(core, dq, picks, n1)
    feed_part = scatter_end(feed_near, wq_send).astype(bf16)
    out_part = across(out_send, out_keep, wq_send).reshape(*groups, 2, per, wide)
    out_near = scatter_start(out_part, "dp", near_group, depth - 1)
    dkv = scatter_end(dkv_y, wq_send).astype(bf16).reshape(blocks, chunk, 2 * hs)
    query_part = across(wq_send, wq_keep, None).reshape(*groups, 2, per, wide)
    query_y = scatter_start(query_part, "mp", y_bit, depth)
    far_low, far_count = near_group[1], bits_of("dp") - near_group[1]
    feed_part = feed_part.reshape(*(2,) * far_count, *feed_shape[1:])
    feed_top = scatter_start(feed_part, "dp", (far_low + far_count - 1, 1), 0)
    spread = after(spread, *feed_top[2], *query_y[2], *out_near[2])

    ig, ig_far, small_send, small_keep = pl.pallas_call(
        functools.partial(input_kernel, heads=heads, per=per),
        grid_spec=pltpu.PrefetchScalarGridSpec(
            num_scalar_prefetch=1,
            grid=(blocks,),
            in_specs=[
                per_block(chunk, wide), per_block(chunk, LANES), per_block(chunk, 2 * hs),
                fixed(weights.shape), fixed(few.shape), per_block(chunk, model), per_block(chunk, model),
                per_block(chunk, model), fixed((8, model)), fixed((8, model)),
            ],
            out_specs=[
                per_block(chunk, model), fixed((chunk, model)),
                fixed((model // 2, 2 * LANES)), fixed((model // 2, 2 * LANES)),
            ],
            scratch_shapes=[
                pltpu.VMEM((model, 2 * hs), f32), pltpu.VMEM((model, LANES), f32), pltpu.VMEM((8, model), f32),
            ],
        ),
        out_shape=[
            like((blocks, chunk, model), f32),
            like((chunk, model), bf16),
            like((model // 2, 2 * LANES), bf16),
            like((model // 2, 2 * LANES), bf16),
        ],
        compiler_params=pltpu.CompilerParams(vmem_limit_bytes=60 * MIB),
        cost_estimate=cost(4e9, 12 * MIB),
        name="inputs_back",
    )(core_moved, spread, glog, dkv, weights, few, x, n1, gm, norms, sums)

    query_part = scatter_end(query_y, ig).astype(bf16)
    query_x = scatter_start(query_part, "dp", near_group, depth - 1)
    small = across(small_send, small_keep, None).reshape(*groups, 2, per, 2 * LANES)
    out_part = scatter_end(out_near, ig).astype(bf16)
    out_y = scatter_start(out_part, "mp", y_bit, depth - 1)
    query_part = scatter_end(query_x)
    small_y = scatter_start(after(small, query_part), "mp", y_bit, depth)
    feed_grad = scatter_end(feed_top, small_y[2][0])
    for bit in reversed(range(far_low, far_low + far_count - 1)):
        feed_grad = scatter_bits(feed_grad.astype(bf16), "dp", (bit, 1), 0)
    small = scatter_end(small_y).astype(bf16)
    small = low_bits(small, "dp", near_group, depth - 1)
    joint = [query_part, scatter_end(out_y), small.astype(f32)]
    joint = far_scatter(jnp.concatenate(joint, axis=-1).astype(bf16))
    up_rows = w_up.shape[0]
    smalls = joint[:, 2 * wide :]
    def returned(a, piece):
        piece = flip(piece, "mp", peers - 1).astype(a.dtype)
        a = a.reshape(rows, 2, chunk, model)
        a = lax.dynamic_update_slice(a, piece[None, None], (single, 1, 0, 0))
        return a.reshape(rows, local, model)

    outs_far, ig_far = (after(a, small_y[2][0]) for a in (outs_far, ig_far))
    outputs, input_grad = returned(outs, outs_far), returned(ig, ig_far)
    counts = sums[2, :heads] + sums[2, heads : 2 * heads]
    return (
        outputs,
        input_grad,
        counts,
        joint[:, :wide],
        smalls[:, : 2 * hs],
        joint[:, wide : 2 * wide],
        smalls[:, LANES : LANES + heads],
        smalls[:, LANES + heads : LANES + heads + 2],
        smalls[:, LANES + heads + 2 : LANES + heads + 4],
        feed_grad[:up_rows],
        feed_grad[up_rows:],
    )


def solution(mesh):
    in_specs = (
        P("dp", "mp", None),
        P("dp", None),
        P("dp", "mp", None),
        P("dp", "mp", None),
        P(("dp", "mp"), None),
        P(("dp", "mp"), None),
        P(("dp", "mp"), None),
        P(("dp", "mp"), None),
        P(("dp", "mp"), None),
        P(("dp", "mp"), None),
        P("dp", "mp"),
        P("dp", "mp"),
    )
    out_specs = (
        P("dp", "mp", None),
        P("dp", "mp", None),
        P(),
        P(("dp", "mp"), None),
        P(("dp", "mp"), None),
        P(("dp", "mp"), None),
        P(("dp", "mp"), None),
        P(("dp", "mp"), None),
        P(("dp", "mp"), None),
        P("dp", "mp"),
        P("dp", "mp"),
    )
    return jax.shard_map(shards, mesh=mesh, in_specs=in_specs, out_specs=out_specs, check_vma=False)
```

```python
import functools
import math
import jax
import jax.numpy as jnp
from jax import lax
from jax.experimental import pallas as pl
from jax.experimental.pallas import tpu as pltpu
from jax.sharding import PartitionSpec as P

epsilon = 1e-05
f32, bf16 = jnp.float32, jnp.bfloat16
NN = (((1,), (0,)), ((), ()))
NT = (((1,), (1,)), ((), ()))
LANES = 128
LOG2E = math.log2(math.e)
MIB = 2**20


def dot(left, right, dims=NN):
    return lax.dot_general(left, right, dims, preferred_element_type=f32)


def bits_of(axis):
    return (lax.axis_size(axis) - 1).bit_length()


def bit_groups(axis):
    count = bits_of(axis)
    groups, at = [], 0
    if count % 2:
        groups.append((0, 1))
        at = 1
    while at < count:
        groups.append((at, 2))
        at += 2
    return groups


def flip(x, axis, mask):
    return lax.ppermute(x, axis, [(i, i ^ mask) for i in range(lax.axis_size(axis))])


def after(x, *others):
    return lax.optimization_barrier((x, *others))[0]


def gather_bits(x, axis, group, dim, until=None):
    low, width = group
    mine = lax.axis_index(axis) >> low
    got = [flip(x, axis, k << low) for k in range(1, 2**width)]
    if until is not None:
        got = lax.optimization_barrier((*got, until))[:-1]
    shape = [1] * (x.ndim + 1)
    shape[dim] = 2**width
    way = lax.iota(jnp.int32, 2**width).reshape(shape) ^ (mine & (2**width - 1))
    pieces = [jnp.expand_dims(p, dim) for p in (x, *got)]
    for b in range(width):
        odd = (way >> b) & 1 == 1
        pieces = [jnp.where(odd, pieces[k + 1], pieces[k]) for k in range(0, len(pieces), 2)]
    return pieces[0]


def scatter_start(x, axis, group, dim):
    low, width = group
    mine = (lax.axis_index(axis) >> low) & (2**width - 1)
    sent = [
        lax.dynamic_index_in_dim(x, mine ^ k, dim, keepdims=False) for k in range(1, 2**width)
    ]
    got = [flip(a, axis, k << low) for k, a in enumerate(sent, 1)]
    return lax.dynamic_index_in_dim(x, mine, dim, keepdims=False), got, sent


def scatter_end(started, until=None):
    total, got, _ = started
    if until is not None:
        got = lax.optimization_barrier((*got, until))[:-1]
    total = total.astype(f32)
    for g in got:
        total = total + g.astype(f32)
    return total


def scatter_bits(x, axis, group, dim, until=None):
    return scatter_end(scatter_start(x, axis, group, dim), until)


def halves(row_first, row_second, like):
    lane = lax.broadcasted_iota(jnp.int32, like, 1)
    return jnp.where(lane < LANES // 2, row_first, row_second)


def slot_lanes(rows, columns, hs):
    shape = (rows, columns)
    slot, column = (lax.broadcasted_iota(jnp.int32, shape, i) for i in range(2))
    return (slot == column // hs).astype(bf16)


def slot_experts(routes, pairs):
    slots = routes.shape[1]
    spread = dot(routes.astype(bf16), slot_lanes(slots, pairs * LANES, LANES // 2)).astype(jnp.int32)
    return [spread[:, j * LANES : (j + 1) * LANES] for j in range(pairs)]


def turn_half(x):
    return pltpu.roll(x, LANES // 2, 1)


def compact(wide, experts, head_pairs):
    lane = lax.broadcasted_iota(jnp.int32, experts[0].shape, 1)
    high = (lane >= LANES // 2).astype(jnp.int32)
    straight = [(e - high).astype(jnp.int16) for e in experts]
    crossed = [(e + high).astype(jnp.int16) for e in experts]
    found = [jnp.zeros(experts[0].shape, bf16) for _ in experts]
    for i in range(head_pairs):
        block = wide(i)
        turned = turn_half(block).astype(bf16)
        block = block.astype(bf16)
        for j in range(len(experts)):
            found[j] = jnp.where(straight[j] == jnp.int16(2 * i), block, found[j])
            found[j] = jnp.where(crossed[j] == jnp.int16(2 * i + 1), turned, found[j])
    return found


def expand(narrow, experts, head_pairs):
    lane = lax.broadcasted_iota(jnp.int32, experts[0].shape, 1)
    high = (lane >= LANES // 2).astype(jnp.int32)
    sources = []
    for block, e in zip(narrow, experts):
        sources.append(((e - high).astype(jnp.int16), block.astype(bf16)))
        sources.append(((turn_half(e) - high).astype(jnp.int16), turn_half(block).astype(bf16)))
    wide = []
    for i in range(head_pairs):
        out = jnp.zeros(experts[0].shape, bf16)
        for e, block in sources:
            out = jnp.where(e == jnp.int16(2 * i), block, out)
        wide.append(out)
    return jnp.concatenate(wide, axis=1)


def split_core(value, core, per, send_ref, keep_ref):
    rows, columns = value.shape
    if per % 16 == 0:
        parts = value.reshape(rows // (2 * per), 2, per, columns)
        first, second = parts[:, 0], parts[:, 1]
        send = jnp.where(core == 0, second, first).reshape(rows // 2, columns)
        keep = jnp.where(core == 0, first, second).reshape(rows // 2, columns)
        send_ref[...], keep_ref[...] = send.astype(bf16), keep.astype(bf16)
        return
    shape = (rows // 2, rows)
    target, source = (lax.broadcasted_iota(jnp.int32, shape, i) for i in range(2))
    start = target // per * (2 * per) + target % per
    for ref, side in ((send_ref, 1 - core), (keep_ref, core)):
        chosen = (source == start + side * per).astype(bf16)
        ref[...] = dot(chosen, value.astype(bf16)).astype(bf16)


def normed_parts(values):
    mean = jnp.mean(values, axis=1, keepdims=True)
    centred = values - mean
    rstd = lax.rsqrt(jnp.mean(centred * centred, axis=1, keepdims=True) + epsilon)
    return centred * rstd, rstd


def norm_back(grad, normed, rstd, gain):
    scaled = grad * gain
    return rstd * (
        scaled
        - jnp.mean(scaled, axis=1, keepdims=True)
        - normed * jnp.mean(scaled * normed, axis=1, keepdims=True)
    )


def norm_kernel(x_ref, w_ref, n_ref, kv_ref, norms_ref, *, heads):
    misc = w_ref[:, -LANES:].astype(f32).T
    norms = misc[heads : heads + 8, :]
    norms = jnp.concatenate(
        [norms[0:2] + norms[2:4], norms[4:6] + norms[6:8], jnp.zeros_like(norms[0:4])], axis=0
    )
    norms_ref[...] = norms
    normed, _ = normed_parts(x_ref[0].astype(f32))
    low = (normed * norms[0:1] + norms[2:3]).astype(bf16)
    n_ref[0] = low
    kv_ref[0] = dot(low, w_ref[:, : kv_ref.shape[2]]).astype(bf16)


def query_kernel(
    n_ref, w_ref, few_ref, routes_ref, routes_t_ref, q_ref, gate_ref, gate_t_ref, *, heads, slots, hs
):
    low = n_ref[0]
    head_pairs = heads // 2
    queries = dot(low, w_ref[...]) * (hs**-0.5 * LOG2E)
    experts = slot_experts(routes_ref[0], slots // 2)
    found = compact(lambda i: queries[:, i * LANES : (i + 1) * LANES], experts, head_pairs)
    q_ref[0] = jnp.concatenate(found, axis=1)
    logits = dot(low, few_ref[:, -LANES:]).T[:heads, :]
    expert = lax.broadcasted_iota(jnp.int32, logits.shape, 0)
    routes_t = routes_t_ref[0]
    picked = [
        jnp.sum(jnp.where(expert == routes_t[s : s + 1, :], logits, 0.0), axis=0, keepdims=True)
        for s in range(slots)
    ]
    chosen = jnp.concatenate(picked, axis=0)
    lifted = jnp.exp(chosen - jnp.max(chosen, axis=0, keepdims=True))
    gate = lifted / jnp.sum(lifted, axis=0, keepdims=True)
    gate_t_ref[0] = gate
    padded = jnp.concatenate([gate, jnp.zeros((LANES - slots, gate.shape[1]), f32)], axis=0)
    gate_ref[0] = padded.T


def key_bias(first_key, first_query, start, keys, queries):
    key = first_key + lax.broadcasted_iota(jnp.int32, (keys, queries), 0)
    query = first_query + lax.broadcasted_iota(jnp.int32, (keys, queries), 1)
    return jnp.where((key <= query) & (key >= start), 0.0, -1e30)


def kv_place(row, chunk, single, rows, peers):
    half, owner = chunk % 2, chunk // 2
    owner = jnp.where((half == 1) & (row == single), peers - 1 - owner, owner)
    return owner * (2 * rows) + row * 2 + half


def over_keys(plan, start_ref, bias, block, keys, queries):
    b = pl.program_id(0)
    row, last, first, full = plan[4 * b], plan[4 * b + 1], plan[4 * b + 2], plan[4 * b + 3]

    def masked(i, carry):
        chunk = jnp.where(i == 0, last, first + i - 1)
        bias[...] = key_bias(chunk * keys, last * keys, start_ref[0], keys, queries)
        block(row, chunk, True)
        return carry

    def plain(chunk, carry):
        block(row, chunk, False)
        return carry

    lax.fori_loop(0, 1 + full - first, masked, 0)
    lax.fori_loop(full, last, plain, 0)


def attend_kernel(
    plan, q_ref, kv_ref, start_ref, gate_ref, out_ref, lse_ref, kvt, qt, acc, top, tot, bias, *, slots, hs, rows, peers
):
    queries, keys = q_ref.shape[1], kv_ref.shape[1]

    @pl.when(pl.program_id(0) == 0)
    def _():
        for i in range(kv_ref.shape[0]):
            kvt[i] = kv_ref[i].T

    qt[...] = q_ref[0].T
    acc[...] = jnp.zeros_like(acc)
    top[...] = jnp.full_like(top, -1e30)
    tot[...] = jnp.zeros_like(tot)
    part = [slice(h * hs, (h + 1) * hs) for h in range(slots)]

    def block(row, chunk, masked):
        at = kv_place(row, chunk, plan[8 * rows], rows, peers)
        k = kv_ref[at][:, :hs]
        vt = kvt[at, hs : 2 * hs, :]
        tops, tots = top[...], tot[...]
        scores = [dot(k, qt[part[h], :]) for h in range(slots)]
        if masked:
            scores = [s + bias[...] for s in scores]
        highest = [
            jnp.maximum(tops[h : h + 1], jnp.max(scores[h], axis=0, keepdims=True)) for h in range(slots)
        ]
        probs = [jnp.exp2(scores[h] - highest[h]) for h in range(slots)]
        shrink = [jnp.exp2(tops[h : h + 1] - highest[h]) for h in range(slots)]
        totals = [
            tots[h : h + 1] * shrink[h] + jnp.sum(probs[h], axis=0, keepdims=True) for h in range(slots)
        ]
        for h in range(slots):
            acc[part[h], :] = acc[part[h], :] * shrink[h] + dot(vt, probs[h].astype(bf16))
        top[...] = jnp.concatenate(highest, axis=0)
        tot[...] = jnp.concatenate(totals, axis=0)

    over_keys(plan, start_ref, bias, block, keys, queries)
    for h in range(slots):
        acc[part[h], :] = acc[part[h], :] * (gate_ref[0, h : h + 1, :] / tot[h : h + 1, :])
    lse_ref[0] = top[...] + jnp.log2(tot[...])
    out_ref[0] = acc[...].astype(bf16).T


def attend_back_kernel(
    plan, q_ref, g_ref, kv_ref, start_ref, lse_ref, delta_ref, dq_ref, send_ref, keep_ref,
    kvt, v_rows, qt, gt, dqt, dk, dv, bias, *, slots, hs, rows, peers,
):
    queries, keys = q_ref.shape[1], kv_ref.shape[1]
    b = pl.program_id(0)

    @pl.when(b == 0)
    def _():
        for i in range(kv_ref.shape[0]):
            kvt[i] = kv_ref[i].T
            v_rows[i] = kv_ref[i][:, hs:]
        dk[...] = jnp.zeros_like(dk)
        dv[...] = jnp.zeros_like(dv)

    qt[...] = q_ref[0].T
    gt[...] = g_ref[0].T
    dqt[...] = jnp.zeros_like(dqt)
    part = [slice(h * hs, (h + 1) * hs) for h in range(slots)]

    def block(row, chunk, masked):
        at = kv_place(row, chunk, plan[8 * rows], rows, peers)
        k = kv_ref[at][:, :hs]
        v = v_rows[at]
        kt = kvt[at, :hs, :]
        scores = [dot(k, qt[part[h], :]) for h in range(slots)]
        grads = [dot(v, gt[part[h], :]) for h in range(slots)]
        if masked:
            scores = [s + bias[...] for s in scores]
        probs = [jnp.exp2(scores[h] - lse_ref[0, h : h + 1, :]) for h in range(slots)]
        ds = [(probs[h] * (grads[h] - delta_ref[0, h : h + 1, :])).astype(bf16) for h in range(slots)]
        low = [p.astype(bf16) for p in probs]
        for h in range(slots):
            dqt[part[h], :] += dot(kt, ds[h])
        dk[at] += sum(dot(ds[h], qt[part[h], :], NT) for h in range(slots))
        dv[at] += sum(dot(low[h], gt[part[h], :], NT) for h in range(slots))

    over_keys(plan, start_ref, bias, block, keys, queries)
    dq_ref[0] = (dqt[...] * hs**-0.5).astype(bf16).T

    @pl.when(b == pl.num_programs(0) - 1)
    def _():
        core, each = plan[8 * rows + 1], kv_ref.shape[0] // peers
        for i in range(send_ref.shape[0]):
            at = i + each * (i // each)
            for ref, place in ((send_ref, at + each * (1 - core)), (keep_ref, at + each * core)):
                ref[i] = jnp.concatenate([dk[place] * (1.0 / LOG2E), dv[place]], axis=1).astype(bf16)


def forward_kernel(
    moved, gc_ref, routes_ref, x_ref, og_ref, wo_ref, ff_ref, norms_ref,
    gated_ref, mid_ref, out_ref, far_ref, back_ref, sum_ref, n2t, ogt, hid, gbef,
    *, heads, slots, width, blocks,
):
    step = pl.program_id(0)
    tokens, model = x_ref.shape[1], x_ref.shape[2]
    peers = ff_ref.shape[1]

    @pl.when(step < blocks)
    def _():
        pairs = slots // 2
        experts = slot_experts(routes_ref[0], pairs)
        gc = [gc_ref[0][:, j * LANES : (j + 1) * LANES].astype(f32) for j in range(pairs)]
        gated = expand(gc, experts, heads // 2)
        gated_ref[0] = gated
        middle = x_ref[0].astype(f32) + dot(gated, wo_ref[:, : gated.shape[1]], NT)
        mid_ref[0] = middle
        vhat, _ = normed_parts(middle)
        low = (vhat * norms_ref[1:2, :] + norms_ref[3:4, :]).astype(bf16)
        og = og_ref[0]
        n2t[step] = low.T
        ogt[step] = og.T
        out = middle
        back = jnp.zeros_like(out)
        slope = math.sqrt(2.0 / math.pi)
        for c in range(peers):
            up, down = (ff_ref[:, c, :, at : at + width].reshape(model, width) for at in (0, width))
            v = dot(low, up)
            square = v * v
            bent = jnp.tanh(slope * v * (1.0 + 0.044715 * square))
            rise = 0.5 * (1.0 + bent)
            hidden = (v * rise).astype(bf16)
            slant = rise + 0.5 * v * (1.0 - bent * bent) * (slope + 3.0 * slope * 0.044715 * square)
            before = (dot(og, down) * slant).astype(bf16)
            out = out + dot(hidden, down, NT)
            back = back + dot(before, up, NT)
            hid[c, step] = hidden
            gbef[c, step] = before
        out_ref[0] = out.astype(bf16)
        back_ref[0] = back

        @pl.when(step == moved[0])
        def _():
            far_ref[...] = out.astype(bf16)

    @pl.when(step >= blocks)
    def _():
        c = step - blocks
        up = sum(dot(n2t[b], gbef[c, b]) for b in range(blocks))
        down = sum(dot(ogt[b], hid[c, b]) for b in range(blocks))
        shape = (sum_ref.shape[1], sum_ref.shape[2] // 2, sum_ref.shape[3])
        sum_ref[0] = jnp.concatenate([up.reshape(shape), down.reshape(shape)], axis=1).astype(bf16)


def branch_back_kernel(
    core, back_ref, mid_ref, og_ref, gc_ref, gate_ref, routes_ref, wo_ref, norms_ref, gated_ref,
    gm_ref, gatt_ref, delta_ref, glog_ref, sums_ref, send_ref, keep_ref, gbrt,
    *, heads, slots, hs, blocks, per,
):
    step = pl.program_id(0)

    @pl.when(step < blocks)
    def _():
        branch_back_block(
            step, back_ref, mid_ref, og_ref, gc_ref, gate_ref, routes_ref, wo_ref, norms_ref,
            gm_ref, gatt_ref, delta_ref, glog_ref, sums_ref, gbrt, heads, slots, hs,
        )

    @pl.when(step >= blocks)
    def _():
        total = sum(dot(gbrt[b], gated_ref[b]) for b in range(blocks))
        split_core(total, core[0], per, send_ref, keep_ref)

        @pl.when(step == blocks)
        def _():
            held = jnp.sum(wo_ref[:, heads * hs :].astype(f32), axis=0, keepdims=True)
            sums_ref[2:3, :LANES] = held * (1.0 / per)


def branch_back_block(
    step, back_ref, mid_ref, og_ref, gc_ref, gate_ref, routes_ref, wo_ref, norms_ref,
    gm_ref, gatt_ref, delta_ref, glog_ref, sums_ref, gbrt, heads, slots, hs,
):
    tokens, model = mid_ref.shape[1], mid_ref.shape[2]
    head_pairs, pairs = heads // 2, slots // 2
    experts = slot_experts(routes_ref[0], pairs)
    back = back_ref[0]
    vhat, rstd = normed_parts(mid_ref[0])
    gm = og_ref[0].astype(f32) + norm_back(back, vhat, rstd, norms_ref[1:2, :])
    gm_ref[0] = gm

    @pl.when(step == 0)
    def _():
        sums_ref[...] = jnp.zeros_like(sums_ref)

    sums_ref[0:1, :] += jnp.sum(back * vhat, axis=0, keepdims=True)
    sums_ref[1:2, :] += jnp.sum(back, axis=0, keepdims=True)
    gbr = gm.astype(bf16)
    gbrt[step] = gbr.T
    wide = dot(gbr, wo_ref[:, : heads * hs])
    found = compact(lambda i: wide[:, i * LANES : (i + 1) * LANES], experts, head_pairs)
    found = [f.astype(f32) for f in found]
    gate = gate_ref[0]
    lanes = slot_lanes(LANES, slots * hs, hs)
    coarse = gate.astype(bf16)
    wide_gate = dot(coarse, lanes) + dot((gate - coarse.astype(f32)).astype(bf16), lanes)
    attended, products = [], []
    for j in range(pairs):
        spread = wide_gate[:, j * LANES : (j + 1) * LANES]
        attended.append((found[j] * spread).astype(bf16))
        products.append(found[j] * gc_ref[0][:, j * LANES : (j + 1) * LANES].astype(f32))
    gatt_ref[0] = jnp.concatenate(attended, axis=1)
    product = jnp.concatenate(products, axis=1)
    owner = lax.broadcasted_iota(jnp.int32, (slots * hs, LANES), 0) // hs
    ones = (owner == lax.broadcasted_iota(jnp.int32, (slots * hs, LANES), 1)).astype(bf16)
    coarse = product.astype(bf16)
    fine = (product - coarse.astype(f32)).astype(bf16)
    inner = dot(coarse, ones) + dot(fine, ones)
    delta_ref[0] = inner.T[:slots, :]
    logit = inner - gate * jnp.sum(inner, axis=1, keepdims=True)
    spread_out = dot(logit.astype(bf16), lanes)
    lane = lax.broadcasted_iota(jnp.int32, spread_out.shape, 1) % hs
    spread_out = jnp.where(lane == jnp.concatenate(experts, axis=1), spread_out, 0.0).astype(bf16)
    column, row = (lax.broadcasted_iota(jnp.int32, (slots * hs, LANES), i) for i in (1, 0))
    glog_ref[0] = dot(spread_out, (row % hs == column).astype(bf16)).astype(bf16)


def query_weights_kernel(
    core, dq_ref, routes_ref, n_ref, send_ref, keep_ref, wide_ref, acc, *, heads, slots, per
):
    pairs = slots // 2
    experts = slot_experts(routes_ref[0], pairs)
    dq = [dq_ref[0][:, j * LANES : (j + 1) * LANES].astype(f32) for j in range(pairs)]
    wide = expand(dq, experts, heads // 2)
    wide_ref[0] = wide

    @pl.when(pl.program_id(0) == 0)
    def _():
        acc[...] = jnp.zeros_like(acc)

    acc[...] += dot(n_ref[0].T, wide)

    @pl.when(pl.program_id(0) == pl.num_programs(0) - 1)
    def _():
        split_core(acc[...], core[0], per, send_ref, keep_ref)


def input_kernel(
    core, wide_ref, glog_ref, dkv_ref, w_ref, few_ref, x_ref, n_ref, gm_ref, norms_ref, sums_ref,
    ig_ref, far_ref, send_ref, keep_ref, acck, accr, sums, *, heads, per,
):
    dkv, glog = dkv_ref[0], glog_ref[0]
    dn = (
        dot(wide_ref[0], w_ref[...], NT)
        + dot(dkv, few_ref[:, : dkv.shape[1]], NT)
        + dot(glog, few_ref[:, -LANES:], NT)
    )
    vhat, rstd = normed_parts(x_ref[0].astype(f32))
    ig = gm_ref[0] + norm_back(dn, vhat, rstd, norms_ref[0:1, :])
    ig_ref[0] = ig

    @pl.when(pl.program_id(0) == core[1])
    def _():
        far_ref[...] = ig.astype(bf16)

    @pl.when(pl.program_id(0) == 0)
    def _():
        acck[...] = jnp.zeros_like(acck)
        accr[...] = jnp.zeros_like(accr)
        sums[...] = jnp.zeros_like(sums)

    nt = n_ref[0].T
    acck[...] += dot(nt, dkv)
    accr[...] += dot(nt, glog)
    sums[0:1, :] += jnp.sum(dn * vhat, axis=0, keepdims=True)
    sums[1:2, :] += jnp.sum(dn, axis=0, keepdims=True)

    @pl.when(pl.program_id(0) == pl.num_programs(0) - 1)
    def _():
        second = sums_ref[...]
        model = second.shape[1]
        rows = jnp.concatenate(
            [
                jnp.zeros((heads, model), f32),
                sums[0:1, :], second[0:1, :], sums[1:2, :], second[1:2, :],
                jnp.zeros((LANES - heads - 4, model), f32),
            ],
            axis=0,
        )
        small = jnp.concatenate([acck[...], accr[...] + rows.T], axis=1)
        split_core(small, core[0], per, send_ref, keep_ref)


def fixed(shape):
    return pl.BlockSpec(shape, lambda b, *_: (0,) * len(shape))


def per_block(*shape):
    return pl.BlockSpec((1, *shape), lambda b, *_: (b,) + (0,) * len(shape))


def like(shape, kind):
    return jax.ShapeDtypeStruct(shape, kind)


def cost(flops, size, exps=0):
    return pl.CostEstimate(flops=int(flops), bytes_accessed=int(size), transcendentals=int(exps))


def shards(
    tokens, segment_ids, routes, out_grad, w_query, w_keyval, w_output, w_router,
    norm_gains, norm_biases, w_up, w_down,
):
    rows, local, model = tokens.shape
    peers = lax.axis_size("mp")
    slots = routes.shape[2]
    heads = w_router.shape[1]
    hs = w_keyval.shape[1] // 2
    width = w_up.shape[1]
    chunk = local // 2
    blocks = rows * 2
    count = rows * local
    place = lax.axis_index("mp")
    wide = heads * hs
    slim = slots * hs

    def two(v):
        high = lax.reduce_precision(v, 8, 7)
        return [high.astype(bf16), (v - high).astype(bf16)]

    pads = jnp.zeros((w_query.shape[0], LANES - heads - 8), bf16)
    first = jnp.concatenate(
        [w_query, w_keyval, w_router, *two(norm_gains), *two(norm_biases), pads], axis=1
    )
    dp_groups = bit_groups("dp")
    far_groups, near_group = dp_groups[1:], dp_groups[0]
    depth = len(dp_groups)

    def far_stage(a, until=None):
        for i, group in enumerate(reversed(far_groups)):
            a = gather_bits(a, "dp", group, i, until)
        return a

    both = jnp.concatenate([w_up, w_down], axis=1)
    feed = lax.all_gather(both, ("dp", "mp"), axis=0, tiled=False)
    feed = feed.reshape(lax.axis_size("dp"), peers, *both.shape)
    y_bit, core_bit = (1, 1), (0, 1)
    first = far_stage(first)
    chosen = after(routes, first)
    chosen = (chosen[..., None] == jnp.arange(heads, dtype=jnp.int32)).astype(f32)
    held = jnp.sum(chosen, axis=(0, 1, 2))
    held_high = lax.reduce_precision(held, 8, 7)
    held = jnp.concatenate([held_high, held - held_high, jnp.zeros(LANES - 2 * heads, f32)])
    held = jnp.broadcast_to(held.astype(bf16), (w_output.shape[0], LANES))
    first_y = gather_bits(first, "mp", y_bit, depth - 1)
    proj = far_stage(after(jnp.concatenate([w_output, held], axis=1), first), first_y)
    few = gather_bits(first_y[..., wide:], "dp", near_group, depth - 1)
    many = after(first_y[..., :wide], few)
    few = gather_bits(few, "mp", core_bit, depth + 1).reshape(model, 2 * hs + LANES)
    first_x = few
    proj = gather_bits(after(proj, first_y), "mp", y_bit, depth - 1, few)

    single = jnp.argmax(segment_ids[:, -1] == 0).astype(jnp.int32)

    def swapped(a, start=None, until=None):
        kind = a.dtype
        if start is not None:
            a = after(a, start)
        a = a.reshape(rows, 2, chunk, -1)
        piece = lax.dynamic_index_in_dim(a[:, 1], single, 0, keepdims=False)
        piece = flip(piece.astype(bf16), "mp", peers - 1)
        if until is not None:
            piece = after(piece, until)
        return lax.dynamic_update_slice(a, piece.astype(kind)[None, None], (single, 1, 0, 0))

    def blocked(a):
        return a.reshape(blocks, chunk, -1)

    x = blocked(swapped(tokens))
    picks = blocked(swapped(routes, first_y, first_x))
    picks_t = jnp.swapaxes(picks, 1, 2)
    segments = after(segment_ids, first_y)
    near, far = 2 * place, 2 * (peers - 1 - place) + 1
    one = jnp.arange(rows, dtype=jnp.int32) == single
    last = jnp.stack(
        [jnp.full((rows,), near, jnp.int32), jnp.where(one, far, near + 1).astype(jnp.int32)], axis=1
    )
    ids = jnp.arange(8, dtype=jnp.int32)
    sizes = jnp.sum((segments[:, :, None] == ids).astype(jnp.int32), axis=1)
    own = jnp.stack(
        [
            jnp.stack(
                [lax.dynamic_slice(segments, (r, last[r, i] * chunk), (1, chunk))[0] for i in range(2)]
            )
            for r in range(rows)
        ]
    )
    start = jnp.sum(jnp.where(ids < own[..., None], sizes[:, None, None, :], 0), axis=-1)
    full = jnp.minimum((start[:, :, -1] + chunk - 1) // chunk, last)
    which = jnp.broadcast_to(jnp.arange(rows, dtype=jnp.int32)[:, None], (rows, 2))
    plan = jnp.stack([which, last, start[:, :, 0] // chunk, full], axis=-1).astype(jnp.int32)
    plan = jnp.concatenate([plan.reshape(-1), single[None], (place & 1).astype(jnp.int32)[None]])
    start = start.astype(jnp.int32).reshape(blocks, 1, chunk)

    n1, kv, norms = pl.pallas_call(
        functools.partial(norm_kernel, heads=heads),
        grid=(blocks,),
        in_specs=[per_block(chunk, model), fixed(few.shape)],
        out_specs=[per_block(chunk, model), per_block(chunk, 2 * hs), fixed((8, model))],
        out_shape=[
            like((blocks, chunk, model), bf16),
            like((blocks, chunk, 2 * hs), bf16),
            like((8, model), f32),
        ],
        cost_estimate=cost(2 * count * model * LANES, 4 * MIB),
        name="norm_one",
    )(x, few)
    many = gather_bits(many, "dp", near_group, depth - 1, kv)
    weights = gather_bits(many, "mp", core_bit, depth + 1).reshape(model, wide)
    kv_half = gather_bits(kv, "mp", y_bit, 0, weights)
    kv_all = gather_bits(kv_half, "mp", core_bit, 1).reshape(peers * blocks, chunk, 2 * hs)

    q, gate, gate_t = pl.pallas_call(
        functools.partial(query_kernel, heads=heads, slots=slots, hs=hs),
        grid=(blocks,),
        in_specs=[
            per_block(chunk, model), fixed(weights.shape), fixed(few.shape),
            per_block(chunk, slots), per_block(slots, chunk),
        ],
        out_specs=[per_block(chunk, slim), per_block(chunk, LANES), per_block(slots, chunk)],
        out_shape=[
            like((blocks, chunk, slim), bf16),
            like((blocks, chunk, LANES), f32),
            like((blocks, slots, chunk), f32),
        ],
        compiler_params=pltpu.CompilerParams(vmem_limit_bytes=24 * MIB),
        cost_estimate=cost(2 * count * model * wide * 2, 6 * MIB),
        name="queries",
    )(after(n1, kv_half), weights, few, picks, picks_t)

    proj = gather_bits(after(proj, many), "dp", near_group, depth - 1, q)
    attention = dict(slots=slots, hs=hs, rows=rows, peers=peers)
    total = peers * blocks
    gc, lse = pl.pallas_call(
        functools.partial(attend_kernel, **attention),
        grid_spec=pltpu.PrefetchScalarGridSpec(
            num_scalar_prefetch=1,
            grid=(blocks,),
            in_specs=[
                per_block(chunk, slim), fixed(kv_all.shape), per_block(1, chunk), per_block(slots, chunk),
            ],
            out_specs=[per_block(chunk, slim), per_block(slots, chunk)],
            scratch_shapes=[
                pltpu.VMEM((total, 2 * hs, chunk), bf16),
                pltpu.VMEM((slim, chunk), bf16),
                pltpu.VMEM((slim, chunk), f32),
                pltpu.VMEM((slots, chunk), f32),
                pltpu.VMEM((slots, chunk), f32),
                pltpu.VMEM((chunk, chunk), f32),
            ],
        ),
        out_shape=[like((blocks, chunk, slim), bf16), like((blocks, slots, chunk), f32)],
        compiler_params=pltpu.CompilerParams(vmem_limit_bytes=24 * MIB),
        cost_estimate=cost(12e9, 4 * MIB),
        name="attend",
    )(plan, q, kv_all, start, gate_t)

    proj = gather_bits(proj, "mp", core_bit, depth + 1, gc).reshape(model, wide + LANES)
    grads = blocked(swapped(out_grad, q, gc))
    core = (place & 1).astype(jnp.int32)[None]
    moved = 2 * single[None] + 1
    core_moved = jnp.concatenate([core, moved])
    pair = peers // 2
    per = w_query.shape[0]

    def early(*shape):
        return pl.BlockSpec((1, *shape), lambda b, *_: (jnp.minimum(b, blocks - 1),) + (0,) * len(shape))

    def once(shape):
        return pl.BlockSpec(shape, lambda b, *_: (0,) * len(shape), pipeline_mode=pl.Buffered(1))

    feed_shape = (lax.axis_size("dp"), 2 * w_up.shape[0], width)
    gated, mid, outs, outs_far, back, feed_sum = pl.pallas_call(
        functools.partial(forward_kernel, heads=heads, slots=slots, width=width, blocks=blocks),
        grid_spec=pltpu.PrefetchScalarGridSpec(
            num_scalar_prefetch=1,
            grid=(blocks + peers,),
            in_specs=[
                early(chunk, slim), early(chunk, slots), early(chunk, model), early(chunk, model),
                once(proj.shape), once(feed.shape), once(norms.shape),
            ],
            out_specs=[
                early(chunk, wide), early(chunk, model), early(chunk, model), fixed((chunk, model)),
                early(chunk, model),
                pl.BlockSpec((1, *feed_shape), lambda b, *_: (jnp.maximum(b - blocks, 0), 0, 0, 0)),
            ],
            scratch_shapes=[
                pltpu.VMEM((blocks, model, chunk), bf16),
                pltpu.VMEM((blocks, model, chunk), bf16),
                pltpu.VMEM((peers, blocks, chunk, width), bf16),
                pltpu.VMEM((peers, blocks, chunk, width), bf16),
            ],
        ),
        out_shape=[
            like((blocks, chunk, wide), bf16),
            like((blocks, chunk, model), f32),
            like((blocks, chunk, model), bf16),
            like((chunk, model), bf16),
            like((blocks, chunk, model), f32),
            like((peers, *feed_shape), bf16),
        ],
        compiler_params=pltpu.CompilerParams(vmem_limit_bytes=60 * MIB),
        cost_estimate=cost(24e9, 24 * MIB),
        name="forward",
    )(moved, gc, picks, x, grads, proj, feed, norms)

    part, parts = model, wide // model

    def late_columns(b, core):
        return 0, jnp.maximum(b - blocks, 0)

    gm, gatt, delta, glog, sums, out_send, out_keep = pl.pallas_call(
        functools.partial(branch_back_kernel, heads=heads, slots=slots, hs=hs, blocks=blocks, per=per),
        grid_spec=pltpu.PrefetchScalarGridSpec(
            num_scalar_prefetch=1,
            grid=(blocks + parts,),
            in_specs=[
                early(chunk, model), early(chunk, model), early(chunk, model),
                early(chunk, slim), early(chunk, LANES), early(chunk, slots),
                once(proj.shape), once(norms.shape),
                pl.BlockSpec((blocks, chunk, part), lambda b, core: (0, *late_columns(b, core))),
            ],
            out_specs=[
                early(chunk, model), early(chunk, slim),
                early(slots, chunk), early(chunk, LANES), fixed((8, model)),
                pl.BlockSpec((model // 2, part), late_columns),
                pl.BlockSpec((model // 2, part), late_columns),
            ],
            scratch_shapes=[pltpu.VMEM((blocks, model, chunk), bf16)],
        ),
        out_shape=[
            like((blocks, chunk, model), f32),
            like((blocks, chunk, slim), bf16),
            like((blocks, slots, chunk), f32),
            like((blocks, chunk, LANES), bf16),
            like((8, model), f32),
            like((model // 2, wide), bf16),
            like((model // 2, wide), bf16),
        ],
        compiler_params=pltpu.CompilerParams(vmem_limit_bytes=60 * MIB),
        cost_estimate=cost(8e9, 14 * MIB),
        name="branch_back",
    )(core, back, mid, grads, gc, gate, picks, proj, norms, gated)

    def low_bits(a, axis, group, dim, until=None):
        return scatter_bits(a, axis, group, dim, until).astype(bf16)

    def across(send, keep, until):
        got = flip(send, "mp", 1)
        if until is not None:
            got = after(got, until)
        return (keep.astype(f32) + got.astype(f32)).astype(bf16)

    def far_scatter(a, until=None):
        for i, group in enumerate(far_groups):
            a = scatter_bits(a, "dp", group, depth - 2 - i, until)
            if i < len(far_groups) - 1:
                a = a.astype(bf16)
        return a

    def across(send, keep, until):
        got = flip(send, "mp", 1)
        if until is not None:
            got = after(got, until)
        return (keep.astype(f32) + got.astype(f32)).astype(bf16)

    groups = [2**bits for _, bits in reversed(dp_groups)]
    feed_part = lax.psum_scatter(feed_sum, "mp", scatter_dimension=0, tiled=False)
    feed_part = feed_part.reshape(*groups, *feed_shape[1:])
    half_kv = (total // 2, chunk, 2 * hs)
    dq, dkv_send, dkv_keep = pl.pallas_call(
        functools.partial(attend_back_kernel, **attention),
        grid_spec=pltpu.PrefetchScalarGridSpec(
            num_scalar_prefetch=1,
            grid=(blocks,),
            in_specs=[
                per_block(chunk, slim), per_block(chunk, slim), fixed(kv_all.shape), per_block(1, chunk),
                per_block(slots, chunk), per_block(slots, chunk),
            ],
            out_specs=[per_block(chunk, slim), fixed(half_kv), fixed(half_kv)],
            scratch_shapes=[
                pltpu.VMEM((total, 2 * hs, chunk), bf16),
                pltpu.VMEM((total, chunk, hs), bf16),
                pltpu.VMEM((slim, chunk), bf16),
                pltpu.VMEM((slim, chunk), bf16),
                pltpu.VMEM((slim, chunk), f32),
                pltpu.VMEM((total, chunk, hs), f32),
                pltpu.VMEM((total, chunk, hs), f32),
                pltpu.VMEM((chunk, chunk), f32),
            ],
        ),
        out_shape=[like((blocks, chunk, slim), bf16), like(half_kv, bf16), like(half_kv, bf16)],
        compiler_params=pltpu.CompilerParams(vmem_limit_bytes=32 * MIB),
        cost_estimate=cost(25e9, 6 * MIB),
        name="attend_back",
    )(plan, q, gatt, kv_all, start, lse, delta)

    feed_near = scatter_start(feed_part, "dp", near_group, depth - 1)
    dkv = across(dkv_send, dkv_keep, None).reshape(pair, blocks * chunk, 2 * hs)
    dkv_y = scatter_start(dkv, "mp", y_bit, 0)
    dq = after(dq, *feed_near[2], *dkv_y[2])
    wq_send, wq_keep, spread = pl.pallas_call(
        functools.partial(query_weights_kernel, heads=heads, slots=slots, per=per),
        grid_spec=pltpu.PrefetchScalarGridSpec(
            num_scalar_prefetch=1,
            grid=(blocks,),
            in_specs=[per_block(chunk, slim), per_block(chunk, slots), per_block(chunk, model)],
            out_specs=[
                fixed((model // 2, wide)), fixed((model // 2, wide)), per_block(chunk, wide),
            ],
            scratch_shapes=[pltpu.VMEM((model, wide), f32)],
        ),
        out_shape=[
            like((model // 2, wide), bf16),
            like((model // 2, wide), bf16),
            like((blocks, chunk, wide), bf16),
        ],
        compiler_params=pltpu.CompilerParams(vmem_limit_bytes=60 * MIB),
        cost_estimate=cost(4e9, 10 * MIB),
        name="query_weights",
    )(core, dq, picks, n1)
    feed_part = scatter_end(feed_near, wq_send).astype(bf16)
    out_part = across(out_send, out_keep, wq_send).reshape(*groups, 2, per, wide)
    out_near = scatter_start(out_part, "dp", near_group, depth - 1)
    dkv = scatter_end(dkv_y, wq_send).astype(bf16).reshape(blocks, chunk, 2 * hs)
    query_part = across(wq_send, wq_keep, None).reshape(*groups, 2, per, wide)
    query_y = scatter_start(query_part, "mp", y_bit, depth)
    far_low, far_count = near_group[1], bits_of("dp") - near_group[1]
    feed_part = feed_part.reshape(*(2,) * far_count, *feed_shape[1:])
    feed_top = scatter_start(feed_part, "dp", (far_low + far_count - 1, 1), 0)
    spread = after(spread, *feed_top[2], *query_y[2], *out_near[2])

    ig, ig_far, small_send, small_keep = pl.pallas_call(
        functools.partial(input_kernel, heads=heads, per=per),
        grid_spec=pltpu.PrefetchScalarGridSpec(
            num_scalar_prefetch=1,
            grid=(blocks,),
            in_specs=[
                per_block(chunk, wide), per_block(chunk, LANES), per_block(chunk, 2 * hs),
                fixed(weights.shape), fixed(few.shape), per_block(chunk, model), per_block(chunk, model),
                per_block(chunk, model), fixed((8, model)), fixed((8, model)),
            ],
            out_specs=[
                per_block(chunk, model), fixed((chunk, model)),
                fixed((model // 2, 2 * LANES)), fixed((model // 2, 2 * LANES)),
            ],
            scratch_shapes=[
                pltpu.VMEM((model, 2 * hs), f32), pltpu.VMEM((model, LANES), f32), pltpu.VMEM((8, model), f32),
            ],
        ),
        out_shape=[
            like((blocks, chunk, model), f32),
            like((chunk, model), bf16),
            like((model // 2, 2 * LANES), bf16),
            like((model // 2, 2 * LANES), bf16),
        ],
        compiler_params=pltpu.CompilerParams(vmem_limit_bytes=60 * MIB),
        cost_estimate=cost(4e9, 12 * MIB),
        name="inputs_back",
    )(core_moved, spread, glog, dkv, weights, few, x, n1, gm, norms, sums)

    query_part = scatter_end(query_y, ig).astype(bf16)
    query_x = scatter_start(query_part, "dp", near_group, depth - 1)
    small = across(small_send, small_keep, None).reshape(*groups, 2, per, 2 * LANES)
    out_part = scatter_end(out_near, ig).astype(bf16)
    out_y = scatter_start(out_part, "mp", y_bit, depth - 1)
    query_part = scatter_end(query_x)
    small_y = scatter_start(small, "mp", y_bit, depth)
    small = scatter_end(small_y).astype(bf16)
    out_part = scatter_end(out_y)
    small = low_bits(after(small, query_part, out_part), "dp", near_group, depth - 1)
    joint = [query_part, out_part, small.astype(f32)]
    joint = jnp.concatenate(joint, axis=-1).astype(bf16)
    feed_grad = scatter_end(feed_top, joint)
    for bit in reversed(range(far_low, far_low + far_count - 1)):
        feed_grad = scatter_bits(feed_grad.astype(bf16), "dp", (bit, 1), 0)
    joint_sum = far_scatter(joint)
    up_rows = w_up.shape[0]
    smalls = joint_sum[:, 2 * wide :]
    def returned(a, piece):
        piece = flip(piece, "mp", peers - 1).astype(a.dtype)
        a = a.reshape(rows, 2, chunk, model)
        a = lax.dynamic_update_slice(a, piece[None, None], (single, 1, 0, 0))
        return a.reshape(rows, local, model)

    outs_far, ig_far = after(outs_far, small), after(ig_far, small_y[2][0])
    outputs, input_grad = returned(outs, outs_far), returned(ig, ig_far)
    counts = sums[2, :heads] + sums[2, heads : 2 * heads]
    return (
        outputs,
        input_grad,
        counts,
        joint_sum[:, :wide],
        smalls[:, : 2 * hs],
        joint_sum[:, wide : 2 * wide],
        smalls[:, LANES : LANES + heads],
        smalls[:, LANES + heads : LANES + heads + 2],
        smalls[:, LANES + heads + 2 : LANES + heads + 4],
        feed_grad[:up_rows],
        feed_grad[up_rows:],
    )


def solution(mesh):
    in_specs = (
        P("dp", "mp", None),
        P("dp", None),
        P("dp", "mp", None),
        P("dp", "mp", None),
        P(("dp", "mp"), None),
        P(("dp", "mp"), None),
        P(("dp", "mp"), None),
        P(("dp", "mp"), None),
        P(("dp", "mp"), None),
        P(("dp", "mp"), None),
        P("dp", "mp"),
        P("dp", "mp"),
    )
    out_specs = (
        P("dp", "mp", None),
        P("dp", "mp", None),
        P(),
        P(("dp", "mp"), None),
        P(("dp", "mp"), None),
        P(("dp", "mp"), None),
        P(("dp", "mp"), None),
        P(("dp", "mp"), None),
        P(("dp", "mp"), None),
        P("dp", "mp"),
        P("dp", "mp"),
    )
    return jax.shard_map(shards, mesh=mesh, in_specs=in_specs, out_specs=out_specs, check_vma=False)
```

```python
import functools
import math
import jax
import jax.numpy as jnp
from jax import lax
from jax.experimental import pallas as pl
from jax.experimental.pallas import tpu as pltpu
from jax.sharding import PartitionSpec as P

epsilon = 1e-05
f32, bf16 = jnp.float32, jnp.bfloat16
NN = (((1,), (0,)), ((), ()))
NT = (((1,), (1,)), ((), ()))
LANES = 128
LOG2E = math.log2(math.e)
MIB = 2**20


def dot(left, right, dims=NN):
    return lax.dot_general(left, right, dims, preferred_element_type=f32)


def bits_of(axis):
    return (lax.axis_size(axis) - 1).bit_length()


def bit_groups(axis):
    count = bits_of(axis)
    groups, at = [], 0
    if count % 2:
        groups.append((0, 1))
        at = 1
    while at < count:
        groups.append((at, 2))
        at += 2
    return groups


def flip(x, axis, mask):
    return lax.ppermute(x, axis, [(i, i ^ mask) for i in range(lax.axis_size(axis))])


def after(x, *others):
    return lax.optimization_barrier((x, *others))[0]


def gather_bits(x, axis, group, dim, until=None):
    low, width = group
    mine = lax.axis_index(axis) >> low
    got = [flip(x, axis, k << low) for k in range(1, 2**width)]
    if until is not None:
        got = lax.optimization_barrier((*got, until))[:-1]
    shape = [1] * (x.ndim + 1)
    shape[dim] = 2**width
    way = lax.iota(jnp.int32, 2**width).reshape(shape) ^ (mine & (2**width - 1))
    pieces = [jnp.expand_dims(p, dim) for p in (x, *got)]
    for b in range(width):
        odd = (way >> b) & 1 == 1
        pieces = [jnp.where(odd, pieces[k + 1], pieces[k]) for k in range(0, len(pieces), 2)]
    return pieces[0]


def scatter_start(x, axis, group, dim):
    low, width = group
    mine = (lax.axis_index(axis) >> low) & (2**width - 1)
    sent = [
        lax.dynamic_index_in_dim(x, mine ^ k, dim, keepdims=False) for k in range(1, 2**width)
    ]
    got = [flip(a, axis, k << low) for k, a in enumerate(sent, 1)]
    return lax.dynamic_index_in_dim(x, mine, dim, keepdims=False), got, sent


def scatter_end(started, until=None):
    total, got, _ = started
    if until is not None:
        got = lax.optimization_barrier((*got, until))[:-1]
    total = total.astype(f32)
    for g in got:
        total = total + g.astype(f32)
    return total


def scatter_bits(x, axis, group, dim, until=None):
    return scatter_end(scatter_start(x, axis, group, dim), until)


def halves(row_first, row_second, like):
    lane = lax.broadcasted_iota(jnp.int32, like, 1)
    return jnp.where(lane < LANES // 2, row_first, row_second)


def slot_lanes(rows, columns, hs):
    shape = (rows, columns)
    slot, column = (lax.broadcasted_iota(jnp.int32, shape, i) for i in range(2))
    return (slot == column // hs).astype(bf16)


def slot_experts(routes, pairs):
    slots = routes.shape[1]
    spread = dot(routes.astype(bf16), slot_lanes(slots, pairs * LANES, LANES // 2)).astype(jnp.int32)
    return [spread[:, j * LANES : (j + 1) * LANES] for j in range(pairs)]


def turn_half(x):
    return pltpu.roll(x, LANES // 2, 1)


def compact(wide, experts, head_pairs):
    lane = lax.broadcasted_iota(jnp.int32, experts[0].shape, 1)
    high = (lane >= LANES // 2).astype(jnp.int32)
    straight = [(e - high).astype(jnp.int16) for e in experts]
    crossed = [(e + high).astype(jnp.int16) for e in experts]
    found = [jnp.zeros(experts[0].shape, bf16) for _ in experts]
    for i in range(head_pairs):
        block = wide(i)
        turned = turn_half(block).astype(bf16)
        block = block.astype(bf16)
        for j in range(len(experts)):
            found[j] = jnp.where(straight[j] == jnp.int16(2 * i), block, found[j])
            found[j] = jnp.where(crossed[j] == jnp.int16(2 * i + 1), turned, found[j])
    return found


def expand(narrow, experts, head_pairs):
    lane = lax.broadcasted_iota(jnp.int32, experts[0].shape, 1)
    high = (lane >= LANES // 2).astype(jnp.int32)
    sources = []
    for block, e in zip(narrow, experts):
        sources.append(((e - high).astype(jnp.int16), block.astype(bf16)))
        sources.append(((turn_half(e) - high).astype(jnp.int16), turn_half(block).astype(bf16)))
    wide = []
    for i in range(head_pairs):
        out = jnp.zeros(experts[0].shape, bf16)
        for e, block in sources:
            out = jnp.where(e == jnp.int16(2 * i), block, out)
        wide.append(out)
    return jnp.concatenate(wide, axis=1)


def split_core(value, core, per, send_ref, keep_ref):
    rows, columns = value.shape
    if per % 16 == 0:
        parts = value.reshape(rows // (2 * per), 2, per, columns)
        first, second = parts[:, 0], parts[:, 1]
        send = jnp.where(core == 0, second, first).reshape(rows // 2, columns)
        keep = jnp.where(core == 0, first, second).reshape(rows // 2, columns)
        send_ref[...], keep_ref[...] = send.astype(bf16), keep.astype(bf16)
        return
    shape = (rows // 2, rows)
    target, source = (lax.broadcasted_iota(jnp.int32, shape, i) for i in range(2))
    start = target // per * (2 * per) + target % per
    for ref, side in ((send_ref, 1 - core), (keep_ref, core)):
        chosen = (source == start + side * per).astype(bf16)
        ref[...] = dot(chosen, value.astype(bf16)).astype(bf16)


def normed_parts(values):
    mean = jnp.mean(values, axis=1, keepdims=True)
    centred = values - mean
    rstd = lax.rsqrt(jnp.mean(centred * centred, axis=1, keepdims=True) + epsilon)
    return centred * rstd, rstd


def norm_back(grad, normed, rstd, gain):
    scaled = grad * gain
    return rstd * (
        scaled
        - jnp.mean(scaled, axis=1, keepdims=True)
        - normed * jnp.mean(scaled * normed, axis=1, keepdims=True)
    )


def norm_kernel(x_ref, w_ref, n_ref, kv_ref, norms_ref, *, heads):
    misc = w_ref[:, -LANES:].astype(f32).T
    norms = misc[heads : heads + 8, :]
    norms = jnp.concatenate(
        [norms[0:2] + norms[2:4], norms[4:6] + norms[6:8], jnp.zeros_like(norms[0:4])], axis=0
    )
    norms_ref[...] = norms
    normed, _ = normed_parts(x_ref[0].astype(f32))
    low = (normed * norms[0:1] + norms[2:3]).astype(bf16)
    n_ref[0] = low
    kv_ref[0] = dot(low, w_ref[:, : kv_ref.shape[2]]).astype(bf16)


def query_kernel(
    n_ref, w_ref, few_ref, routes_ref, routes_t_ref, q_ref, gate_ref, gate_t_ref, *, heads, slots, hs
):
    low = n_ref[0]
    head_pairs = heads // 2
    queries = dot(low, w_ref[...]) * (hs**-0.5 * LOG2E)
    experts = slot_experts(routes_ref[0], slots // 2)
    found = compact(lambda i: queries[:, i * LANES : (i + 1) * LANES], experts, head_pairs)
    q_ref[0] = jnp.concatenate(found, axis=1)
    logits = dot(low, few_ref[:, -LANES:]).T[:heads, :]
    expert = lax.broadcasted_iota(jnp.int32, logits.shape, 0)
    routes_t = routes_t_ref[0]
    picked = [
        jnp.sum(jnp.where(expert == routes_t[s : s + 1, :], logits, 0.0), axis=0, keepdims=True)
        for s in range(slots)
    ]
    chosen = jnp.concatenate(picked, axis=0)
    lifted = jnp.exp(chosen - jnp.max(chosen, axis=0, keepdims=True))
    gate = lifted / jnp.sum(lifted, axis=0, keepdims=True)
    gate_t_ref[0] = gate
    padded = jnp.concatenate([gate, jnp.zeros((LANES - slots, gate.shape[1]), f32)], axis=0)
    gate_ref[0] = padded.T


def key_bias(first_key, first_query, start, keys, queries):
    key = first_key + lax.broadcasted_iota(jnp.int32, (keys, queries), 0)
    query = first_query + lax.broadcasted_iota(jnp.int32, (keys, queries), 1)
    return jnp.where((key <= query) & (key >= start), 0.0, -1e30)


def kv_place(row, chunk, single, rows, peers):
    half, owner = chunk % 2, chunk // 2
    owner = jnp.where((half == 1) & (row == single), peers - 1 - owner, owner)
    return owner * (2 * rows) + row * 2 + half


def over_keys(plan, start_ref, bias, block, keys, queries):
    b = pl.program_id(0)
    row, last, first, full = plan[4 * b], plan[4 * b + 1], plan[4 * b + 2], plan[4 * b + 3]

    def masked(i, carry):
        chunk = jnp.where(i == 0, last, first + i - 1)
        bias[...] = key_bias(chunk * keys, last * keys, start_ref[0], keys, queries)
        block(row, chunk, True)
        return carry

    def plain(chunk, carry):
        block(row, chunk, False)
        return carry

    lax.fori_loop(0, 1 + full - first, masked, 0)
    lax.fori_loop(full, last, plain, 0)


def attend_kernel(
    plan, q_ref, kv_ref, start_ref, gate_ref, out_ref, lse_ref, kvt, qt, acc, top, tot, bias, *, slots, hs, rows, peers
):
    queries, keys = q_ref.shape[1], kv_ref.shape[1]

    @pl.when(pl.program_id(0) == 0)
    def _():
        for i in range(kv_ref.shape[0]):
            kvt[i] = kv_ref[i].T

    qt[...] = q_ref[0].T
    acc[...] = jnp.zeros_like(acc)
    top[...] = jnp.full_like(top, -1e30)
    tot[...] = jnp.zeros_like(tot)
    part = [slice(h * hs, (h + 1) * hs) for h in range(slots)]

    def block(row, chunk, masked):
        at = kv_place(row, chunk, plan[8 * rows], rows, peers)
        k = kv_ref[at][:, :hs]
        vt = kvt[at, hs : 2 * hs, :]
        tops, tots = top[...], tot[...]
        scores = [dot(k, qt[part[h], :]) for h in range(slots)]
        if masked:
            scores = [s + bias[...] for s in scores]
        highest = [
            jnp.maximum(tops[h : h + 1], jnp.max(scores[h], axis=0, keepdims=True)) for h in range(slots)
        ]
        probs = [jnp.exp2(scores[h] - highest[h]) for h in range(slots)]
        shrink = [jnp.exp2(tops[h : h + 1] - highest[h]) for h in range(slots)]
        totals = [
            tots[h : h + 1] * shrink[h] + jnp.sum(probs[h], axis=0, keepdims=True) for h in range(slots)
        ]
        for h in range(slots):
            acc[part[h], :] = acc[part[h], :] * shrink[h] + dot(vt, probs[h].astype(bf16))
        top[...] = jnp.concatenate(highest, axis=0)
        tot[...] = jnp.concatenate(totals, axis=0)

    over_keys(plan, start_ref, bias, block, keys, queries)
    for h in range(slots):
        acc[part[h], :] = acc[part[h], :] * (gate_ref[0, h : h + 1, :] / tot[h : h + 1, :])
    lse_ref[0] = top[...] + jnp.log2(tot[...])
    out_ref[0] = acc[...].astype(bf16).T


def attend_back_kernel(
    plan, q_ref, g_ref, kv_ref, start_ref, lse_ref, delta_ref, dq_ref, send_ref, keep_ref,
    kvt, v_rows, qt, gt, dqt, dk, dv, bias, *, slots, hs, rows, peers,
):
    queries, keys = q_ref.shape[1], kv_ref.shape[1]
    b = pl.program_id(0)

    @pl.when(b == 0)
    def _():
        for i in range(kv_ref.shape[0]):
            kvt[i] = kv_ref[i].T
            v_rows[i] = kv_ref[i][:, hs:]
        dk[...] = jnp.zeros_like(dk)
        dv[...] = jnp.zeros_like(dv)

    qt[...] = q_ref[0].T
    gt[...] = g_ref[0].T
    dqt[...] = jnp.zeros_like(dqt)
    part = [slice(h * hs, (h + 1) * hs) for h in range(slots)]

    def block(row, chunk, masked):
        at = kv_place(row, chunk, plan[8 * rows], rows, peers)
        k = kv_ref[at][:, :hs]
        v = v_rows[at]
        kt = kvt[at, :hs, :]
        scores = [dot(k, qt[part[h], :]) for h in range(slots)]
        grads = [dot(v, gt[part[h], :]) for h in range(slots)]
        if masked:
            scores = [s + bias[...] for s in scores]
        probs = [jnp.exp2(scores[h] - lse_ref[0, h : h + 1, :]) for h in range(slots)]
        ds = [(probs[h] * (grads[h] - delta_ref[0, h : h + 1, :])).astype(bf16) for h in range(slots)]
        low = [p.astype(bf16) for p in probs]
        for h in range(slots):
            dqt[part[h], :] += dot(kt, ds[h])
        dk[at] += sum(dot(ds[h], qt[part[h], :], NT) for h in range(slots))
        dv[at] += sum(dot(low[h], gt[part[h], :], NT) for h in range(slots))

    over_keys(plan, start_ref, bias, block, keys, queries)
    dq_ref[0] = (dqt[...] * hs**-0.5).astype(bf16).T

    @pl.when(b == pl.num_programs(0) - 1)
    def _():
        core, each = plan[8 * rows + 1], kv_ref.shape[0] // peers
        for i in range(send_ref.shape[0]):
            at = i + each * (i // each)
            for ref, place in ((send_ref, at + each * (1 - core)), (keep_ref, at + each * core)):
                ref[i] = jnp.concatenate([dk[place] * (1.0 / LOG2E), dv[place]], axis=1).astype(bf16)


def forward_kernel(
    moved, gc_ref, routes_ref, x_ref, og_ref, wo_ref, ff_ref, norms_ref,
    gated_ref, mid_ref, out_ref, far_ref, back_ref, sum_ref, n2t, ogt, hid, gbef,
    *, heads, slots, width, blocks,
):
    step = pl.program_id(0)
    tokens, model = x_ref.shape[1], x_ref.shape[2]
    peers = ff_ref.shape[1]

    @pl.when(step < blocks)
    def _():
        pairs = slots // 2
        experts = slot_experts(routes_ref[0], pairs)
        gc = [gc_ref[0][:, j * LANES : (j + 1) * LANES].astype(f32) for j in range(pairs)]
        gated = expand(gc, experts, heads // 2)
        gated_ref[0] = gated
        middle = x_ref[0].astype(f32) + dot(gated, wo_ref[:, : gated.shape[1]], NT)
        mid_ref[0] = middle
        vhat, _ = normed_parts(middle)
        low = (vhat * norms_ref[1:2, :] + norms_ref[3:4, :]).astype(bf16)
        og = og_ref[0]
        n2t[step] = low.T
        ogt[step] = og.T
        out = middle
        back = jnp.zeros_like(out)
        slope = math.sqrt(2.0 / math.pi)
        for c in range(peers):
            up, down = (ff_ref[:, c, :, at : at + width].reshape(model, width) for at in (0, width))
            v = dot(low, up)
            square = v * v
            bent = jnp.tanh(slope * v * (1.0 + 0.044715 * square))
            rise = 0.5 * (1.0 + bent)
            hidden = (v * rise).astype(bf16)
            slant = rise + 0.5 * v * (1.0 - bent * bent) * (slope + 3.0 * slope * 0.044715 * square)
            before = (dot(og, down) * slant).astype(bf16)
            out = out + dot(hidden, down, NT)
            back = back + dot(before, up, NT)
            hid[c, step] = hidden
            gbef[c, step] = before
        out_ref[0] = out.astype(bf16)
        back_ref[0] = back

        @pl.when(step == moved[0])
        def _():
            far_ref[...] = out.astype(bf16)

    @pl.when(step >= blocks)
    def _():
        c = step - blocks
        up = sum(dot(n2t[b], gbef[c, b]) for b in range(blocks))
        down = sum(dot(ogt[b], hid[c, b]) for b in range(blocks))
        shape = (sum_ref.shape[1], sum_ref.shape[2] // 2, sum_ref.shape[3])
        sum_ref[0] = jnp.concatenate([up.reshape(shape), down.reshape(shape)], axis=1).astype(bf16)


def branch_back_kernel(
    core, back_ref, mid_ref, og_ref, gc_ref, gate_ref, routes_ref, wo_ref, norms_ref, gated_ref,
    gm_ref, gatt_ref, delta_ref, glog_ref, sums_ref, send_ref, keep_ref, gbrt,
    *, heads, slots, hs, blocks, per,
):
    step = pl.program_id(0)

    @pl.when(step < blocks)
    def _():
        branch_back_block(
            step, back_ref, mid_ref, og_ref, gc_ref, gate_ref, routes_ref, wo_ref, norms_ref,
            gm_ref, gatt_ref, delta_ref, glog_ref, sums_ref, gbrt, heads, slots, hs,
        )

    @pl.when(step >= blocks)
    def _():
        total = sum(dot(gbrt[b], gated_ref[b]) for b in range(blocks))
        split_core(total, core[0], per, send_ref, keep_ref)

        @pl.when(step == blocks)
        def _():
            held = jnp.sum(wo_ref[:, heads * hs :].astype(f32), axis=0, keepdims=True)
            sums_ref[2:3, :LANES] = held * (1.0 / per)


def branch_back_block(
    step, back_ref, mid_ref, og_ref, gc_ref, gate_ref, routes_ref, wo_ref, norms_ref,
    gm_ref, gatt_ref, delta_ref, glog_ref, sums_ref, gbrt, heads, slots, hs,
):
    tokens, model = mid_ref.shape[1], mid_ref.shape[2]
    head_pairs, pairs = heads // 2, slots // 2
    experts = slot_experts(routes_ref[0], pairs)
    back = back_ref[0]
    vhat, rstd = normed_parts(mid_ref[0])
    gm = og_ref[0].astype(f32) + norm_back(back, vhat, rstd, norms_ref[1:2, :])
    gm_ref[0] = gm

    @pl.when(step == 0)
    def _():
        sums_ref[...] = jnp.zeros_like(sums_ref)

    sums_ref[0:1, :] += jnp.sum(back * vhat, axis=0, keepdims=True)
    sums_ref[1:2, :] += jnp.sum(back, axis=0, keepdims=True)
    gbr = gm.astype(bf16)
    gbrt[step] = gbr.T
    wide = dot(gbr, wo_ref[:, : heads * hs])
    found = compact(lambda i: wide[:, i * LANES : (i + 1) * LANES], experts, head_pairs)
    found = [f.astype(f32) for f in found]
    gate = gate_ref[0]
    lanes = slot_lanes(LANES, slots * hs, hs)
    coarse = gate.astype(bf16)
    wide_gate = dot(coarse, lanes) + dot((gate - coarse.astype(f32)).astype(bf16), lanes)
    attended, products = [], []
    for j in range(pairs):
        spread = wide_gate[:, j * LANES : (j + 1) * LANES]
        attended.append((found[j] * spread).astype(bf16))
        products.append(found[j] * gc_ref[0][:, j * LANES : (j + 1) * LANES].astype(f32))
    gatt_ref[0] = jnp.concatenate(attended, axis=1)
    product = jnp.concatenate(products, axis=1)
    owner = lax.broadcasted_iota(jnp.int32, (slots * hs, LANES), 0) // hs
    ones = (owner == lax.broadcasted_iota(jnp.int32, (slots * hs, LANES), 1)).astype(bf16)
    coarse = product.astype(bf16)
    fine = (product - coarse.astype(f32)).astype(bf16)
    inner = dot(coarse, ones) + dot(fine, ones)
    delta_ref[0] = inner.T[:slots, :]
    logit = inner - gate * jnp.sum(inner, axis=1, keepdims=True)
    spread_out = dot(logit.astype(bf16), lanes)
    lane = lax.broadcasted_iota(jnp.int32, spread_out.shape, 1) % hs
    spread_out = jnp.where(lane == jnp.concatenate(experts, axis=1), spread_out, 0.0).astype(bf16)
    column, row = (lax.broadcasted_iota(jnp.int32, (slots * hs, LANES), i) for i in (1, 0))
    glog_ref[0] = dot(spread_out, (row % hs == column).astype(bf16)).astype(bf16)


def query_weights_kernel(
    core, dq_ref, routes_ref, n_ref, send_ref, keep_ref, wide_ref, acc, *, heads, slots, per
):
    pairs = slots // 2
    experts = slot_experts(routes_ref[0], pairs)
    dq = [dq_ref[0][:, j * LANES : (j + 1) * LANES].astype(f32) for j in range(pairs)]
    wide = expand(dq, experts, heads // 2)
    wide_ref[0] = wide

    @pl.when(pl.program_id(0) == 0)
    def _():
        acc[...] = jnp.zeros_like(acc)

    acc[...] += dot(n_ref[0].T, wide)

    @pl.when(pl.program_id(0) == pl.num_programs(0) - 1)
    def _():
        split_core(acc[...], core[0], per, send_ref, keep_ref)


def input_kernel(
    core, wide_ref, glog_ref, dkv_ref, w_ref, few_ref, x_ref, n_ref, gm_ref, norms_ref, sums_ref,
    ig_ref, far_ref, send_ref, keep_ref, acck, accr, sums, *, heads, per,
):
    dkv, glog = dkv_ref[0], glog_ref[0]
    dn = (
        dot(wide_ref[0], w_ref[...], NT)
        + dot(dkv, few_ref[:, : dkv.shape[1]], NT)
        + dot(glog, few_ref[:, -LANES:], NT)
    )
    vhat, rstd = normed_parts(x_ref[0].astype(f32))
    ig = gm_ref[0] + norm_back(dn, vhat, rstd, norms_ref[0:1, :])
    ig_ref[0] = ig

    @pl.when(pl.program_id(0) == core[1])
    def _():
        far_ref[...] = ig.astype(bf16)

    @pl.when(pl.program_id(0) == 0)
    def _():
        acck[...] = jnp.zeros_like(acck)
        accr[...] = jnp.zeros_like(accr)
        sums[...] = jnp.zeros_like(sums)

    nt = n_ref[0].T
    acck[...] += dot(nt, dkv)
    accr[...] += dot(nt, glog)
    sums[0:1, :] += jnp.sum(dn * vhat, axis=0, keepdims=True)
    sums[1:2, :] += jnp.sum(dn, axis=0, keepdims=True)

    @pl.when(pl.program_id(0) == pl.num_programs(0) - 1)
    def _():
        second = sums_ref[...]
        model = second.shape[1]
        rows = jnp.concatenate(
            [
                jnp.zeros((heads, model), f32),
                sums[0:1, :], second[0:1, :], sums[1:2, :], second[1:2, :],
                jnp.zeros((LANES - heads - 4, model), f32),
            ],
            axis=0,
        )
        small = jnp.concatenate([acck[...], accr[...] + rows.T], axis=1)
        split_core(small, core[0], per, send_ref, keep_ref)


def fixed(shape):
    return pl.BlockSpec(shape, lambda b, *_: (0,) * len(shape))


def per_block(*shape):
    return pl.BlockSpec((1, *shape), lambda b, *_: (b,) + (0,) * len(shape))


def like(shape, kind):
    return jax.ShapeDtypeStruct(shape, kind)


def cost(flops, size, exps=0):
    return pl.CostEstimate(flops=int(flops), bytes_accessed=int(size), transcendentals=int(exps))


def shards(
    tokens, segment_ids, routes, out_grad, w_query, w_keyval, w_output, w_router,
    norm_gains, norm_biases, w_up, w_down,
):
    rows, local, model = tokens.shape
    peers = lax.axis_size("mp")
    slots = routes.shape[2]
    heads = w_router.shape[1]
    hs = w_keyval.shape[1] // 2
    width = w_up.shape[1]
    chunk = local // 2
    blocks = rows * 2
    count = rows * local
    place = lax.axis_index("mp")
    wide = heads * hs
    slim = slots * hs

    def two(v):
        high = lax.reduce_precision(v, 8, 7)
        return [high.astype(bf16), (v - high).astype(bf16)]

    pads = jnp.zeros((w_query.shape[0], LANES - heads - 8), bf16)
    first = jnp.concatenate(
        [w_query, w_keyval, w_router, *two(norm_gains), *two(norm_biases), pads], axis=1
    )
    dp_groups = bit_groups("dp")
    far_groups, near_group = dp_groups[1:], dp_groups[0]
    depth = len(dp_groups)

    def far_stage(a, until=None):
        for i, group in enumerate(reversed(far_groups)):
            a = gather_bits(a, "dp", group, i, until)
        return a

    both = jnp.concatenate([w_up, w_down], axis=1)
    feed = lax.all_gather(both, ("dp", "mp"), axis=0, tiled=False)
    feed = feed.reshape(lax.axis_size("dp"), peers, *both.shape)
    y_bit, core_bit = (1, 1), (0, 1)
    first = far_stage(first)
    chosen = after(routes, first)
    chosen = (chosen[..., None] == jnp.arange(heads, dtype=jnp.int32)).astype(f32)
    held = jnp.sum(chosen, axis=(0, 1, 2))
    held_high = lax.reduce_precision(held, 8, 7)
    held = jnp.concatenate([held_high, held - held_high, jnp.zeros(LANES - 2 * heads, f32)])
    held = jnp.broadcast_to(held.astype(bf16), (w_output.shape[0], LANES))
    first_y = gather_bits(first, "mp", y_bit, depth - 1)
    proj = far_stage(after(jnp.concatenate([w_output, held], axis=1), first), first_y)
    few = gather_bits(first_y[..., wide:], "dp", near_group, depth - 1)
    many = after(first_y[..., :wide], few)
    few = gather_bits(few, "mp", core_bit, depth + 1).reshape(model, 2 * hs + LANES)
    first_x = few
    proj = gather_bits(after(proj, first_y), "mp", y_bit, depth - 1, few)

    single = jnp.argmax(segment_ids[:, -1] == 0).astype(jnp.int32)

    def swapped(a, start=None, until=None):
        kind = a.dtype
        if start is not None:
            a = after(a, start)
        a = a.reshape(rows, 2, chunk, -1)
        piece = lax.dynamic_index_in_dim(a[:, 1], single, 0, keepdims=False)
        piece = flip(piece.astype(bf16), "mp", peers - 1)
        if until is not None:
            piece = after(piece, until)
        return lax.dynamic_update_slice(a, piece.astype(kind)[None, None], (single, 1, 0, 0))

    def blocked(a):
        return a.reshape(blocks, chunk, -1)

    x = blocked(swapped(tokens))
    picks = blocked(swapped(routes, first_y, first_x))
    picks_t = jnp.swapaxes(picks, 1, 2)
    segments = after(segment_ids, first_y)
    near, far = 2 * place, 2 * (peers - 1 - place) + 1
    one = jnp.arange(rows, dtype=jnp.int32) == single
    last = jnp.stack(
        [jnp.full((rows,), near, jnp.int32), jnp.where(one, far, near + 1).astype(jnp.int32)], axis=1
    )
    ids = jnp.arange(8, dtype=jnp.int32)
    sizes = jnp.sum((segments[:, :, None] == ids).astype(jnp.int32), axis=1)
    own = jnp.stack(
        [
            jnp.stack(
                [lax.dynamic_slice(segments, (r, last[r, i] * chunk), (1, chunk))[0] for i in range(2)]
            )
            for r in range(rows)
        ]
    )
    start = jnp.sum(jnp.where(ids < own[..., None], sizes[:, None, None, :], 0), axis=-1)
    full = jnp.minimum((start[:, :, -1] + chunk - 1) // chunk, last)
    which = jnp.broadcast_to(jnp.arange(rows, dtype=jnp.int32)[:, None], (rows, 2))
    plan = jnp.stack([which, last, start[:, :, 0] // chunk, full], axis=-1).astype(jnp.int32)
    plan = jnp.concatenate([plan.reshape(-1), single[None], (place & 1).astype(jnp.int32)[None]])
    start = start.astype(jnp.int32).reshape(blocks, 1, chunk)

    n1, kv, norms = pl.pallas_call(
        functools.partial(norm_kernel, heads=heads),
        grid=(blocks,),
        in_specs=[per_block(chunk, model), fixed(few.shape)],
        out_specs=[per_block(chunk, model), per_block(chunk, 2 * hs), fixed((8, model))],
        out_shape=[
            like((blocks, chunk, model), bf16),
            like((blocks, chunk, 2 * hs), bf16),
            like((8, model), f32),
        ],
        cost_estimate=cost(2 * count * model * LANES, 4 * MIB),
        name="norm_one",
    )(x, few)
    many = gather_bits(many, "dp", near_group, depth - 1, kv)
    weights = gather_bits(many, "mp", core_bit, depth + 1).reshape(model, wide)
    kv_half = gather_bits(kv, "mp", y_bit, 0, weights)
    kv_all = gather_bits(kv_half, "mp", core_bit, 1).reshape(peers * blocks, chunk, 2 * hs)

    q, gate, gate_t = pl.pallas_call(
        functools.partial(query_kernel, heads=heads, slots=slots, hs=hs),
        grid=(blocks,),
        in_specs=[
            per_block(chunk, model), fixed(weights.shape), fixed(few.shape),
            per_block(chunk, slots), per_block(slots, chunk),
        ],
        out_specs=[per_block(chunk, slim), per_block(chunk, LANES), per_block(slots, chunk)],
        out_shape=[
            like((blocks, chunk, slim), bf16),
            like((blocks, chunk, LANES), f32),
            like((blocks, slots, chunk), f32),
        ],
        compiler_params=pltpu.CompilerParams(vmem_limit_bytes=24 * MIB),
        cost_estimate=cost(2 * count * model * wide * 2, 6 * MIB),
        name="queries",
    )(after(n1, kv_half), weights, few, picks, picks_t)

    proj = gather_bits(after(proj, many), "dp", near_group, depth - 1, q)
    attention = dict(slots=slots, hs=hs, rows=rows, peers=peers)
    total = peers * blocks
    gc, lse = pl.pallas_call(
        functools.partial(attend_kernel, **attention),
        grid_spec=pltpu.PrefetchScalarGridSpec(
            num_scalar_prefetch=1,
            grid=(blocks,),
            in_specs=[
                per_block(chunk, slim), fixed(kv_all.shape), per_block(1, chunk), per_block(slots, chunk),
            ],
            out_specs=[per_block(chunk, slim), per_block(slots, chunk)],
            scratch_shapes=[
                pltpu.VMEM((total, 2 * hs, chunk), bf16),
                pltpu.VMEM((slim, chunk), bf16),
                pltpu.VMEM((slim, chunk), f32),
                pltpu.VMEM((slots, chunk), f32),
                pltpu.VMEM((slots, chunk), f32),
                pltpu.VMEM((chunk, chunk), f32),
            ],
        ),
        out_shape=[like((blocks, chunk, slim), bf16), like((blocks, slots, chunk), f32)],
        compiler_params=pltpu.CompilerParams(vmem_limit_bytes=24 * MIB),
        cost_estimate=cost(12e9, 4 * MIB),
        name="attend",
    )(plan, q, kv_all, start, gate_t)

    proj = gather_bits(proj, "mp", core_bit, depth + 1, gc).reshape(model, wide + LANES)
    grads = blocked(swapped(out_grad, q, gc))
    core = (place & 1).astype(jnp.int32)[None]
    moved = 2 * single[None] + 1
    core_moved = jnp.concatenate([core, moved])
    pair = peers // 2
    per = w_query.shape[0]

    def early(*shape):
        return pl.BlockSpec((1, *shape), lambda b, *_: (jnp.minimum(b, blocks - 1),) + (0,) * len(shape))

    def once(shape):
        return pl.BlockSpec(shape, lambda b, *_: (0,) * len(shape), pipeline_mode=pl.Buffered(1))

    feed_shape = (lax.axis_size("dp"), 2 * w_up.shape[0], width)
    gated, mid, outs, outs_far, back, feed_sum = pl.pallas_call(
        functools.partial(forward_kernel, heads=heads, slots=slots, width=width, blocks=blocks),
        grid_spec=pltpu.PrefetchScalarGridSpec(
            num_scalar_prefetch=1,
            grid=(blocks + peers,),
            in_specs=[
                early(chunk, slim), early(chunk, slots), early(chunk, model), early(chunk, model),
                once(proj.shape), once(feed.shape), once(norms.shape),
            ],
            out_specs=[
                early(chunk, wide), early(chunk, model), early(chunk, model), fixed((chunk, model)),
                early(chunk, model),
                pl.BlockSpec((1, *feed_shape), lambda b, *_: (jnp.maximum(b - blocks, 0), 0, 0, 0)),
            ],
            scratch_shapes=[
                pltpu.VMEM((blocks, model, chunk), bf16),
                pltpu.VMEM((blocks, model, chunk), bf16),
                pltpu.VMEM((peers, blocks, chunk, width), bf16),
                pltpu.VMEM((peers, blocks, chunk, width), bf16),
            ],
        ),
        out_shape=[
            like((blocks, chunk, wide), bf16),
            like((blocks, chunk, model), f32),
            like((blocks, chunk, model), bf16),
            like((chunk, model), bf16),
            like((blocks, chunk, model), f32),
            like((peers, *feed_shape), bf16),
        ],
        compiler_params=pltpu.CompilerParams(vmem_limit_bytes=60 * MIB),
        cost_estimate=cost(24e9, 24 * MIB),
        name="forward",
    )(moved, gc, picks, x, grads, proj, feed, norms)

    part, parts = model, wide // model

    def late_columns(b, core):
        return 0, jnp.maximum(b - blocks, 0)

    gm, gatt, delta, glog, sums, out_send, out_keep = pl.pallas_call(
        functools.partial(branch_back_kernel, heads=heads, slots=slots, hs=hs, blocks=blocks, per=per),
        grid_spec=pltpu.PrefetchScalarGridSpec(
            num_scalar_prefetch=1,
            grid=(blocks + parts,),
            in_specs=[
                early(chunk, model), early(chunk, model), early(chunk, model),
                early(chunk, slim), early(chunk, LANES), early(chunk, slots),
                once(proj.shape), once(norms.shape),
                pl.BlockSpec((blocks, chunk, part), lambda b, core: (0, *late_columns(b, core))),
            ],
            out_specs=[
                early(chunk, model), early(chunk, slim),
                early(slots, chunk), early(chunk, LANES), fixed((8, model)),
                pl.BlockSpec((model // 2, part), late_columns),
                pl.BlockSpec((model // 2, part), late_columns),
            ],
            scratch_shapes=[pltpu.VMEM((blocks, model, chunk), bf16)],
        ),
        out_shape=[
            like((blocks, chunk, model), f32),
            like((blocks, chunk, slim), bf16),
            like((blocks, slots, chunk), f32),
            like((blocks, chunk, LANES), bf16),
            like((8, model), f32),
            like((model // 2, wide), bf16),
            like((model // 2, wide), bf16),
        ],
        compiler_params=pltpu.CompilerParams(vmem_limit_bytes=60 * MIB),
        cost_estimate=cost(8e9, 14 * MIB),
        name="branch_back",
    )(core, back, mid, grads, gc, gate, picks, proj, norms, gated)

    def low_bits(a, axis, group, dim, until=None):
        return scatter_bits(a, axis, group, dim, until).astype(bf16)

    def across(send, keep, until):
        got = flip(send, "mp", 1)
        if until is not None:
            got = after(got, until)
        return (keep.astype(f32) + got.astype(f32)).astype(bf16)

    def far_scatter(a, until=None):
        for i, group in enumerate(far_groups):
            a = scatter_bits(a, "dp", group, depth - 2 - i, until)
            if i < len(far_groups) - 1:
                a = a.astype(bf16)
        return a

    def across(send, keep, until):
        got = flip(send, "mp", 1)
        if until is not None:
            got = after(got, until)
        return (keep.astype(f32) + got.astype(f32)).astype(bf16)

    groups = [2**bits for _, bits in reversed(dp_groups)]
    feed_part = lax.psum_scatter(feed_sum, "mp", scatter_dimension=0, tiled=False)
    feed_part = feed_part.reshape(*groups, *feed_shape[1:])
    half_kv = (total // 2, chunk, 2 * hs)
    dq, dkv_send, dkv_keep = pl.pallas_call(
        functools.partial(attend_back_kernel, **attention),
        grid_spec=pltpu.PrefetchScalarGridSpec(
            num_scalar_prefetch=1,
            grid=(blocks,),
            in_specs=[
                per_block(chunk, slim), per_block(chunk, slim), fixed(kv_all.shape), per_block(1, chunk),
                per_block(slots, chunk), per_block(slots, chunk),
            ],
            out_specs=[per_block(chunk, slim), fixed(half_kv), fixed(half_kv)],
            scratch_shapes=[
                pltpu.VMEM((total, 2 * hs, chunk), bf16),
                pltpu.VMEM((total, chunk, hs), bf16),
                pltpu.VMEM((slim, chunk), bf16),
                pltpu.VMEM((slim, chunk), bf16),
                pltpu.VMEM((slim, chunk), f32),
                pltpu.VMEM((total, chunk, hs), f32),
                pltpu.VMEM((total, chunk, hs), f32),
                pltpu.VMEM((chunk, chunk), f32),
            ],
        ),
        out_shape=[like((blocks, chunk, slim), bf16), like(half_kv, bf16), like(half_kv, bf16)],
        compiler_params=pltpu.CompilerParams(vmem_limit_bytes=32 * MIB),
        cost_estimate=cost(25e9, 6 * MIB),
        name="attend_back",
    )(plan, q, gatt, kv_all, start, lse, delta)

    feed_near = scatter_start(feed_part, "dp", near_group, depth - 1)
    dkv = across(dkv_send, dkv_keep, None).reshape(pair, blocks * chunk, 2 * hs)
    dkv_y = scatter_start(dkv, "mp", y_bit, 0)
    dq = after(dq, *feed_near[2], *dkv_y[2])
    wq_send, wq_keep, spread = pl.pallas_call(
        functools.partial(query_weights_kernel, heads=heads, slots=slots, per=per),
        grid_spec=pltpu.PrefetchScalarGridSpec(
            num_scalar_prefetch=1,
            grid=(blocks,),
            in_specs=[per_block(chunk, slim), per_block(chunk, slots), per_block(chunk, model)],
            out_specs=[
                fixed((model // 2, wide)), fixed((model // 2, wide)), per_block(chunk, wide),
            ],
            scratch_shapes=[pltpu.VMEM((model, wide), f32)],
        ),
        out_shape=[
            like((model // 2, wide), bf16),
            like((model // 2, wide), bf16),
            like((blocks, chunk, wide), bf16),
        ],
        compiler_params=pltpu.CompilerParams(vmem_limit_bytes=60 * MIB),
        cost_estimate=cost(4e9, 10 * MIB),
        name="query_weights",
    )(core, dq, picks, n1)
    feed_part = scatter_end(feed_near, wq_send).astype(bf16)
    out_part = across(out_send, out_keep, wq_send).reshape(*groups, 2, per, wide)
    out_near = scatter_start(out_part, "dp", near_group, depth - 1)
    dkv = scatter_end(dkv_y, wq_send).astype(bf16).reshape(blocks, chunk, 2 * hs)
    query_part = across(wq_send, wq_keep, None).reshape(*groups, 2, per, wide)
    query_y = scatter_start(query_part, "mp", y_bit, depth)
    far_low, far_count = near_group[1], bits_of("dp") - near_group[1]
    feed_part = feed_part.reshape(*(2,) * far_count, *feed_shape[1:])
    feed_top = scatter_start(feed_part, "dp", (far_low + far_count - 1, 1), 0)
    spread = after(spread, *feed_top[2], *query_y[2], *out_near[2])

    ig, ig_far, small_send, small_keep = pl.pallas_call(
        functools.partial(input_kernel, heads=heads, per=per),
        grid_spec=pltpu.PrefetchScalarGridSpec(
            num_scalar_prefetch=1,
            grid=(blocks,),
            in_specs=[
                per_block(chunk, wide), per_block(chunk, LANES), per_block(chunk, 2 * hs),
                fixed(weights.shape), fixed(few.shape), per_block(chunk, model), per_block(chunk, model),
                per_block(chunk, model), fixed((8, model)), fixed((8, model)),
            ],
            out_specs=[
                per_block(chunk, model), fixed((chunk, model)),
                fixed((model // 2, 2 * LANES)), fixed((model // 2, 2 * LANES)),
            ],
            scratch_shapes=[
                pltpu.VMEM((model, 2 * hs), f32), pltpu.VMEM((model, LANES), f32), pltpu.VMEM((8, model), f32),
            ],
        ),
        out_shape=[
            like((blocks, chunk, model), f32),
            like((chunk, model), bf16),
            like((model // 2, 2 * LANES), bf16),
            like((model // 2, 2 * LANES), bf16),
        ],
        compiler_params=pltpu.CompilerParams(vmem_limit_bytes=60 * MIB),
        cost_estimate=cost(4e9, 12 * MIB),
        name="inputs_back",
    )(core_moved, spread, glog, dkv, weights, few, x, n1, gm, norms, sums)

    query_part = scatter_end(query_y, ig).astype(bf16)
    query_x = scatter_start(query_part, "dp", near_group, depth - 1)
    small = across(small_send, small_keep, None).reshape(*groups, 2, per, 2 * LANES)
    out_part = scatter_end(out_near, ig).astype(bf16)
    out_y = scatter_start(out_part, "mp", y_bit, depth - 1)
    query_part = scatter_end(query_x)
    small_y = scatter_start(small, "mp", y_bit, depth)
    small = scatter_end(small_y).astype(bf16)
    out_part = scatter_end(out_y)
    small = low_bits(after(small, query_part, out_part), "dp", near_group, depth - 1)
    joint = [query_part, out_part, small.astype(f32)]
    joint = jnp.concatenate(joint, axis=-1).astype(bf16)
    feed_grad = scatter_end(feed_top, joint)
    for bit in reversed(range(far_low, far_low + far_count - 1)):
        feed_grad = scatter_bits(feed_grad.astype(bf16), "dp", (bit, 1), 0)
    started = [joint]
    for i, group in enumerate(far_groups[:-1]):
        started = [scatter_bits(started[0], "dp", group, depth - 2 - i).astype(bf16)]
    own, got, _ = scatter_start(started[0], "dp", far_groups[-1], 0)

    def summed(first, last):
        return scatter_end((own[:, first:last], [g[:, first:last] for g in got], None))

    query_grad, out_grads = summed(0, wide), summed(wide, 2 * wide)
    up_rows = w_up.shape[0]
    smalls = summed(2 * wide, 2 * wide + 2 * LANES)
    def returned(a, piece):
        piece = flip(piece, "mp", peers - 1).astype(a.dtype)
        a = a.reshape(rows, 2, chunk, model)
        a = lax.dynamic_update_slice(a, piece[None, None], (single, 1, 0, 0))
        return a.reshape(rows, local, model)

    outs_far, ig_far = after(outs_far, small), after(ig_far, small_y[2][0])
    outputs, input_grad = returned(outs, outs_far), returned(ig, ig_far)
    counts = sums[2, :heads] + sums[2, heads : 2 * heads]
    return (
        outputs,
        input_grad,
        counts,
        query_grad,
        smalls[:, : 2 * hs],
        out_grads,
        smalls[:, LANES : LANES + heads],
        smalls[:, LANES + heads : LANES + heads + 2],
        smalls[:, LANES + heads + 2 : LANES + heads + 4],
        feed_grad[:up_rows],
        feed_grad[up_rows:],
    )


def solution(mesh):
    in_specs = (
        P("dp", "mp", None),
        P("dp", None),
        P("dp", "mp", None),
        P("dp", "mp", None),
        P(("dp", "mp"), None),
        P(("dp", "mp"), None),
        P(("dp", "mp"), None),
        P(("dp", "mp"), None),
        P(("dp", "mp"), None),
        P(("dp", "mp"), None),
        P("dp", "mp"),
        P("dp", "mp"),
    )
    out_specs = (
        P("dp", "mp", None),
        P("dp", "mp", None),
        P(),
        P(("dp", "mp"), None),
        P(("dp", "mp"), None),
        P(("dp", "mp"), None),
        P(("dp", "mp"), None),
        P(("dp", "mp"), None),
        P(("dp", "mp"), None),
        P("dp", "mp"),
        P("dp", "mp"),
    )
    return jax.shard_map(shards, mesh=mesh, in_specs=in_specs, out_specs=out_specs, check_vma=False)
```
